32 devices in a mesh: section: 2 (over x), seq: 4 (over y, core), dp: 4 (over z).
Axes of the slice: x: 2, y: 2, z: 4, core: 2. Of those that a mesh axis runs over, the one named last changes fastest.
Arguments:
- boundary: bfloat16 [2, 16, 1024, 1280], P('section', 'dp', 'seq'), may hold values from -6 to 6
- lengths: int32 [16, 4], P('dp'), may hold values from 0 to 1024, as said below
- masked: int32 [16, 1024], P('dp', 'seq'), may hold values 0 or 1
- residues: int32 [16, 1024], P('dp', 'seq'), may hold values from 0 to 29
- readout: bfloat16 [1280, 30], replicated, may hold values from -0.15625 to 0.15625
- first_gain: float32 [2, 1280], P('section'), may hold values from 0.5 to 1.5
- first_shift: float32 [2, 1280], P('section'), may hold values from -2 to 2
- in_weight: bfloat16 [2, 1280, 640], P('section'), may hold values from -0.15625 to 0.15625
- in_bias: float32 [2, 640], P('section'), may hold values from -2 to 2
- second_gain: float32 [2, 640], P('section'), may hold values from 0.5 to 1.5
- second_shift: float32 [2, 640], P('section'), may hold values from -2 to 2
- conv_weight: bfloat16 [2, 5, 640, 640], P('section'), may hold values from -0.109375 to 0.109375
- conv_bias: float32 [2, 640], P('section'), may hold values from -2 to 2
- third_gain: float32 [2, 640], P('section'), may hold values from 0.5 to 1.5
- third_shift: float32 [2, 640], P('section'), may hold values from -2 to 2
- out_weight: bfloat16 [2, 640, 1280], P('section'), may hold values from -0.25 to 0.25
- out_bias: float32 [2, 1280], P('section'), may hold values from -2 to 2
Outputs:
- boundary_out: bfloat16 [2, 16, 1024, 1280], P('section', 'dp', 'seq')
- grad_first_gain: float32 [2, 1280], P('section')
- grad_first_shift: float32 [2, 1280], P('section')
- grad_in_weight: float32 [2, 1280, 640], P('section')
- grad_in_bias: float32 [2, 640], P('section')
- grad_second_gain: float32 [2, 640], P('section')
- grad_second_shift: float32 [2, 640], P('section')
- grad_conv_weight: float32 [2, 5, 640, 640], P('section')
- grad_conv_bias: float32 [2, 640], P('section')
- grad_third_gain: float32 [2, 640], P('section')
- grad_third_shift: float32 [2, 640], P('section')
- grad_out_weight: float32 [2, 640, 1280], P('section')
- grad_out_bias: float32 [2, 1280], P('section')
- type_scores: float32 [30], replicated
- type_counts: int32 [30], replicated
The draws below stay inside these ranges and needn't reach their ends.
Inputs may be any that keep to these rules, and one draw needn't show every extreme that they name: `lengths`: the items of a row lie one after another from position 0 and the rest of the row is padding; in each aligned block of 4 rows one row is a single item of 1024 positions.
All inputs are finite; a program needn't handle non-finite values. No bound on the sum of `masked` on one device may be relied on, other than what follows from the above.
Results may differ from the reference program's by a relative error of at most 0.012.
Values may be sent and summed in bfloat16 or wider, within the bound.
A program may use at most 256 MiB of HBM per device.

```python
import jax
import jax.numpy as jnp
from jax import lax

D = 1280
H = 640
KERNEL = 5
VOCAB = 30
DILATION_STEP = 128
ITEMS = 4
MB = 4
ROW_LEN = 1024
ROWS = 16


def draw_lengths(key, part):
    key = jax.random.fold_in(key, 11)
    first_key, second_key = jax.random.split(key)
    spans = jax.random.randint(first_key, (ROWS, ITEMS), ROW_LEN // (4 * ITEMS), ROW_LEN // ITEMS + 1)
    whole_row = jax.random.randint(second_key, (ROWS // MB,), 0, MB)
    row_ids = jnp.arange(ROWS, dtype=jnp.int32)
    chosen = row_ids % MB == jnp.repeat(whole_row, MB)
    single = jnp.where(jnp.arange(ITEMS, dtype=jnp.int32) == 0, ROW_LEN, 0)
    return jnp.where(chosen[:, None], single[None, :], spans).astype(jnp.int32)


def plant(values, own_key, smallest, high):
    dims = values.shape
    spot = [jax.random.randint(jax.random.fold_in(own_key, axis), (), 0, dims[axis]) for axis in range(len(dims))]
    values = values.at[tuple(spot)].set(smallest)
    longest = dims.index(max(dims))
    spot[longest] = (spot[longest] + 1) % dims[longest]
    return values.at[tuple(spot)].set(high)


def shard_levels(stream_key, shape, shards, least, high):
    factor_of = 1.0
    for axis_at, parts in shards:
        heights = jax.random.uniform(jax.random.fold_in(jax.random.fold_in(stream_key, 6), axis_at), (parts,), jnp.float32, least / len(shards), high / len(shards))
        factor_of = factor_of * jnp.repeat(jnp.exp(heights), shape[axis_at] // parts).reshape((-1,) + (1,) * (len(shape) - 1 - axis_at))
    return factor_of


def gaussian(rng, dims, scale, reach, cuts=(), kind=jnp.bfloat16):
    drawn = scale * jax.random.normal(rng, dims, jnp.float32)
    if cuts:
        drawn = drawn * shard_levels(rng, dims, cuts, -0.22, 0.18)
    return jnp.clip(drawn, -reach, reach).astype(kind)


def setup_inputs(seed: int = 0) -> dict:
    splits = jax.random.split(jax.random.key(seed), 18)
    boundary = gaussian(splits[0], (2, ROWS, ROW_LEN, D), 1.0, 6.0, ((0, 2), (1, 4), (2, 4)))
    lengths = draw_lengths(jax.random.fold_in(splits[17], 71), 0)
    masked = plant((jax.random.randint(splits[2], (ROWS, ROW_LEN), 0, 20) < 3).astype(jnp.int32), jax.random.fold_in(splits[2], 1), 0, 1)
    residues = plant(jax.random.randint(splits[3], (ROWS, ROW_LEN), 0, VOCAB), jax.random.fold_in(splits[3], 1), 0, VOCAB - 1).astype(jnp.int32)
    readout = gaussian(splits[4], (D, VOCAB), D ** -0.5, 0.15625)
    first_gain = jnp.clip(1.0 + 0.1 * jax.random.normal(splits[5], (2, D), jnp.float32), 0.5, 1.5)
    first_shift = gaussian(splits[6], (2, D), 0.3, 2.0, ((0, 2),), jnp.float32)
    in_weight = gaussian(splits[7], (2, D, H), D ** -0.5, 0.15625, ((0, 2),))
    in_bias = gaussian(splits[8], (2, H), 0.3, 2.0, ((0, 2),), jnp.float32)
    second_gain = jnp.clip(1.0 + 0.1 * jax.random.normal(splits[9], (2, H), jnp.float32), 0.5, 1.5)
    second_shift = gaussian(splits[10], (2, H), 0.3, 2.0, ((0, 2),), jnp.float32)
    conv_weight = gaussian(splits[11], (2, KERNEL, H, H), (KERNEL * H) ** -0.5, 0.109375, ((0, 2),))
    conv_bias = gaussian(splits[12], (2, H), 0.3, 2.0, ((0, 2),), jnp.float32)
    third_gain = jnp.clip(1.0 + 0.1 * jax.random.normal(splits[13], (2, H), jnp.float32), 0.5, 1.5)
    third_shift = gaussian(splits[14], (2, H), 0.3, 2.0, ((0, 2),), jnp.float32)
    out_weight = gaussian(splits[15], (2, H, D), H ** -0.5, 0.25, ((0, 2),))
    out_bias = gaussian(splits[16], (2, D), 0.3, 2.0, ((0, 2),), jnp.float32)
    return dict(boundary=boundary, lengths=lengths, masked=masked, residues=residues, readout=readout, first_gain=first_gain, first_shift=first_shift, in_weight=in_weight, in_bias=in_bias, second_gain=second_gain, second_shift=second_shift, conv_weight=conv_weight, conv_bias=conv_bias, third_gain=third_gain, third_shift=third_shift, out_weight=out_weight, out_bias=out_bias)


EPSILON = 1e-05
PRECISE = lax.Precision.HIGHEST

@jax.custom_vjp
def lower_part(v):
    return lax.optimization_barrier(v.astype(jnp.bfloat16)).astype(jnp.float32)

@jax.custom_vjp
def low_back(v):
    return v

def low_keep(v):
    return (lower_part(v), None)

def low_pass(kept, grad):
    return (grad,)

def back_keep(v):
    return (v, None)

def back_low(kept, grad):
    return (lower_part(grad),)
lower_part.defvjp(low_keep, low_pass)
low_back.defvjp(back_keep, back_low)

def norm_act(values, gain, bias, genuine_rows):
    average = lax.optimization_barrier(jnp.mean(values, axis=-1, keepdims=True))
    centred = values - average
    spread = lax.optimization_barrier(jnp.mean(centred * centred, axis=-1, keepdims=True))
    normalized = centred * lax.rsqrt(spread + EPSILON) * gain + bias
    return jax.nn.gelu(normalized, approximate=False) * genuine_rows

def segment_of(lengths_row):
    item_ends = jnp.cumsum(lengths_row, dtype=jnp.int32)
    position_ids = jnp.arange(ROW_LEN, dtype=jnp.int32)
    return lax.optimization_barrier(jnp.sum((position_ids[:, None] >= item_ends[None, :]).astype(jnp.int32), axis=1, dtype=jnp.int32))

def dilated_conv(acts, conv_weight, segment_slice, dilation_rate):
    row_count = acts.shape[0]
    margin = 2 * dilation_rate
    padded = jnp.pad(acts, ((margin, margin), (0, 0)))
    padded_segment = jnp.pad(segment_slice, (margin, margin), constant_values=-1)
    real_item = segment_slice < ITEMS
    taps = []
    for tap_index in range(KERNEL):
        start = margin + (tap_index - 2) * dilation_rate
        piece = padded[start:start + row_count]
        valid = ((padded_segment[start:start + row_count] == segment_slice) & real_item)[:, None]
        taps.append(jnp.where(valid, piece, 0.0))
    stacked = jnp.concatenate(taps, axis=1)
    flat_weight = conv_weight.reshape(KERNEL * conv_weight.shape[1], conv_weight.shape[2])
    return jnp.dot(stacked, flat_weight, precision=PRECISE)

def residual_block(values, weights, segment_slice, genuine_rows, dilation_rate):
    first_gain, first_shift, in_weight, in_bias, second_gain, second_shift, conv_weight, conv_bias, third_gain, third_shift, out_weight, out_bias = weights
    values = low_back(values)
    first_act = lower_part(norm_act(values, first_gain, first_shift, genuine_rows))
    first_pre = low_back(jnp.dot(first_act, in_weight, precision=PRECISE) + in_bias)
    second_act = lower_part(norm_act(first_pre, second_gain, second_shift, genuine_rows))
    second_pre = low_back(dilated_conv(second_act, conv_weight, segment_slice, dilation_rate) + conv_bias)
    third_act = lower_part(norm_act(second_pre, third_gain, third_shift, genuine_rows))
    third_pre = low_back(jnp.dot(third_act, out_weight, precision=PRECISE) + out_bias)
    return values + third_pre

def reference(boundary, lengths, masked, residues, readout, first_gain, first_shift, in_weight, in_bias, second_gain, second_shift, conv_weight, conv_bias, third_gain, third_shift, out_weight, out_bias):
    stacked_weights = (first_gain, first_shift, in_weight, in_bias, second_gain, second_shift, conv_weight, conv_bias, third_gain, third_shift, out_weight, out_bias)
    lower = tuple((item[0].astype(jnp.float32) for item in stacked_weights))
    upper = tuple((item[1].astype(jnp.float32) for item in stacked_weights))
    readout_float = readout.astype(jnp.float32)
    vocab_ids = jnp.arange(VOCAB, dtype=jnp.int32)

    def row_step(totals, row_data):
        block_in, cotangent, lengths_row, masked_row, residue_row = row_data
        segment_slice = segment_of(lengths_row)
        genuine_rows = (segment_slice < ITEMS).astype(jnp.float32)[:, None]

        def stack_forward(start_values, lower_weights, upper_weight_set):
            central_part = lower_part(residual_block(start_values, lower_weights, segment_slice, genuine_rows, 1))
            return lower_part(residual_block(central_part, upper_weight_set, segment_slice, genuine_rows, DILATION_STEP))
        result, pullback = jax.vjp(stack_forward, block_in.astype(jnp.float32), lower, upper)
        input_grad, lower_grad, upper_grad = pullback(cotangent.astype(jnp.float32))
        logits = jnp.dot(result, readout_float, precision=PRECISE)
        probability = jax.nn.softmax(logits, axis=-1)
        one_hot = (residue_row[:, None] == vocab_ids[None, :]).astype(jnp.float32)
        chosen = masked_row.astype(jnp.float32) * genuine_rows[:, 0]
        truth = lax.optimization_barrier(jnp.sum(one_hot * probability, axis=1))
        type_hits = lax.optimization_barrier(jnp.sum(one_hot * (chosen * truth)[:, None], axis=0))
        type_tally = lax.optimization_barrier(jnp.sum(one_hot * chosen[:, None], axis=0))
        totals = jax.tree.map(jnp.add, totals, (lower_grad, upper_grad, type_hits, type_tally))
        return (totals, (result.astype(jnp.bfloat16), input_grad.astype(jnp.bfloat16)))
    starting = (jax.tree.map(jnp.zeros_like, lower), jax.tree.map(jnp.zeros_like, upper), jnp.zeros((VOCAB,), jnp.float32), jnp.zeros((VOCAB,), jnp.float32))
    totals, (results, input_grads) = lax.scan(row_step, starting, (boundary[0], boundary[1], lengths, masked, residues))
    lower_total, upper_total, type_hits, type_tally = totals
    boundary_out = jnp.stack([input_grads, results], axis=0)
    grad_first_gain, grad_first_shift, grad_in_weight, grad_in_bias, grad_second_gain, grad_second_shift, grad_conv_weight, grad_conv_bias, grad_third_gain, grad_third_shift, grad_out_weight, grad_out_bias = tuple((jnp.stack([early, later], axis=0) for early, later in zip(lower_total, upper_total)))
    type_scores = type_hits / jnp.maximum(type_tally, 1.0)
    type_counts = type_tally.astype(jnp.int32)
    return (boundary_out, grad_first_gain, grad_first_shift, grad_in_weight, grad_in_bias, grad_second_gain, grad_second_shift, grad_conv_weight, grad_conv_bias, grad_third_gain, grad_third_shift, grad_out_weight, grad_out_bias, type_scores, type_counts)
```

```python
import functools

import jax
import jax.numpy as jnp
from jax import lax
from jax.experimental import pallas as pl
from jax.experimental.pallas import tpu as pltpu
from jax.sharding import PartitionSpec as P

KERNEL = 5
VOCAB = 30
DILATION_STEP = 128
ITEMS = 4


EPSILON = 1e-05


MESH = pl.DeviceIdType.MESH
WIDE = 640
SUBS = 2

def ring_sizes(rows, nodes):
    units = -(-rows // (nodes * 16))
    long = -(-units // 2)
    return [[16 * ((way + i) // SUBS) for i in range(SUBS)] for way in (long, units - long)]


def ring_kernel(ny, nz, sizes, w_ref, s_ref, o_ref, t_ref, core_land, *rest):
    nodes = ny * nz
    flows = [(way, i) for way in range(2) for i in range(len(sizes[way])) if sizes[way][i]]
    lands = rest[:len(flows)]
    small_land, core_send, core_recv, ring_send, ring_recv, back_send, back_recv, small_send, small_recv = rest[len(flows):]
    s = lax.axis_index("section")
    q = lax.axis_index("seq")
    d = lax.axis_index("dp")
    core = q % 2
    ypos = q // 2
    odd = ypos % 2
    spot = ypos * nz + d + odd * (nz - 1 - 2 * d)

    def at_spot(place):
        yy = place // nz
        dd = place % nz
        dd = dd + (yy % 2) * (nz - 1 - 2 * dd)
        return (s, yy * 2 + core, dd)

    other_core = (s, q + 1 - 2 * core, d)
    other_x = (1 - s, q, d)
    ahead = at_spot((spot + 1) % nodes)
    behind = at_spot((spot + nodes - 1) % nodes)
    half = sum(sum(way) for way in sizes) * nodes
    turn = [1 - 2 * core, 2 * core - 1]

    peers = [other_core]
    reach = 1
    while reach < ny:
        peers.append((s, q + 2 * reach - 4 * reach * ((ypos // reach) % 2), d))
        reach *= 2
    reach = 1
    while reach < nz:
        peers.append((s, q, d + reach - 2 * reach * ((d // reach) % 2)))
        reach *= 2

    barrier = pltpu.get_barrier_semaphore()
    greet = [other_core, other_x, ahead, behind] + peers[1:]
    for peer in greet:
        pl.semaphore_signal(barrier, inc=1, device_id=peer, device_id_type=MESH)
    pl.semaphore_wait(barrier, len(greet))

    first = {}
    at = 0
    for way, i in flows:
        first[way, i] = at
        at += sizes[way][i] * nodes

    def rows_of(flow, side, shard):
        way, i = flow
        return pl.ds(pl.multiple_of(side * half + first[flow] + shard * sizes[way][i], 16), sizes[way][i])

    def shard_at(flow, step):
        return (spot + 2 * nodes - turn[flow[0]] * step) % nodes

    def next_of(flow):
        return at_spot((spot + nodes + turn[flow[0]]) % nodes)

    def core_copy(f, shard):
        flow = flows[f]
        return pltpu.make_async_remote_copy(
            src_ref=w_ref.at[rows_of(flow, 1 - core, shard)],
            dst_ref=core_land.at[rows_of(flow, 0, shard)],
            send_sem=core_send.at[f, shard], recv_sem=core_recv.at[f, shard],
            device_id=other_core, device_id_type=MESH)

    def ring_copy(f, step, shard):
        flow = flows[f]
        return pltpu.make_async_remote_copy(
            src_ref=w_ref.at[rows_of(flow, core, shard)],
            dst_ref=lands[f].at[step],
            send_sem=ring_send.at[f, step], recv_sem=ring_recv.at[f, step],
            device_id=next_of(flow), device_id_type=MESH)

    def back_copy(f, step, shard):
        block = o_ref.at[rows_of(flows[f], core, shard)]
        return pltpu.make_async_remote_copy(
            src_ref=block, dst_ref=block,
            send_sem=ring_send.at[f, nodes - 1 + step], recv_sem=ring_recv.at[f, nodes - 1 + step],
            device_id=next_of(flows[f]), device_id_type=MESH)

    def over_copy(f, shard):
        block = o_ref.at[rows_of(flows[f], core, shard)]
        return pltpu.make_async_remote_copy(
            src_ref=block, dst_ref=block,
            send_sem=back_send.at[f, shard], recv_sem=back_recv.at[f, shard],
            device_id=other_core, device_id_type=MESH)

    def add(f, shard, step, target):
        flow = flows[f]
        rows = sizes[flow[0]][flow[1]]
        here = rows_of(flow, core, shard).start
        there = rows_of(flow, 0, shard).start

        def body(i, carry):
            off = pl.multiple_of(i * 16, 16)
            total = w_ref[pl.ds(here + off, 16)].astype(jnp.float32)
            total = total + core_land[pl.ds(there + off, 16)].astype(jnp.float32)
            if step is not None:
                total = total + lands[f][step, pl.ds(off, 16)].astype(jnp.float32)
            target[pl.ds(here + off, 16)] = total.astype(target.dtype)
            return carry

        lax.fori_loop(0, rows // 16, body, 0)

    def to_other_core(step, carry):
        for f, flow in enumerate(flows):
            core_copy(f, shard_at(flow, step)).start()
        return carry

    lax.fori_loop(0, nodes, to_other_core, 0)

    def towards(step, carry):
        for f, flow in enumerate(flows):
            shard = shard_at(flow, step)
            core_copy(f, shard).wait_recv()
            if carry is None:
                add(f, shard, None, w_ref)
            else:
                ring_copy(f, step - 1, shard).wait_recv()
                add(f, shard, step - 1, w_ref)
            ring_copy(f, step, shard).start()
        return carry

    towards(0, None)
    count = s_ref.shape[0]

    def held(k):
        return s_ref if k == 0 else small_land.at[2 * k - 1]

    def small_copy(k):
        last = k == len(peers)
        return pltpu.make_async_remote_copy(
            src_ref=held(k), dst_ref=t_ref.at[pl.ds(count, count)] if last else small_land.at[2 * k],
            send_sem=small_send.at[k], recv_sem=small_recv.at[k],
            device_id=other_x if last else peers[k], device_id_type=MESH)

    def small_step(k):
        if 0 < k <= len(peers):
            small_copy(k - 1).wait_recv()
            small_land[2 * k - 1] = held(k - 1)[...] + small_land[2 * k - 2]
        if k <= len(peers):
            small_copy(k).start()
        if k == len(peers):
            t_ref[pl.ds(0, count)] = held(k)[...]

    small_step(0)
    for k in range(1, len(peers) + 1):
        if k < nodes - 1:
            towards(k, 0)
        small_step(k)
    lax.fori_loop(min(len(peers) + 1, nodes - 1), nodes - 1, towards, 0)
    for f, flow in enumerate(flows):
        shard = shard_at(flow, nodes - 1)
        core_copy(f, shard).wait_recv()
        ring_copy(f, nodes - 2, shard).wait_recv()
        add(f, shard, nodes - 2, o_ref)
        back_copy(f, 0, shard).start()
        over_copy(f, shard).start()

    def back(step, carry):
        for f, flow in enumerate(flows):
            shard = shard_at(flow, nodes - 1 + step)
            back_copy(f, step - 1, shard).wait_recv()
            back_copy(f, step, shard).start()
            over_copy(f, shard).start()
        return carry

    lax.fori_loop(1, nodes - 1, back, 0)
    for f, flow in enumerate(flows):
        shard = shard_at(flow, 2 * nodes - 2)
        back_copy(f, nodes - 2, shard).wait_recv()
        over_copy(f, shard).start()

    def settle(step, carry):
        for f, flow in enumerate(flows):
            core_copy(f, step).wait_send()
            over_copy(f, step).wait()
        return carry

    def settle_ring(step, carry):
        for f, flow in enumerate(flows):
            ring_copy(f, step, 0).wait_send()
            back_copy(f, step, 0).wait_send()
        return carry

    lax.fori_loop(0, nodes, settle, 0)
    lax.fori_loop(0, nodes - 1, settle_ring, 0)
    for k in range(len(peers) + 1):
        small_copy(k).wait_send()
    small_copy(len(peers)).wait_recv()


def sum_everywhere(big, small, ny, nz, cid=1):
    rows = big.shape[0]
    nodes = ny * nz
    sizes = ring_sizes(rows // 2, nodes)
    flows = [(w, i) for w in range(2) for i in range(len(sizes[w])) if sizes[w][i]]
    half = sum(map(sum, sizes)) * nodes
    assert rows == 2 * half, (rows, half, sizes)
    n = len(flows)
    return pl.pallas_call(
        functools.partial(ring_kernel, ny, nz, sizes),
        out_shape=(jax.ShapeDtypeStruct(big.shape, big.dtype),
                   jax.ShapeDtypeStruct((2 * small.shape[0], small.shape[1]), small.dtype)),
        in_specs=[pl.BlockSpec(memory_space=pltpu.VMEM)] * 2,
        out_specs=[pl.BlockSpec(memory_space=pltpu.VMEM)] * 2,
        scratch_shapes=[pltpu.VMEM((half, WIDE), big.dtype)]
        + [pltpu.VMEM((nodes - 1, sizes[w][i], WIDE), big.dtype) for w, i in flows]
        + [pltpu.VMEM((16,) + small.shape, small.dtype)]
        + [pltpu.SemaphoreType.DMA((n, nodes))] * 2
        + [pltpu.SemaphoreType.DMA((n, 2 * nodes - 2))] * 2
        + [pltpu.SemaphoreType.DMA((n, nodes))] * 2
        + [pltpu.SemaphoreType.DMA((8,))] * 2,
        compiler_params=pltpu.CompilerParams(collective_id=cid, has_side_effects=True, vmem_limit_bytes=56 << 20),
    )(big, small)


def from_behind(value, axis, by):
    length = lax.axis_size(axis)
    pairs = [(i, i + by) for i in range(length) if 0 <= i + by < length]
    return lax.ppermute(value, axis, pairs)


def norm_act(values, gain, bias, genuine_rows):
    average = jnp.mean(values, axis=-1, keepdims=True)
    centred = values - average
    spread = jnp.mean(centred * centred, axis=-1, keepdims=True)
    normalized = centred * lax.rsqrt(spread + EPSILON) * gain + bias
    return jax.nn.gelu(normalized, approximate=False) * genuine_rows


def local_pullback(values, gain, bias, genuine_rows, cotangent):

    def piece(inner, inner_gain, inner_bias):
        return norm_act(inner, inner_gain, inner_bias, genuine_rows)

    result, pullback = jax.vjp(piece, values, gain, bias)
    return pullback(cotangent)


def conv_rims(values):
    pieces = []
    for offset in (2, 1, -1, -2):
        pieces.append(from_behind(values, "seq", offset))
    return jnp.concatenate([pieces[0], pieces[1], values, pieces[2], pieces[3]], axis=0)


def grad_rims(values):
    pieces = []
    for offset in (2, 1, -1, -2):
        pieces.append(from_behind(values, "seq", offset))
    return jnp.concatenate([pieces[0], pieces[1], values, pieces[2], pieces[3]], axis=0)


def make_context(lengths, batch_index, seq_first, positions, row_len):
    lengths_row = lengths[batch_index]
    item_ends = jnp.cumsum(lengths_row, dtype=jnp.int32)
    position_ids = seq_first - 2 * positions + jnp.arange(5 * positions, dtype=jnp.int32)
    segment_ext = jnp.sum(
        (position_ids[:, None] >= item_ends[None, :]).astype(jnp.int32), axis=1, dtype=jnp.int32
    )
    inside = (position_ids >= 0) & (position_ids < row_len)
    segment_ext = jnp.where(inside, segment_ext, -1)
    segment_own = segment_ext[2 * positions : 3 * positions]
    genuine_rows = ((segment_own >= 0) & (segment_own < ITEMS)).astype(jnp.float32)[:, None]
    return (segment_ext, segment_own, genuine_rows)


def tap_mask(segment_ext, segment_own, start, positions):
    other = lax.dynamic_slice_in_dim(segment_ext, start, positions, 0)
    valid = (other == segment_own) & (segment_own >= 0) & (segment_own < ITEMS)
    return valid.astype(jnp.bfloat16)[:, None]


def gather_taps(extended, segment_ext, segment_own, dilation_rate, positions, direction):
    taps = []
    for tap_index in range(KERNEL):
        start = 2 * positions + direction * (tap_index - 2) * dilation_rate
        piece = lax.dynamic_slice_in_dim(extended, start, positions, 0)
        taps.append(piece * tap_mask(segment_ext, segment_own, start, positions))
    return jnp.concatenate(taps, axis=1)


def forward_block(block_in, weights, context, dilation_rate):
    (
        first_gain,
        first_shift,
        in_weight,
        in_bias,
        second_gain,
        second_shift,
        conv_weight,
        conv_bias,
        third_gain,
        third_shift,
        out_weight,
        out_bias,
    ) = weights
    segment_ext, segment_own, genuine_rows = context
    positions = block_in.shape[0]
    values = block_in.astype(jnp.float32)
    first_act = norm_act(values, first_gain, first_shift, genuine_rows).astype(jnp.bfloat16)
    first_pre = jnp.dot(first_act, in_weight, preferred_element_type=jnp.float32) + in_bias
    second_act = norm_act(first_pre, second_gain, second_shift, genuine_rows).astype(jnp.bfloat16)
    extended = conv_rims(second_act)
    stacked = gather_taps(extended, segment_ext, segment_own, dilation_rate, positions, 1)
    conv_flat = conv_weight.reshape(-1, conv_weight.shape[2])
    second_pre = jnp.dot(stacked, conv_flat, preferred_element_type=jnp.float32) + conv_bias
    third_act = norm_act(second_pre, third_gain, third_shift, genuine_rows).astype(jnp.bfloat16)
    third_pre = jnp.dot(third_act, out_weight, preferred_element_type=jnp.float32) + out_bias
    block_out = (values + third_pre).astype(jnp.bfloat16)
    return (block_out, (values, first_act, first_pre, stacked, second_pre, third_act))


def backward_block(grad_out, kept, weights, context, dilation_rate):
    (
        first_gain,
        first_shift,
        in_weight,
        in_bias,
        second_gain,
        second_shift,
        conv_weight,
        conv_bias,
        third_gain,
        third_shift,
        out_weight,
        out_bias,
    ) = weights
    values, first_act, first_pre, stacked, second_pre, third_act = kept
    segment_ext, segment_own, genuine_rows = context
    positions = grad_out.shape[0]
    contract = (((0,), (0,)), ((), ()))
    grad_float = grad_out.astype(jnp.float32)
    grad_out_bias = jnp.sum(grad_float, axis=0)
    grad_out_weight = lax.dot_general(
        third_act, grad_out, contract, preferred_element_type=jnp.float32
    )
    grad_third_act = jnp.dot(grad_out, out_weight.T, preferred_element_type=jnp.float32)
    grad_second_pre, grad_third_gain, grad_third_shift = local_pullback(
        second_pre, third_gain, third_shift, genuine_rows, grad_third_act
    )
    grad_second_low = grad_second_pre.astype(jnp.bfloat16)
    grad_conv_bias = jnp.sum(grad_second_low, axis=0, dtype=jnp.float32)
    grad_conv_weight = lax.dot_general(
        stacked, grad_second_low, contract, preferred_element_type=jnp.float32
    ).reshape(conv_weight.shape)
    grad_extended = grad_rims(grad_second_low)
    back_stacked = gather_taps(
        grad_extended, segment_ext, segment_own, dilation_rate, positions, -1
    )
    conv_back = jnp.transpose(conv_weight, (0, 2, 1)).reshape(-1, conv_weight.shape[1])
    grad_second_act = jnp.dot(back_stacked, conv_back, preferred_element_type=jnp.float32)
    grad_first_pre, grad_second_gain, grad_second_shift = local_pullback(
        first_pre, second_gain, second_shift, genuine_rows, grad_second_act
    )
    grad_first_low = grad_first_pre.astype(jnp.bfloat16)
    grad_in_bias = jnp.sum(grad_first_low, axis=0, dtype=jnp.float32)
    grad_in_weight = lax.dot_general(
        first_act, grad_first_low, contract, preferred_element_type=jnp.float32
    )
    grad_first_act = jnp.dot(grad_first_low, in_weight.T, preferred_element_type=jnp.float32)
    grad_values, grad_first_gain, grad_first_shift = local_pullback(
        values, first_gain, first_shift, genuine_rows, grad_first_act
    )
    grad_in = (grad_float + grad_values).astype(jnp.bfloat16)
    return (
        grad_in,
        (
            grad_first_gain,
            grad_first_shift,
            grad_in_weight,
            grad_in_bias,
            grad_second_gain,
            grad_second_shift,
            grad_conv_weight,
            grad_conv_bias,
            grad_third_gain,
            grad_third_shift,
            grad_out_weight,
            grad_out_bias,
        ),
    )


def shards(
    boundary,
    lengths,
    masked,
    residues,
    readout,
    first_gain,
    first_shift,
    in_weight,
    in_bias,
    second_gain,
    second_shift,
    conv_weight,
    conv_bias,
    third_gain,
    third_shift,
    out_weight,
    out_bias,
):
    weights = tuple(
        (
            item[0]
            for item in (
                first_gain,
                first_shift,
                in_weight,
                in_bias,
                second_gain,
                second_shift,
                conv_weight,
                conv_bias,
                third_gain,
                third_shift,
                out_weight,
                out_bias,
            )
        )
    )
    section_index = lax.axis_index("section")
    leading_section = section_index == 0
    last_section = section_index == lax.axis_size("section") - 1
    micro_count = boundary.shape[1]
    positions = boundary.shape[2]
    width = boundary.shape[3]
    row_len = positions * lax.axis_size("seq")
    seq_first = lax.axis_index("seq") * positions
    dilation_rate = jnp.where(leading_section, 1, DILATION_STEP)
    vocab_ids = jnp.arange(VOCAB, dtype=jnp.int32)
    incoming = jnp.zeros((positions, width), jnp.bfloat16)
    seen_inputs = []
    kept_list = []
    outputs = []
    type_hits = jnp.zeros((VOCAB,), jnp.float32)
    type_tally = jnp.zeros((VOCAB,), jnp.float32)
    for time_step in range(micro_count + 1):
        offset_index = time_step - section_index
        active = (offset_index >= 0) & (offset_index < micro_count)
        batch_index = jnp.clip(offset_index, 0, micro_count - 1)
        block_in = jnp.where(
            leading_section, boundary[0, min(time_step, micro_count - 1)], incoming
        )
        context = make_context(lengths, batch_index, seq_first, positions, row_len)
        block_out, kept = forward_block(block_in, weights, context, dilation_rate)
        seen_inputs.append(block_in)
        kept_list.append(kept)
        outputs.append(block_out)
        logits = jnp.dot(block_out, readout, preferred_element_type=jnp.float32)
        probability = jax.nn.softmax(logits, axis=-1)
        one_hot = (residues[batch_index][:, None] == vocab_ids[None, :]).astype(jnp.float32)
        chosen = (
            masked[batch_index].astype(jnp.float32)
            * context[2][:, 0]
            * (active & last_section).astype(jnp.float32)
        )
        truth = jnp.sum(one_hot * probability, axis=1)
        type_hits = type_hits + jnp.sum(one_hot * (chosen * truth)[:, None], axis=0)
        type_tally = type_tally + jnp.sum(one_hot * chosen[:, None], axis=0)
        if time_step < micro_count:
            incoming = from_behind(block_out, "section", 1)
    grad_totals = tuple((jnp.zeros(item.shape, jnp.float32) for item in weights))
    incoming_grad = jnp.zeros((positions, width), jnp.bfloat16)
    input_grads = []
    for time_step in range(micro_count + 1):
        offset_index = time_step - 1 + section_index
        active = (offset_index >= 0) & (offset_index < micro_count)
        batch_index = jnp.clip(offset_index, 0, micro_count - 1)
        lower_step = min(max(time_step - 1, 0), micro_count)
        upper_step = min(time_step + 1, micro_count)
        context = make_context(lengths, batch_index, seq_first, positions, row_len)
        kept = jax.tree.map(
            lambda early, later: jnp.where(leading_section, early, later),
            kept_list[lower_step],
            kept_list[upper_step],
        )
        grad_out = jnp.where(
            leading_section, incoming_grad, boundary[0, min(time_step, micro_count - 1)]
        )
        grad_in, grads = backward_block(grad_out, kept, weights, context, dilation_rate)
        grad_totals = tuple(
            (total + jnp.where(active, grad, 0.0) for total, grad in zip(grad_totals, grads))
        )
        input_grads.append(grad_in)
        if time_step < micro_count:
            incoming_grad = from_behind(grad_in, "section", -1)
    ends_grad = jnp.stack(input_grads[1:], axis=0)
    ends_out = jnp.stack(outputs[1:], axis=0)
    boundary_out = jnp.where(leading_section, ends_grad, ends_out)[None]
    (
        grad_first_gain,
        grad_first_shift,
        grad_in_weight,
        grad_in_bias,
        grad_second_gain,
        grad_second_shift,
        grad_conv_weight,
        grad_conv_bias,
        grad_third_gain,
        grad_third_shift,
        grad_out_weight,
        grad_out_bias,
    ) = grad_totals
    hidden = in_bias.shape[1]
    ny, nz = lax.axis_size("seq") // 2, lax.axis_size("dp")
    taps = conv_weight.shape[1]
    count = (taps + 4) * hidden
    spare = 2 * ny * nz * sum(map(sum, ring_sizes(count // 2, ny * nz))) - count
    big = jnp.concatenate(
        [
            grad_in_weight,
            grad_conv_weight.reshape(taps * hidden, hidden),
            grad_out_weight[:, :hidden],
            grad_out_weight[:, hidden:],
            jnp.zeros((spare, hidden), jnp.float32),
        ]
    ).astype(jnp.bfloat16)
    small = jnp.stack(
        [
            grad_first_gain,
            grad_first_shift,
            grad_out_bias,
            jnp.concatenate([grad_in_bias, grad_second_gain]),
            jnp.concatenate([grad_second_shift, grad_conv_bias]),
            jnp.concatenate([grad_third_gain, grad_third_shift]),
            jnp.pad(type_hits, (0, width - VOCAB)),
            jnp.pad(type_tally, (0, width - VOCAB)),
        ]
    )
    big, small = sum_everywhere(big, small, ny, nz)
    big = big.astype(jnp.float32)
    grad_in_weight = big[None, :width]
    grad_conv_weight = big[width : width + taps * hidden].reshape(conv_weight.shape)
    at = width + taps * hidden
    grad_out_weight = jnp.concatenate([big[at : at + hidden], big[at + hidden : at + 2 * hidden]], axis=1)[None]
    grad_first_gain, grad_first_shift, grad_out_bias = small[0:1], small[1:2], small[2:3]
    grad_in_bias, grad_second_gain = small[3:4, :hidden], small[3:4, hidden:]
    grad_second_shift, grad_conv_bias = small[4:5, :hidden], small[4:5, hidden:]
    grad_third_gain, grad_third_shift = small[5:6, :hidden], small[5:6, hidden:]
    type_hits = small[6, :VOCAB] + small[14, :VOCAB]
    type_tally = small[7, :VOCAB] + small[15, :VOCAB]
    type_scores = type_hits / jnp.maximum(type_tally, 1.0)
    type_counts = type_tally.astype(jnp.int32)
    return (
        boundary_out,
        grad_first_gain,
        grad_first_shift,
        grad_in_weight,
        grad_in_bias,
        grad_second_gain,
        grad_second_shift,
        grad_conv_weight,
        grad_conv_bias,
        grad_third_gain,
        grad_third_shift,
        grad_out_weight,
        grad_out_bias,
        type_scores,
        type_counts,
    )


def solution(mesh):
    in_specs = (
        P("section", "dp", "seq", None),
        P("dp", None),
        P("dp", "seq"),
        P("dp", "seq"),
        P(),
        P("section", None),
        P("section", None),
        P("section", None, None),
        P("section", None),
        P("section", None),
        P("section", None),
        P("section", None, None, None),
        P("section", None),
        P("section", None),
        P("section", None),
        P("section", None, None),
        P("section", None),
    )
    out_specs = (
        P("section", "dp", "seq", None),
        P("section", None),
        P("section", None),
        P("section", None, None),
        P("section", None),
        P("section", None),
        P("section", None),
        P("section", None, None, None),
        P("section", None),
        P("section", None),
        P("section", None),
        P("section", None, None),
        P("section", None),
        P(),
        P(),
    )
    return jax.shard_map(shards, mesh=mesh, in_specs=in_specs, out_specs=out_specs, check_vma=False)
```

```python
import functools

import jax
import jax.numpy as jnp
from jax import lax
from jax.experimental import pallas as pl
from jax.experimental.pallas import tpu as pltpu
from jax.sharding import PartitionSpec as P

KERNEL = 5
VOCAB = 30
DILATION_STEP = 128
ITEMS = 4
EPSILON = 1e-05
ROOT_HALF = 0.7071067811865476
HALF_LOG = -0.7213475204444817
ROOT_TAU = 0.3989422804014327

MESH = pl.DeviceIdType.MESH
WIDE = 640
SUBS = 2
VMEM_BYTES = 64 << 20


def far_rows(left, own, right, offset):
    edge, positions = left.shape[0], own.shape[0]
    first, last = offset + edge, offset + edge + positions
    pieces, at = [], 0
    for block in (left, own, right):
        lo, hi = max(first, at), min(last, at + block.shape[0])
        if lo < hi:
            pieces.append(block[lo - at : hi - at])
        at += block.shape[0]
    return pieces[0] if len(pieces) == 1 else jnp.concatenate(pieces, axis=0)


def act_forward(values, gain, shift, real):
    scale = 1.0 / values.shape[1]
    centred = values - jnp.sum(values, axis=1, keepdims=True) * scale
    spread = jnp.sum(centred * centred, axis=1, keepdims=True) * scale
    inverse = lax.rsqrt(spread + EPSILON)
    hat = centred * inverse
    moved = hat * gain + shift
    below = (0.5 + 0.5 * lax.erf(moved * ROOT_HALF)) * real
    density = jnp.exp2(moved * moved * HALF_LOG) * (ROOT_TAU * real)
    return moved * below, hat, below + moved * density, inverse


def fold(values):
    rows, columns = values.shape
    return jnp.sum(values.reshape(rows // 8, 8, columns), axis=0)


def act_backward(grad, hat, slope, inverse, gain, gain_sum, shift_sum):
    scale = 1.0 / grad.shape[1]
    hat = hat.astype(jnp.float32)
    moved = grad * slope.astype(jnp.float32)
    turned = moved * hat
    shift_sum[...] += fold(moved)
    gain_sum[...] += fold(turned)
    mean = jnp.sum(moved * gain, axis=1, keepdims=True) * scale
    tilt = jnp.sum(turned * gain, axis=1, keepdims=True) * scale
    return inverse * (moved * gain - mean - hat * tilt)


def dot_nn(a, b):
    return jnp.dot(a, b, preferred_element_type=jnp.float32)


def dot_nt(a, b):
    return lax.dot_general(a, b, (((1,), (1,)), ((), ())), preferred_element_type=jnp.float32)


def dot_tn(a, b):
    return lax.dot_general(a, b, (((0,), (0,)), ((), ())), preferred_element_type=jnp.float32)


def blocks_kernel(
    edge,
    boundary, lengths, masked, residues, readout,
    first_gain, first_shift, in_weight, in_bias, second_gain, second_shift, conv_weight, conv_bias,
    third_gain, third_shift, out_weight, out_bias,
    result, big, small,
    buf, w_in, w_conv, w_out, total, hat1, slope1, act1, taps, back_taps,
    hat2, slope2, hat3, slope3, act3, grad1, grad2, rim_left, rim_right, near, masks, spreads,
    sums_wide, sums, hits, tally, stage,
    load_sem, weight_sem, result_sem, hand_send, hand_recv, rim_send, rim_recv, stage_sem,
):
    section = lax.axis_index("section")
    seq = lax.axis_index("seq")
    dp = lax.axis_index("dp")
    n_seq = lax.axis_size("seq")
    rows, positions = buf.shape[0] // 2, buf.shape[1]
    hidden = w_in.shape[1]
    leading = section == 0
    trailing = section == 1
    row_len = n_seq * positions
    first_position = seq * positions
    reach = edge // positions
    dilation = jnp.where(leading, 1, DILATION_STEP)

    def load(m):
        return pltpu.make_async_copy(boundary.at[0, m], buf.at[section * rows + m], load_sem.at[m])

    weight_loads = [
        pltpu.make_async_copy(source.at[0], target, weight_sem.at[i])
        for i, (source, target) in enumerate(((in_weight, w_in), (conv_weight, w_conv), (out_weight, w_out)))
    ]
    load(0).start()
    for copy in weight_loads:
        copy.start()
    for m in range(1, rows):
        load(m).start()

    def partner():
        return (1 - section, seq, dp)

    barrier = pltpu.get_barrier_semaphore()
    pl.semaphore_signal(barrier, inc=1, device_id=partner(), device_id_type=MESH)
    greeted = 1
    for j in range(1, reach + 1):
        for side in (-j, j):
            on = (seq + side >= 0) & (seq + side < n_seq)
            greeted = greeted + on.astype(jnp.int32)

            @pl.when(on)
            def _():
                pl.semaphore_signal(barrier, inc=1, device_id=(section, seq + side, dp), device_id_type=MESH)

    sums_wide[...] = jnp.zeros_like(sums_wide)
    sums[...] = jnp.zeros_like(sums)
    hits[...] = jnp.zeros_like(hits)
    tally[...] = jnp.zeros_like(tally)

    @pl.when(seq < reach)
    def _():
        rim_left[...] = jnp.zeros_like(rim_left)

    @pl.when(seq >= n_seq - reach)
    def _():
        rim_right[...] = jnp.zeros_like(rim_right)

    lane = lax.broadcasted_iota(jnp.int32, (positions, 128), 1)
    place = lax.broadcasted_iota(jnp.int32, (positions, 128), 0) + first_position
    other = place + (lane - KERNEL // 2) * dilation
    for m in range(rows):
        end = 0
        here = jnp.zeros((positions, 128), jnp.int32)
        there = jnp.zeros((positions, 128), jnp.int32)
        for j in range(ITEMS):
            end = end + lengths[m, j]
            here = here + (place >= end).astype(jnp.int32)
            there = there + (other >= end).astype(jnp.int32)
        counts = (here == there) & (here < ITEMS) & (other >= 0) & (other < row_len)
        masks[m] = counts.astype(jnp.float32)

    pl.semaphore_wait(barrier, greeted)

    def hand(m):
        forward = pltpu.make_async_remote_copy(
            src_ref=buf.at[m], dst_ref=buf.at[m], send_sem=hand_send.at[m], recv_sem=hand_recv.at[m],
            device_id=partner(), device_id_type=MESH)
        backward = pltpu.make_async_remote_copy(
            src_ref=hat1.at[m], dst_ref=buf.at[rows + m], send_sem=hand_send.at[m], recv_sem=hand_recv.at[m],
            device_id=partner(), device_id_type=MESH)
        return forward, backward

    def rim_copies(backward, m):
        slot = 2 * backward + m % 2
        own = grad2.at[m] if backward else taps.at[m, KERNEL // 2]
        turn = backward * rows + m

        def copy(source, target, index, to):
            return pltpu.make_async_remote_copy(
                src_ref=source, dst_ref=target, send_sem=rim_send.at[turn, index], recv_sem=rim_recv.at[turn, index],
                device_id=(section, to, dp), device_id_type=MESH)

        near_copies = [
            (seq + 1 < n_seq, seq >= 1,
             copy(own.at[pl.ds(positions - 16, 16)], rim_left.at[slot, pl.ds(edge - 16, 16)], 0, seq + 1)),
            (seq >= 1, seq + 1 < n_seq,
             copy(own.at[pl.ds(0, 16)], rim_right.at[slot, pl.ds(0, 16)], 1, seq - 1)),
        ]
        far_copies = []
        for j in range(1, reach + 1):
            far_copies.append((
                seq + j < n_seq, seq >= j,
                copy(own, rim_left.at[slot, pl.ds(edge - j * positions, positions)], 2 * j - 2, seq + j)))
            far_copies.append((
                seq >= j, seq + j < n_seq,
                copy(own, rim_right.at[slot, pl.ds((j - 1) * positions, positions)], 2 * j - 1, seq - j)))
        return near_copies, far_copies

    def rim_start(backward, m):
        for here, copies in zip((leading, trailing), rim_copies(backward, m)):
            for sends, _, copy in copies:
                pl.when(here & sends)(copy.start)

    def rim_wait(backward, m):
        for here, copies in zip((leading, trailing), rim_copies(backward, m)):
            for sends, receives, copy in copies:
                pl.when(here & receives)(copy.wait_recv)
                pl.when(here & sends)(copy.wait_send)

    def gather(backward, m, own, store):
        slot = 2 * backward + m % 2
        mask = masks[m]

        @pl.when(leading)
        def _():
            near[16 : 16 + positions] = own().astype(jnp.float32)
            near[0:16] = rim_left[slot, edge - 16 : edge].astype(jnp.float32)
            near[16 + positions : 32 + positions] = rim_right[slot, 0:16].astype(jnp.float32)
            for k in range(KERNEL):
                if k != KERNEL // 2:
                    at = 16 + k - KERNEL // 2
                    store(k, jnp.where(mask[:, k : k + 1] > 0, near[at : at + positions], 0.0))

        @pl.when(trailing)
        def _():
            for k in range(KERNEL):
                if k != KERNEL // 2:
                    piece = far_rows(rim_left[slot], own(), rim_right[slot], (k - KERNEL // 2) * DILATION_STEP)
                    store(k, jnp.where(mask[:, k : k + 1] > 0, piece.astype(jnp.float32), 0.0))

    def real_of(m):
        return masks[m][:, KERNEL // 2 : KERNEL // 2 + 1]

    def forward_start(m):
        @pl.when(leading)
        def _():
            load(m).wait()

        @pl.when(trailing)
        def _():
            hand(m)[0].wait_recv()

        real = real_of(m)
        act, hat, slope, inverse = act_forward(buf[m].astype(jnp.float32), first_gain[...], first_shift[...], real)
        act1[m] = act.astype(jnp.bfloat16)
        hat1[m] = hat.astype(jnp.bfloat16)
        slope1[m] = slope.astype(jnp.bfloat16)
        spreads[m, 0] = inverse
        pre = dot_nn(act1[m], w_in[...]) + in_bias[...]
        act, hat, slope, inverse = act_forward(pre, second_gain[...], second_shift[...], real)
        taps[m, KERNEL // 2] = act.astype(jnp.bfloat16)
        rim_start(0, m)
        hat2[m] = hat.astype(jnp.bfloat16)
        slope2[m] = slope.astype(jnp.bfloat16)
        spreads[m, 1] = inverse

    def forward_end(m):
        def store(k, value):
            taps[m, k] = value.astype(jnp.bfloat16)

        rim_wait(0, m)
        gather(0, m, lambda: taps[m, KERNEL // 2], store)
        pre = conv_bias[...]
        for k in range(KERNEL):
            pre = pre + dot_nn(taps[m, k], w_conv[k])
        act, hat, slope, inverse = act_forward(pre, third_gain[...], third_shift[...], real_of(m))
        act3[m] = act.astype(jnp.bfloat16)
        hat3[m] = hat.astype(jnp.bfloat16)
        slope3[m] = slope.astype(jnp.bfloat16)
        spreads[m, 2] = inverse
        out = buf[m].astype(jnp.float32) + (dot_nn(act3[m], w_out[...]) + out_bias[...])
        buf[m] = out.astype(jnp.bfloat16)

        @pl.when(leading)
        def _():
            hand(m)[0].start()

        @pl.when(trailing)
        def _():
            pltpu.make_async_copy(buf.at[m], result.at[0, m], result_sem.at[m]).start()
            logits = dot_nt(readout[...], buf[m])
            kind = lax.broadcasted_iota(jnp.int32, logits.shape, 0)
            logits = jnp.where(kind < VOCAB, logits, -1e30)
            odds = jnp.exp(logits - jnp.max(logits, axis=0, keepdims=True))
            odds = odds / jnp.sum(odds, axis=0, keepdims=True)
            end = lengths[m, 0]
            for j in range(1, ITEMS):
                end = end + lengths[m, j]
            spot = lax.broadcasted_iota(jnp.int32, (1, positions), 1) + first_position
            chosen = jnp.where(spot < end, masked[pl.ds(m, 1)].astype(jnp.float32), 0.0)
            chosen = jnp.where(kind == residues[pl.ds(m, 1)], chosen, 0.0)
            hits[...] += chosen * odds
            tally[...] += chosen

    def backward_start(m):
        @pl.when(leading)
        def _():
            hand(m)[1].wait_recv()

        @pl.when(trailing)
        def _():
            load(m).wait()

        sums_wide[2] += fold(buf[rows + m].astype(jnp.float32))
        grad = dot_nt(buf[rows + m], w_out[...])
        low = act_backward(
            grad, hat3[m], slope3[m], spreads[m, 2], third_gain[...], sums.at[4], sums.at[5]
        ).astype(jnp.bfloat16)
        grad2[m] = low
        back_taps[KERNEL // 2] = low
        rim_start(1, m)
        sums[3] += fold(low.astype(jnp.float32))

    def backward_end(m):
        def store(k, value):
            back_taps[k] = value.astype(jnp.bfloat16)

        rim_wait(1, m)
        gather(1, m, lambda: grad2[m], store)
        grad = dot_nt(back_taps[0], w_conv[KERNEL - 1])
        for k in range(1, KERNEL):
            grad = grad + dot_nt(back_taps[k], w_conv[KERNEL - 1 - k])
        low = act_backward(
            grad, hat2[m], slope2[m], spreads[m, 1], second_gain[...], sums.at[1], sums.at[2]
        ).astype(jnp.bfloat16)
        grad1[m] = low
        grad = dot_nt(low, w_in[...])
        grad = act_backward(
            grad, hat1[m], slope1[m], spreads[m, 0], first_gain[...], sums_wide.at[0], sums_wide.at[1]
        )
        hat1[m] = (buf[rows + m].astype(jnp.float32) + grad).astype(jnp.bfloat16)

        @pl.when(leading)
        def _():
            pltpu.make_async_copy(hat1.at[m], result.at[0, m], result_sem.at[m]).start()

        @pl.when(trailing)
        def _():
            hand(m)[1].start()

        sums[0] += fold(low.astype(jnp.float32))

    wide = buf.shape[2] // hidden

    def add_block(block, value):
        total[pl.ds(block * hidden, hidden)] += value

    def weights_out(m):
        for j in range(wide):
            add_block(wide + KERNEL + j, dot_tn(act3[m], buf[rows + m, :, j * hidden : (j + 1) * hidden]))

    def weights_rest(m):
        for k in range(KERNEL):
            add_block(wide + k, dot_tn(taps[m, k], grad2[m]))
        for j in range(wide):
            add_block(j, dot_tn(act1[m, :, j * hidden : (j + 1) * hidden], grad1[m]))

    def step(i, carry):
        m_front = i - 1
        m_back = jnp.where(leading, i - 1 - rows, i - 1)
        m_next = i
        m_sum = i - 1 - rows

        def on(m, allowed=True):
            return (m >= 0) & (m < rows) & allowed

        @pl.when(i == 1)
        def _():
            weight_loads[1].wait()
            weight_loads[2].wait()

        @pl.when(on(m_front))
        def _():
            forward_end(m_front)

        @pl.when(on(m_back))
        def _():
            backward_start(m_back)

        @pl.when(i == 0)
        def _():
            weight_loads[0].wait()

        @pl.when(on(m_next))
        def _():
            forward_start(m_next)

        @pl.when((leading & (i == 3)) | (trailing & (i == 0)))
        def _():
            total[...] = jnp.zeros_like(total)

        @pl.when(on(m_sum))
        def _():
            weights_out(m_sum)

        @pl.when(on(m_back))
        def _():
            backward_end(m_back)

        @pl.when(on(m_sum))
        def _():
            weights_rest(m_sum)

        return carry

    lax.fori_loop(0, 2 * rows + 1, step, 0)

    blocks = wide + KERNEL + wide

    def give(b, slot):
        return pltpu.make_async_copy(stage.at[slot], big.at[pl.ds(b * hidden, hidden)], stage_sem.at[slot])

    for b in range(blocks):
        slot = b % 2
        if b >= 2:
            give(b - 2, slot).wait()
        stage[slot] = total[b * hidden : (b + 1) * hidden].astype(jnp.bfloat16)
        give(b, slot).start()
    for b in range(blocks - 2, blocks):
        give(b, b % 2).wait()
    spare = big.shape[0] - blocks * hidden
    stage[0, :spare] = jnp.zeros((spare, hidden), jnp.bfloat16)
    tail = pltpu.make_async_copy(stage.at[0, pl.ds(0, spare)], big.at[pl.ds(blocks * hidden, spare)], stage_sem.at[0])
    tail.start()
    for i in range(3):
        small[i : i + 1, :] = jnp.sum(sums_wide[i], axis=0, keepdims=True)
    for i in range(6):
        small[3 + i // 2 : 4 + i // 2, (i % 2) * hidden : (i % 2 + 1) * hidden] = jnp.sum(sums[i], axis=0, keepdims=True)
    small[6:8, :] = jnp.zeros((2, small.shape[1]), jnp.float32)
    ones = jnp.ones((8, positions), jnp.float32)
    for i, counted in ((6, hits), (7, tally)):
        row = lax.dot_general(
            ones, counted[...], (((1,), (1,)), ((), ())), precision=lax.Precision.HIGHEST,
            preferred_element_type=jnp.float32)
        small[i : i + 1, 0 : counted.shape[0]] = row[0:1]
    tail.wait()
    for m in range(rows):
        @pl.when(leading)
        def _():
            hand(m)[0].wait_send()
            pltpu.make_async_copy(hat1.at[m], result.at[0, m], result_sem.at[m]).wait()

        @pl.when(trailing)
        def _():
            hand(m)[1].wait_send()
            pltpu.make_async_copy(buf.at[m], result.at[0, m], result_sem.at[m]).wait()


def run_blocks(args, big_rows, cid=0):
    boundary, in_weight, conv_weight = args[0], args[7], args[11]
    _, rows, positions, width = boundary.shape
    hidden = in_weight.shape[2]
    edge = KERNEL // 2 * DILATION_STEP
    assert edge % positions == 0 and positions % 16 == 0 and width % hidden == 0
    reach = edge // positions
    low, full = jnp.bfloat16, jnp.float32
    wide_rows = pltpu.VMEM((rows, positions, width), low)
    thin_rows = pltpu.VMEM((rows, positions, hidden), low)
    blocks = (2 * width // hidden + KERNEL) * hidden
    where = [pl.ANY, pltpu.SMEM] + [pltpu.VMEM] * 15
    for i in (7, 11, 15):
        where[i] = pl.ANY
    return pl.pallas_call(
        functools.partial(blocks_kernel, edge),
        out_shape=(
            jax.ShapeDtypeStruct(boundary.shape, low),
            jax.ShapeDtypeStruct((big_rows, hidden), low),
            jax.ShapeDtypeStruct((8, width), full),
        ),
        in_specs=[pl.BlockSpec(memory_space=space) for space in where],
        out_specs=[pl.BlockSpec(memory_space=space) for space in (pl.ANY, pl.ANY, pltpu.VMEM)],
        scratch_shapes=[
            pltpu.VMEM((2 * rows, positions, width), low),
            pltpu.VMEM((width, hidden), low),
            pltpu.VMEM((KERNEL, hidden, hidden), low),
            pltpu.VMEM((hidden, width), low),
            pltpu.VMEM((blocks, hidden), full),
            wide_rows, wide_rows, wide_rows,
            pltpu.VMEM((rows, KERNEL, positions, hidden), low),
            pltpu.VMEM((KERNEL, positions, hidden), low),
            thin_rows, thin_rows, thin_rows, thin_rows, thin_rows, thin_rows, thin_rows,
            pltpu.VMEM((4, edge, hidden), low),
            pltpu.VMEM((4, edge, hidden), low),
            pltpu.VMEM((positions + 32, hidden), full),
            pltpu.VMEM((rows, positions, 128), full),
            pltpu.VMEM((rows, 3, positions, 1), full),
            pltpu.VMEM((3, 8, width), full),
            pltpu.VMEM((6, 8, hidden), full),
            pltpu.VMEM((32, positions), full),
            pltpu.VMEM((32, positions), full),
            pltpu.VMEM((2, hidden, hidden), low),
            pltpu.SemaphoreType.DMA((rows,)),
            pltpu.SemaphoreType.DMA((3,)),
            pltpu.SemaphoreType.DMA((rows,)),
            pltpu.SemaphoreType.DMA((rows,)),
            pltpu.SemaphoreType.DMA((rows,)),
            pltpu.SemaphoreType.DMA((2 * rows, 2 * reach)),
            pltpu.SemaphoreType.DMA((2 * rows, 2 * reach)),
            pltpu.SemaphoreType.DMA((2,)),
        ],
        compiler_params=pltpu.CompilerParams(
            collective_id=cid, has_side_effects=True, vmem_limit_bytes=VMEM_BYTES),
    )(*args)


def ring_sizes(rows, nodes):
    units = -(-rows // (nodes * 16))
    long = -(-units // 2)
    return [[16 * ((way + i) // SUBS) for i in range(SUBS)] for way in (long, units - long)]


def ring_kernel(ny, nz, sizes, w_ref, s_ref, o_ref, t_ref, core_land, *rest):
    nodes = ny * nz
    flows = [(way, i) for way in range(2) for i in range(len(sizes[way])) if sizes[way][i]]
    lands = rest[:len(flows)]
    small_land, core_send, core_recv, ring_send, ring_recv, back_send, back_recv, small_send, small_recv = rest[len(flows):]
    s = lax.axis_index("section")
    q = lax.axis_index("seq")
    d = lax.axis_index("dp")
    core = q % 2
    ypos = q // 2
    odd = ypos % 2
    spot = ypos * nz + d + odd * (nz - 1 - 2 * d)

    def at_spot(place):
        yy = place // nz
        dd = place % nz
        dd = dd + (yy % 2) * (nz - 1 - 2 * dd)
        return (s, yy * 2 + core, dd)

    other_core = (s, q + 1 - 2 * core, d)
    other_x = (1 - s, q, d)
    ahead = at_spot((spot + 1) % nodes)
    behind = at_spot((spot + nodes - 1) % nodes)
    half = sum(sum(way) for way in sizes) * nodes
    turn = [1 - 2 * core, 2 * core - 1]

    peers = [other_core]
    reach = 1
    while reach < ny:
        peers.append((s, q + 2 * reach - 4 * reach * ((ypos // reach) % 2), d))
        reach *= 2
    reach = 1
    while reach < nz:
        peers.append((s, q, d + reach - 2 * reach * ((d // reach) % 2)))
        reach *= 2

    barrier = pltpu.get_barrier_semaphore()
    greet = [other_core, other_x, ahead, behind] + peers[1:]
    for peer in greet:
        pl.semaphore_signal(barrier, inc=1, device_id=peer, device_id_type=MESH)
    pl.semaphore_wait(barrier, len(greet))

    first = {}
    at = 0
    for way, i in flows:
        first[way, i] = at
        at += sizes[way][i] * nodes

    def rows_of(flow, side, shard):
        way, i = flow
        return pl.ds(pl.multiple_of(side * half + first[flow] + shard * sizes[way][i], 16), sizes[way][i])

    def shard_at(flow, step):
        return (spot + 2 * nodes - turn[flow[0]] * step) % nodes

    def next_of(flow):
        return at_spot((spot + nodes + turn[flow[0]]) % nodes)

    def core_copy(f, shard):
        flow = flows[f]
        return pltpu.make_async_remote_copy(
            src_ref=w_ref.at[rows_of(flow, 1 - core, shard)],
            dst_ref=core_land.at[rows_of(flow, 0, shard)],
            send_sem=core_send.at[f, shard], recv_sem=core_recv.at[f, shard],
            device_id=other_core, device_id_type=MESH)

    def ring_copy(f, step, shard):
        flow = flows[f]
        return pltpu.make_async_remote_copy(
            src_ref=w_ref.at[rows_of(flow, core, shard)],
            dst_ref=lands[f].at[step],
            send_sem=ring_send.at[f, step], recv_sem=ring_recv.at[f, step],
            device_id=next_of(flow), device_id_type=MESH)

    def back_copy(f, step, shard):
        block = o_ref.at[rows_of(flows[f], core, shard)]
        return pltpu.make_async_remote_copy(
            src_ref=block, dst_ref=block,
            send_sem=ring_send.at[f, nodes - 1 + step], recv_sem=ring_recv.at[f, nodes - 1 + step],
            device_id=next_of(flows[f]), device_id_type=MESH)

    def over_copy(f, shard):
        block = o_ref.at[rows_of(flows[f], core, shard)]
        return pltpu.make_async_remote_copy(
            src_ref=block, dst_ref=block,
            send_sem=back_send.at[f, shard], recv_sem=back_recv.at[f, shard],
            device_id=other_core, device_id_type=MESH)

    def add(f, shard, step, target):
        flow = flows[f]
        rows = sizes[flow[0]][flow[1]]
        here = rows_of(flow, core, shard).start
        there = rows_of(flow, 0, shard).start

        def body(i, carry):
            off = pl.multiple_of(i * 16, 16)
            total = w_ref[pl.ds(here + off, 16)].astype(jnp.float32)
            total = total + core_land[pl.ds(there + off, 16)].astype(jnp.float32)
            if step is not None:
                total = total + lands[f][step, pl.ds(off, 16)].astype(jnp.float32)
            target[pl.ds(here + off, 16)] = total.astype(target.dtype)
            return carry

        lax.fori_loop(0, rows // 16, body, 0)

    def to_other_core(step, carry):
        for f, flow in enumerate(flows):
            core_copy(f, shard_at(flow, step)).start()
        return carry

    lax.fori_loop(0, nodes, to_other_core, 0)

    def towards(step, carry):
        for f, flow in enumerate(flows):
            shard = shard_at(flow, step)
            core_copy(f, shard).wait_recv()
            if carry is None:
                add(f, shard, None, w_ref)
            else:
                ring_copy(f, step - 1, shard).wait_recv()
                add(f, shard, step - 1, w_ref)
            ring_copy(f, step, shard).start()
        return carry

    towards(0, None)
    count = s_ref.shape[0]

    def held(k):
        return s_ref if k == 0 else small_land.at[2 * k - 1]

    def small_copy(k):
        last = k == len(peers)
        return pltpu.make_async_remote_copy(
            src_ref=held(k), dst_ref=t_ref.at[pl.ds(count, count)] if last else small_land.at[2 * k],
            send_sem=small_send.at[k], recv_sem=small_recv.at[k],
            device_id=other_x if last else peers[k], device_id_type=MESH)

    def small_step(k):
        if 0 < k <= len(peers):
            small_copy(k - 1).wait_recv()
            small_land[2 * k - 1] = held(k - 1)[...] + small_land[2 * k - 2]
        if k <= len(peers):
            small_copy(k).start()
        if k == len(peers):
            t_ref[pl.ds(0, count)] = held(k)[...]

    small_step(0)
    for k in range(1, len(peers) + 1):
        if k < nodes - 1:
            towards(k, 0)
        small_step(k)
    lax.fori_loop(min(len(peers) + 1, nodes - 1), nodes - 1, towards, 0)
    for f, flow in enumerate(flows):
        shard = shard_at(flow, nodes - 1)
        core_copy(f, shard).wait_recv()
        ring_copy(f, nodes - 2, shard).wait_recv()
        add(f, shard, nodes - 2, o_ref)
        back_copy(f, 0, shard).start()
        over_copy(f, shard).start()

    def back(step, carry):
        for f, flow in enumerate(flows):
            shard = shard_at(flow, nodes - 1 + step)
            back_copy(f, step - 1, shard).wait_recv()
            back_copy(f, step, shard).start()
            over_copy(f, shard).start()
        return carry

    lax.fori_loop(1, nodes - 1, back, 0)
    for f, flow in enumerate(flows):
        shard = shard_at(flow, 2 * nodes - 2)
        back_copy(f, nodes - 2, shard).wait_recv()
        over_copy(f, shard).start()

    def settle(step, carry):
        for f, flow in enumerate(flows):
            core_copy(f, step).wait_send()
            over_copy(f, step).wait()
        return carry

    def settle_ring(step, carry):
        for f, flow in enumerate(flows):
            ring_copy(f, step, 0).wait_send()
            back_copy(f, step, 0).wait_send()
        return carry

    lax.fori_loop(0, nodes, settle, 0)
    lax.fori_loop(0, nodes - 1, settle_ring, 0)
    for k in range(len(peers) + 1):
        small_copy(k).wait_send()
    small_copy(len(peers)).wait_recv()


def sum_everywhere(big, small, ny, nz, cid=1):
    rows = big.shape[0]
    nodes = ny * nz
    sizes = ring_sizes(rows // 2, nodes)
    flows = [(w, i) for w in range(2) for i in range(len(sizes[w])) if sizes[w][i]]
    half = sum(map(sum, sizes)) * nodes
    assert rows == 2 * half, (rows, half, sizes)
    n = len(flows)
    return pl.pallas_call(
        functools.partial(ring_kernel, ny, nz, sizes),
        out_shape=(jax.ShapeDtypeStruct(big.shape, big.dtype),
                   jax.ShapeDtypeStruct((2 * small.shape[0], small.shape[1]), small.dtype)),
        in_specs=[pl.BlockSpec(memory_space=pltpu.VMEM)] * 2,
        out_specs=[pl.BlockSpec(memory_space=pltpu.VMEM)] * 2,
        scratch_shapes=[pltpu.VMEM((half, WIDE), big.dtype)]
        + [pltpu.VMEM((nodes - 1, sizes[w][i], WIDE), big.dtype) for w, i in flows]
        + [pltpu.VMEM((16,) + small.shape, small.dtype)]
        + [pltpu.SemaphoreType.DMA((n, nodes))] * 2
        + [pltpu.SemaphoreType.DMA((n, 2 * nodes - 2))] * 2
        + [pltpu.SemaphoreType.DMA((n, nodes))] * 2
        + [pltpu.SemaphoreType.DMA((8,))] * 2,
        compiler_params=pltpu.CompilerParams(collective_id=cid, has_side_effects=True, vmem_limit_bytes=56 << 20),
    )(big, small)


def shards(
    boundary, lengths, masked, residues, readout,
    first_gain, first_shift, in_weight, in_bias, second_gain, second_shift, conv_weight, conv_bias,
    third_gain, third_shift, out_weight, out_bias,
):
    ny, nz = lax.axis_size("seq") // 2, lax.axis_size("dp")
    width, hidden = in_weight.shape[1], in_weight.shape[2]
    count = (KERNEL + 2 * width // hidden) * hidden
    big_rows = 2 * ny * nz * sum(map(sum, ring_sizes(count // 2, ny * nz)))
    readout = jnp.pad(readout.T, ((0, 32 - VOCAB), (0, 0)))
    boundary_out, big, small = run_blocks(
        (
            boundary, lengths, masked, residues, readout,
            first_gain, first_shift, in_weight, in_bias, second_gain, second_shift, conv_weight, conv_bias,
            third_gain, third_shift, out_weight, out_bias,
        ),
        big_rows,
    )
    big, small = sum_everywhere(big, small, ny, nz)
    big = big.astype(jnp.float32)
    at = width + KERNEL * hidden
    grad_in_weight = big[None, :width]
    grad_conv_weight = big[width:at].reshape(conv_weight.shape)
    grad_out_weight = jnp.concatenate(
        [big[at + j : at + j + hidden] for j in range(0, width, hidden)], axis=1
    )[None]
    type_hits = small[6, :VOCAB] + small[14, :VOCAB]
    type_tally = small[7, :VOCAB] + small[15, :VOCAB]
    return (
        boundary_out,
        small[0:1],
        small[1:2],
        grad_in_weight,
        small[3:4, :hidden],
        small[3:4, hidden:],
        small[4:5, :hidden],
        grad_conv_weight,
        small[4:5, hidden:],
        small[5:6, :hidden],
        small[5:6, hidden:],
        grad_out_weight,
        small[2:3],
        type_hits / jnp.maximum(type_tally, 1.0),
        type_tally.astype(jnp.int32),
    )


def solution(mesh):
    in_specs = (
        P("section", "dp", "seq", None),
        P("dp", None),
        P("dp", "seq"),
        P("dp", "seq"),
        P(),
        P("section", None),
        P("section", None),
        P("section", None, None),
        P("section", None),
        P("section", None),
        P("section", None),
        P("section", None, None, None),
        P("section", None),
        P("section", None),
        P("section", None),
        P("section", None, None),
        P("section", None),
    )
    out_specs = (
        P("section", "dp", "seq", None),
        P("section", None),
        P("section", None),
        P("section", None, None),
        P("section", None),
        P("section", None),
        P("section", None),
        P("section", None, None, None),
        P("section", None),
        P("section", None),
        P("section", None),
        P("section", None, None),
        P("section", None),
        P(),
        P(),
    )
    return jax.shard_map(shards, mesh=mesh, in_specs=in_specs, out_specs=out_specs, check_vma=False)
```

```python
import functools

import jax
import jax.numpy as jnp
from jax import lax
from jax.experimental import pallas as pl
from jax.experimental.pallas import tpu as pltpu
from jax.sharding import PartitionSpec as P

KERNEL = 5
VOCAB = 30
DILATION_STEP = 128
ITEMS = 4
EPSILON = 1e-05
ROOT_HALF = 0.7071067811865476
HALF_LOG = -0.7213475204444817
ROOT_TAU = 0.3989422804014327

MESH = pl.DeviceIdType.MESH
LANES = 2
LOADS_AHEAD = 4
VMEM_BYTES = 64 << 20


def far_rows(left, own, right, offset):
    edge, positions = left.shape[0], own.shape[0]
    first, last = offset + edge, offset + edge + positions
    pieces, at = [], 0
    for block in (left, own, right):
        lo, hi = max(first, at), min(last, at + block.shape[0])
        if lo < hi:
            pieces.append(block[lo - at : hi - at])
        at += block.shape[0]
    return pieces[0] if len(pieces) == 1 else jnp.concatenate(pieces, axis=0)


def act_forward(values, gain, shift, real):
    scale = 1.0 / values.shape[1]
    centred = values - jnp.sum(values, axis=1, keepdims=True) * scale
    spread = jnp.sum(centred * centred, axis=1, keepdims=True) * scale
    inverse = lax.rsqrt(spread + EPSILON)
    hat = centred * inverse
    moved = hat * gain + shift
    below = (0.5 + 0.5 * lax.erf(moved * ROOT_HALF)) * real
    density = jnp.exp2(moved * moved * HALF_LOG) * (ROOT_TAU * real)
    return moved * below, hat, below + moved * density, inverse


def fold(values):
    rows, columns = values.shape
    return jnp.sum(values.reshape(rows // 8, 8, columns), axis=0)


def act_backward(grad, hat, slope, inverse, gain, gain_sum, shift_sum):
    scale = 1.0 / grad.shape[1]
    hat = hat.astype(jnp.float32)
    moved = grad * slope.astype(jnp.float32)
    turned = moved * hat
    shift_sum[...] += fold(moved)
    gain_sum[...] += fold(turned)
    mean = jnp.sum(moved * gain, axis=1, keepdims=True) * scale
    tilt = jnp.sum(turned * gain, axis=1, keepdims=True) * scale
    return inverse * (moved * gain - mean - hat * tilt)


def dot_nn(a, b):
    return jnp.dot(a, b, preferred_element_type=jnp.float32)


def dot_nt(a, b):
    return lax.dot_general(a, b, (((1,), (1,)), ((), ())), preferred_element_type=jnp.float32)


def dot_tn(a, b):
    return lax.dot_general(a, b, (((0,), (0,)), ((), ())), preferred_element_type=jnp.float32)


def blocks_kernel(
    edge, plan,
    boundary, lengths, masked, residues, readout,
    first_gain, first_shift, in_weight, in_bias, second_gain, second_shift, conv_weight, conv_bias,
    third_gain, third_shift, out_weight, out_bias,
    result, big, small_out,
    buf, w_in, w_conv, w_out, total, hat1, slope1, act1, taps, back_taps,
    hat2, slope2, hat3, slope3, act3, rim_left, rim_right, near, masks,
    sums_wide, sums, hits, tally, core_land, small, small_land,
    load_sem, weight_sem, result_sem, hand_send, hand_recv, rim_send, rim_recv, small_send, small_recv, *ring_refs,
):
    grad1, grad2 = hat2, hat3
    section = lax.axis_index("section")
    seq = lax.axis_index("seq")
    dp = lax.axis_index("dp")
    n_seq = lax.axis_size("seq")
    rows, positions = buf.shape[0] // 2, buf.shape[1]
    hidden = w_in.shape[1]
    leading = section == 0
    trailing = section == 1
    row_len = n_seq * positions
    first_position = seq * positions
    reach = edge // positions
    dilation = jnp.where(leading, 1, DILATION_STEP)

    def load(m):
        return pltpu.make_async_copy(boundary.at[0, m], buf.at[section * rows + m], load_sem.at[m])

    weight_loads = [
        pltpu.make_async_copy(source.at[0], target, weight_sem.at[i])
        for i, (source, target) in enumerate(((in_weight, w_in), (conv_weight, w_conv), (out_weight, w_out)))
    ]
    load(0).start()
    weight_loads[0].start()

    def partner():
        return (1 - section, seq, dp)

    rings, at = [], 0
    for sizes, base, land in plan:
        ring = Ring(sizes, base, land, section, seq, dp, n_seq // 2, lax.axis_size("dp"))
        ring.bind(total, taps, core_land, big, ring_refs[at : at + ring.refs])
        at += ring.refs
        rings.append(ring)
    barrier = pltpu.get_barrier_semaphore()
    greet = [partner()] + rings[0].neighbours()
    for peer in greet:
        pl.semaphore_signal(barrier, inc=1, device_id=peer, device_id_type=MESH)
    greeted = len(greet)
    for j in range(1, reach + 1):
        for side in (-j, j):
            on = (seq + side >= 0) & (seq + side < n_seq)
            greeted = greeted + on.astype(jnp.int32)

            @pl.when(on)
            def _():
                pl.semaphore_signal(barrier, inc=1, device_id=(section, seq + side, dp), device_id_type=MESH)

    @pl.when(seq < reach)
    def _():
        rim_left[...] = jnp.zeros_like(rim_left)

    @pl.when(seq >= n_seq - reach)
    def _():
        rim_right[...] = jnp.zeros_like(rim_right)

    last = rows - 1
    half, quarter = positions // 2, positions // 4
    parts = ((0, half), (half, half))
    thirds = ((quarter, half), (0, quarter), (half + quarter, quarter))
    whole = ((0, positions),)

    def make_mask(m):
        lane = lax.broadcasted_iota(jnp.int32, (positions, 128), 1)
        place = lax.broadcasted_iota(jnp.int32, (positions, 128), 0) + first_position
        other = place + (lane - KERNEL // 2) * dilation
        end = 0
        here = jnp.zeros((positions, 128), jnp.int32)
        there = jnp.zeros((positions, 128), jnp.int32)
        for j in range(ITEMS):
            end = end + lengths[m, j]
            here = here + (place >= end).astype(jnp.int32)
            there = there + (other >= end).astype(jnp.int32)
        counts = (here == there) & (here < ITEMS) & (other >= 0) & (other < row_len)
        masks[m] = counts.astype(jnp.float32)

    def hand(source, m, part):
        first, count = thirds[part]
        block = pl.ds(first, count)
        target = buf.at[m, block] if source is buf else buf.at[rows + m, block]
        return pltpu.make_async_remote_copy(
            src_ref=source.at[m, block], dst_ref=target,
            send_sem=hand_send.at[m, part], recv_sem=hand_recv.at[m, part],
            device_id=partner(), device_id_type=MESH)

    def tap_rows(m, k, first=0, count=None):
        start = (m * KERNEL + k) * positions + first
        return pl.ds(pl.multiple_of(start, 16), positions if count is None else count)

    def near_copies(backward, m):
        slot = 2 * backward + m % 2
        turn = backward * rows + m

        def edge_rows(first):
            return grad2.at[m, pl.ds(first, 16)] if backward else taps.at[tap_rows(m, KERNEL // 2, first, 16)]

        def copy(source, target, index, to):
            return pltpu.make_async_remote_copy(
                src_ref=source, dst_ref=target, send_sem=rim_send.at[turn, index], recv_sem=rim_recv.at[turn, index],
                device_id=(section, to, dp), device_id_type=MESH)

        return [
            (seq + 1 < n_seq, seq >= 1,
             copy(edge_rows(positions - 16), rim_left.at[slot, pl.ds(edge - 16, 16)], 0, seq + 1)),
            (seq >= 1, seq + 1 < n_seq,
             copy(edge_rows(0), rim_right.at[slot, pl.ds(0, 16)], 1, seq - 1)),
        ]

    def far_copies(backward, m, part, pieces):
        first, count = pieces[part]
        slot = 2 * backward + m % 2
        turn = backward * rows + m
        own = grad2.at[m, pl.ds(first, count)] if backward else taps.at[tap_rows(m, KERNEL // 2, first, count)]

        def copy(target, index, to):
            return pltpu.make_async_remote_copy(
                src_ref=own, dst_ref=target,
                send_sem=rim_send.at[turn, 3 * index + part], recv_sem=rim_recv.at[turn, 3 * index + part],
                device_id=(section, to, dp), device_id_type=MESH)

        copies = []
        for j in range(1, reach + 1):
            copies.append((
                seq + j < n_seq, seq >= j,
                copy(rim_left.at[slot, pl.ds(edge - j * positions + first, count)], 2 * j - 2, seq + j)))
            copies.append((
                seq >= j, seq + j < n_seq,
                copy(rim_right.at[slot, pl.ds((j - 1) * positions + first, count)], 2 * j - 1, seq - j)))
        return copies

    def begin(copies):
        for sends, _, copy in copies:
            pl.when(sends)(copy.start)

    def end(copies):
        for sends, receives, copy in copies:
            pl.when(receives)(copy.wait_recv)
            pl.when(sends)(copy.wait_send)

    def gather_near(backward, m, own, store, rims):
        slot = 2 * backward + m % 2
        if not rims:
            near[16 : 16 + positions] = own.astype(jnp.float32)
            pieces = thirds[:1]
        else:
            near[0:16] = rim_left[slot, edge - 16 : edge].astype(jnp.float32)
            near[16 + positions : 32 + positions] = rim_right[slot, 0:16].astype(jnp.float32)
            pieces = thirds[1:]
        for first, count in pieces:
            mask = masks[m, first : first + count]
            for k in range(KERNEL):
                if k != KERNEL // 2:
                    at = 16 + first + k - KERNEL // 2
                    store(k, first, jnp.where(mask[:, k : k + 1] > 0, near[at : at + count], 0.0))

    def gather_far(backward, m, own, store):
        slot = 2 * backward + m % 2
        mask = masks[m]
        for k in range(KERNEL):
            if k != KERNEL // 2:
                piece = far_rows(rim_left[slot], own, rim_right[slot], (k - KERNEL // 2) * DILATION_STEP)
                store(k, 0, jnp.where(mask[:, k : k + 1] > 0, piece.astype(jnp.float32), 0.0))

    def store_tap(m):
        def store(k, first, value):
            taps[tap_rows(m, k, first, value.shape[0])] = value.astype(jnp.bfloat16)

        return store

    def store_back(k, first, value):
        back_taps[k - (k > KERNEL // 2), first : first + value.shape[0]] = value.astype(jnp.bfloat16)

    def front(m, piece):
        block = slice(piece[0], piece[0] + piece[1])
        real = masks[m, block, KERNEL // 2 : KERNEL // 2 + 1]
        act, hat, slope, inverse = act_forward(
            buf[m, block].astype(jnp.float32), first_gain[...], first_shift[...], real)
        act1[m, block] = act.astype(jnp.bfloat16)
        hat1[m, block] = hat.astype(jnp.bfloat16)
        slope1[m, block] = slope.astype(jnp.bfloat16)
        masks[m, block, 8:9] = inverse
        pre = dot_nn(act1[m, block], w_in[...]) + in_bias[...]
        act, hat, slope, inverse = act_forward(pre, second_gain[...], second_shift[...], real)
        taps[tap_rows(m, KERNEL // 2, *piece)] = act.astype(jnp.bfloat16)
        hat2[m, block] = hat.astype(jnp.bfloat16)
        slope2[m, block] = slope.astype(jnp.bfloat16)
        masks[m, block, 9:10] = inverse

    def middle_tap(m, piece):
        return conv_bias[...] + dot_nn(taps[tap_rows(m, KERNEL // 2, *piece)], w_conv[KERNEL // 2])

    def rear(m, piece, pre):
        block = slice(piece[0], piece[0] + piece[1])
        for k in range(KERNEL):
            if k != KERNEL // 2:
                pre = pre + dot_nn(taps[tap_rows(m, k, *piece)], w_conv[k])
        real = masks[m, block, KERNEL // 2 : KERNEL // 2 + 1]
        act, hat, slope, inverse = act_forward(pre, third_gain[...], third_shift[...], real)
        act3[m, block] = act.astype(jnp.bfloat16)
        hat3[m, block] = hat.astype(jnp.bfloat16)
        slope3[m, block] = slope.astype(jnp.bfloat16)
        masks[m, block, 10:11] = inverse
        out = buf[m, block].astype(jnp.float32) + (dot_nn(act3[m, block], w_out[...]) + out_bias[...])
        buf[m, block] = out.astype(jnp.bfloat16)

    def count_types(m):
        logits = dot_nt(readout[...], buf[m])
        kind = lax.broadcasted_iota(jnp.int32, logits.shape, 0)
        odds = jnp.exp(logits - jnp.max(logits, axis=0, keepdims=True))
        odds = odds / jnp.sum(odds, axis=0, keepdims=True)
        stop = lengths[m, 0]
        for j in range(1, ITEMS):
            stop = stop + lengths[m, j]
        spot = lax.broadcasted_iota(jnp.int32, (1, positions), 1) + first_position
        chosen = jnp.where(spot < stop, masked[pl.ds(m, 1)].astype(jnp.float32), 0.0)
        chosen = jnp.where(kind == residues[pl.ds(m, 1)], chosen, 0.0)
        hits[...] += chosen * odds
        tally[...] += chosen

    def back_front(m, piece):
        block = slice(piece[0], piece[0] + piece[1])
        sums_wide[2] += fold(buf[rows + m, block].astype(jnp.float32))
        grad = dot_nt(buf[rows + m, block], w_out[...])
        low = act_backward(
            grad, hat3[m, block], slope3[m, block], masks[m, block, 10:11], third_gain[...], sums.at[4], sums.at[5]
        ).astype(jnp.bfloat16)
        grad2[m, block] = low
        sums[3] += fold(low.astype(jnp.float32))

    def back_middle_tap(m):
        return dot_nt(grad2[m], w_conv[KERNEL // 2])

    def back_rear(m, grad, between=None):
        for k in range(KERNEL):
            if k != KERNEL // 2:
                grad = grad + dot_nt(back_taps[k - (k > KERNEL // 2)], w_conv[KERNEL - 1 - k])
        if between is not None:
            between()
        low = act_backward(
            grad, hat2[m], slope2[m], masks[m, :, 9:10], second_gain[...], sums.at[1], sums.at[2]
        ).astype(jnp.bfloat16)
        grad1[m] = low
        sums[0] += fold(low.astype(jnp.float32))

    def back_last(m, piece):
        block = slice(piece[0], piece[0] + piece[1])
        grad = dot_nt(grad1[m, block], w_in[...])
        grad = act_backward(
            grad, hat1[m, block], slope1[m, block], masks[m, block, 8:9], first_gain[...],
            sums_wide.at[0], sums_wide.at[1])
        hat1[m, block] = (buf[rows + m, block].astype(jnp.float32) + grad).astype(jnp.bfloat16)

    def give(source, m):
        return pltpu.make_async_copy(source.at[m], result.at[0, m], result_sem.at[m])

    wide = buf.shape[2] // hidden

    def add_block(start, value):
        total[pl.ds(start, hidden)] += value

    def weights_out(m):
        for j in range(wide):
            add_block((KERNEL + j) * hidden, dot_tn(act3[m], buf[rows + m, :, j * hidden : (j + 1) * hidden]))

    def weights_conv(m):
        for k in range(KERNEL):
            add_block(k * hidden, dot_tn(taps[tap_rows(m, k)], grad2[m]))

    def weights_in(m):
        for j in range(wide):
            add_block(rings[1].base + j * hidden, dot_tn(act1[m, :, j * hidden : (j + 1) * hidden], grad1[m]))

    def first_lane():
        rings[0].exchange(2)
        rings[0].towards(0, 0, True)

    def step(i, carry):
        m_back = i - rows
        front_due = i < rows
        back_due = i >= rows
        final = i == 2 * rows - 1

        @pl.when(front_due)
        def _():
            make_mask(i)

        @pl.when(i == 0)
        def _():
            weight_loads[0].wait()
            for copy in weight_loads[1:]:
                copy.start()

        @pl.when(leading & front_due)
        def _():
            load(i).wait()

        @pl.when(i == 0)
        def _():
            for m in range(1, rows):
                load(m).start()

        @pl.when(leading & front_due)
        def _():
            front(i, whole[0])

        @pl.when(i == 0)
        def _():
            pl.semaphore_wait(barrier, greeted)

        @pl.when(leading & front_due)
        def _():
            begin(near_copies(0, i))

        @pl.when(trailing & (i < last))
        def _():
            for part in range(3):
                hand(buf, i, part).wait_recv()
            front(i, whole[0])
            begin(far_copies(0, i, 0, whole))

        @pl.when(trailing & (i == last))
        def _():
            for part in range(3):
                hand(buf, last, part).wait_recv()
                front(last, thirds[part])
                begin(far_copies(0, last, part, thirds))

        @pl.when(i == 0)
        def _():
            weight_loads[1].wait()
            weight_loads[2].wait()

        def finish_row(m, pieces):
            grad = back_middle_tap(m)
            for part in range(len(pieces)):
                end(far_copies(1, m, part, pieces))
            gather_far(1, m, grad2[m], store_back)
            back_rear(m, grad)
            for part in range(3):
                back_last(m, thirds[part])
                hand(hat1, m, part).start()

        @pl.when(trailing & (i >= 1) & (i <= last))
        def _():
            finish_row(i - 1, whole)

        @pl.when(trailing & (i == rows))
        def _():
            finish_row(last, parts)

        @pl.when(leading & front_due)
        def _():
            gather_near(0, i, taps[tap_rows(i, KERNEL // 2)], store_tap(i), False)
            rear(i, thirds[0], middle_tap(i, thirds[0]))
            hand(buf, i, 0).start()
            end(near_copies(0, i))
            gather_near(0, i, taps[tap_rows(i, KERNEL // 2)], store_tap(i), True)
            for part in (1, 2):
                rear(i, thirds[part], middle_tap(i, thirds[part]))
                hand(buf, i, part).start()

        @pl.when((leading & (i == 2)) | (trailing & (i == 0)))
        def _():
            total[...] = jnp.zeros_like(total)
            sums_wide[...] = jnp.zeros_like(sums_wide)
            sums[...] = jnp.zeros_like(sums)
            hits[...] = jnp.zeros_like(hits)
            tally[...] = jnp.zeros_like(tally)

        def turn_row(m, waits):
            pre = middle_tap(m, whole[0])
            for copies in waits:
                end(copies)
            gather_far(0, m, taps[tap_rows(m, KERNEL // 2)], store_tap(m))
            rear(m, whole[0], pre)
            give(buf, m).start()

        @pl.when(trailing & (i < last))
        def _():
            turn_row(i, [far_copies(0, i, 0, whole)])
            load(i).wait()
            back_front(i, whole[0])
            begin(far_copies(1, i, 0, whole))
            count_types(i)

        @pl.when(trailing & (i == last))
        def _():
            turn_row(last, [far_copies(0, last, part, thirds) for part in range(3)])
            load(last).wait()
            for part in range(2):
                back_front(last, parts[part])
                begin(far_copies(1, last, part, parts))
            count_types(last)

        @pl.when(leading & back_due)
        def _():
            for part in range(3):
                hand(hat1, m_back, part).wait_recv()
                back_front(m_back, thirds[part])
            begin(near_copies(1, m_back))

        @pl.when(back_due)
        def _():
            weights_out(m_back)
            weights_conv(m_back)

        @pl.when(final)
        def _():
            rings[0].exchange(0)
            rings[0].exchange(1)

        @pl.when(leading & back_due)
        def _():
            grad = back_middle_tap(m_back)
            gather_near(1, m_back, grad2[m_back], store_back, False)
            end(near_copies(1, m_back))
            gather_near(1, m_back, grad2[m_back], store_back, True)
            back_rear(m_back, grad, lambda: pl.when(final)(first_lane))

        @pl.when(trailing & final)
        def _():
            first_lane()

        @pl.when(leading & back_due)
        def _():
            back_last(m_back, whole[0])
            give(hat1, m_back).start()

        @pl.when(back_due)
        def _():
            weights_in(m_back)

        @pl.when(final)
        def _():
            for lane in range(1, rings[0].lanes):
                rings[0].towards(0, lane, True)
            rings[1].exchange(0)
            rings[1].exchange(1)

        return carry

    lax.fori_loop(0, 2 * rows, step, 0)

    for i in range(3):
        small[i : i + 1, :] = jnp.sum(sums_wide[i], axis=0, keepdims=True)
    for i in range(6):
        small[3 + i // 2 : 4 + i // 2, (i % 2) * hidden : (i % 2 + 1) * hidden] = jnp.sum(sums[i], axis=0, keepdims=True)
    small[6:8, :] = jnp.zeros((2, small.shape[1]), jnp.float32)
    ones = jnp.ones((8, positions), jnp.float32)
    for i, counted in ((6, hits), (7, tally)):
        row = lax.dot_general(
            ones, counted[...], (((1,), (1,)), ((), ())), precision=lax.Precision.HIGHEST,
            preferred_element_type=jnp.float32)
        small[i : i + 1, 0 : counted.shape[0]] = row[0:1]
    run_rings(rings, SmallSum(rings[0], small, small_land, small_out, small_send, small_recv, partner()))
    for m in range(rows):
        @pl.when(leading)
        def _():
            for part in range(3):
                hand(buf, m, part).wait_send()
            give(hat1, m).wait()

        @pl.when(trailing)
        def _():
            for part in range(3):
                hand(hat1, m, part).wait_send()
            give(buf, m).wait()


def ring_plan(width, hidden, nodes):
    plan, base, land = [], 0, 0
    for rows, subs in (((KERNEL + width // hidden) * hidden, LANES), (width, 1)):
        sizes = ring_sizes(rows // 2, nodes, subs)
        plan.append((sizes, base, land))
        land += nodes * sum(map(sum, sizes))
        base = 2 * land
    return plan, land


def run_blocks(args, ny, nz, cid=0):
    nodes = ny * nz
    doublings = 1 + (ny - 1).bit_length() + (nz - 1).bit_length()
    boundary, in_weight, conv_weight = args[0], args[7], args[11]
    _, rows, positions, width = boundary.shape
    hidden = in_weight.shape[2]
    edge = KERNEL // 2 * DILATION_STEP
    assert edge % positions == 0 and positions % 32 == 0 and width % hidden == 0
    reach = edge // positions
    low, full = jnp.bfloat16, jnp.float32
    wide_rows = pltpu.VMEM((rows, positions, width), low)
    thin_rows = pltpu.VMEM((rows, positions, hidden), low)
    plan, half = ring_plan(width, hidden, nodes)
    where = [pltpu.HBM, pltpu.SMEM] + [pltpu.VMEM] * 15
    for i in (7, 11, 15):
        where[i] = pltpu.HBM
    return pl.pallas_call(
        functools.partial(blocks_kernel, edge, plan),
        out_shape=(
            jax.ShapeDtypeStruct(boundary.shape, low),
            jax.ShapeDtypeStruct((2 * half, hidden), low),
            jax.ShapeDtypeStruct((16, width), full),
        ),
        in_specs=[pl.BlockSpec(memory_space=space) for space in where],
        out_specs=[pl.BlockSpec(memory_space=space) for space in (pltpu.HBM, pltpu.HBM, pltpu.VMEM)],
        scratch_shapes=[
            pltpu.VMEM((2 * rows, positions, width), low),
            pltpu.VMEM((width, hidden), low),
            pltpu.VMEM((KERNEL, hidden, hidden), low),
            pltpu.VMEM((hidden, width), low),
            pltpu.VMEM((2 * half, hidden), full),
            wide_rows, wide_rows, wide_rows,
            pltpu.VMEM((max(rows * KERNEL * positions, half), hidden), low),
            pltpu.VMEM((KERNEL - 1, positions, hidden), low),
            thin_rows, thin_rows, thin_rows, thin_rows, thin_rows,
            pltpu.VMEM((4, edge, hidden), low),
            pltpu.VMEM((4, edge, hidden), low),
            pltpu.VMEM((positions + 32, hidden), full),
            pltpu.VMEM((rows, positions, 128), full),
            pltpu.VMEM((3, 8, width), full),
            pltpu.VMEM((6, 8, hidden), full),
            pltpu.VMEM((VOCAB, positions), full),
            pltpu.VMEM((VOCAB, positions), full),
            pltpu.VMEM((half, hidden), low),
            pltpu.VMEM((8, width), full),
            pltpu.VMEM((2 * doublings, 8, width), full),
            pltpu.SemaphoreType.DMA((rows,)),
            pltpu.SemaphoreType.DMA((3,)),
            pltpu.SemaphoreType.DMA((rows,)),
            pltpu.SemaphoreType.DMA((rows, 3)),
            pltpu.SemaphoreType.DMA((rows, 3)),
            pltpu.SemaphoreType.DMA((2 * rows, 6 * reach)),
            pltpu.SemaphoreType.DMA((2 * rows, 6 * reach)),
            pltpu.SemaphoreType.DMA((doublings + 1,)),
            pltpu.SemaphoreType.DMA((doublings + 1,)),
        ]
        + [scratch for sizes, _, _ in plan for scratch in ring_scratch(sizes, nodes, hidden)],
        compiler_params=pltpu.CompilerParams(
            collective_id=cid, has_side_effects=True, vmem_limit_bytes=VMEM_BYTES),
    )(*args)


def ring_sizes(rows, nodes, subs):
    units = -(-rows // (nodes * 16))
    long = -(-units // 2)
    return [[16 * ((way + i) // subs) for i in range(subs)] for way in (long, units - long)]


def ring_flows(sizes):
    return [(way, i) for i in range(len(sizes[0])) for way in range(2) if sizes[way][i]]


def ring_scratch(sizes, nodes, columns):
    flows = ring_flows(sizes)
    n = len(flows)
    counts = [(n, nodes)] * 2 + [(n, 2 * nodes - 2)] * 2 + [(n, nodes)] * 2 + [(n,)]
    return [pltpu.SemaphoreType.DMA(count) for count in counts] + [
        pltpu.VMEM((nodes - 1, sizes[way][i], columns), jnp.bfloat16) for way, i in flows]


class Ring:
    def __init__(self, sizes, base, land, section, seq, dp, ny, nz):
        self.sizes, self.base, self.land, self.nodes = sizes, base, land, ny * nz
        self.flows = ring_flows(sizes)
        self.refs = 7 + len(self.flows)
        self.lanes = len(sizes[0])
        self.section, self.nz = section, nz
        self.core, ypos = seq % 2, seq // 2
        self.spot = ypos * nz + dp + (ypos % 2) * (nz - 1 - 2 * dp)
        self.other_core = (section, seq + 1 - 2 * self.core, dp)
        self.turn = [1 - 2 * self.core, 2 * self.core - 1]
        self.next = [self.at_spot(self.wrap(self.spot + self.nodes + turn)) for turn in self.turn]
        self.half = sum(map(sum, sizes)) * self.nodes
        self.first, at = {}, 0
        for way, i in self.flows:
            self.first[way, i] = at
            at += sizes[way][i] * self.nodes
        self.peers = [self.other_core]
        reach = 1
        while reach < ny:
            self.peers.append((section, seq + 2 * reach - 4 * reach * ((ypos // reach) % 2), dp))
            reach *= 2
        reach = 1
        while reach < nz:
            self.peers.append((section, seq, dp + reach - 2 * reach * ((dp // reach) % 2)))
            reach *= 2

    def wrap(self, place):
        if self.nodes & (self.nodes - 1) == 0:
            return place & (self.nodes - 1)
        return lax.rem(place, self.nodes)

    def at_spot(self, place):
        y = place // self.nz
        z = place % self.nz
        return (self.section, y * 2 + self.core, z + (y % 2) * (self.nz - 1 - 2 * z))

    def neighbours(self):
        around = self.next
        return self.peers + around

    def bind(self, total, stage, core_land, big, refs):
        self.total, self.stage, self.core_land, self.big = total, stage, core_land, big
        self.core_sems, self.ring_sems, self.over_sems = refs[0:2], refs[2:4], refs[4:6]
        self.keep_sem, self.lands = refs[6], refs[7:]

    def count(self, f):
        way, i = self.flows[f]
        return self.sizes[way][i]

    def rows(self, f, side, shard):
        start = self.base + side * self.half + self.first[self.flows[f]] + shard * self.count(f)
        return pl.ds(pl.multiple_of(start, 16), self.count(f))

    def land_rows(self, f, shard):
        start = self.land + self.first[self.flows[f]] + shard * self.count(f)
        return pl.ds(pl.multiple_of(start, 16), self.count(f))

    def shard(self, f, step):
        return self.wrap(self.spot + 2 * self.nodes - self.turn[self.flows[f][0]] * step)

    def ahead(self, f):
        return self.next[self.flows[f][0]]

    def remote(self, source, target, sems, index, peer):
        return pltpu.make_async_remote_copy(
            src_ref=source, dst_ref=target, send_sem=sems[0].at[index], recv_sem=sems[1].at[index],
            device_id=peer, device_id_type=MESH)

    def core_copy(self, f, shard):
        rows = self.land_rows(f, shard)
        return self.remote(self.stage.at[rows], self.core_land.at[rows], self.core_sems, (f, shard), self.other_core)

    def ring_copy(self, f, step, shard):
        return self.remote(
            self.core_land.at[self.land_rows(f, shard)], self.lands[f].at[step], self.ring_sems, (f, step), self.ahead(f))

    def back_copy(self, f, step, shard):
        block = self.big.at[self.rows(f, self.core, shard)]
        return self.remote(
            self.core_land.at[self.land_rows(f, shard)] if step is None else block, block,
            self.ring_sems, (f, self.nodes - 1 + (0 if step is None else step)), self.ahead(f))

    def over_copy(self, f, shard, own=False):
        block = self.big.at[self.rows(f, self.core, shard)]
        return self.remote(
            self.core_land.at[self.land_rows(f, shard)] if own else block, block,
            self.over_sems, (f, shard), self.other_core)

    def keep_copy(self, f, shard):
        return pltpu.make_async_copy(
            self.core_land.at[self.land_rows(f, shard)], self.big.at[self.rows(f, self.core, shard)], self.keep_sem.at[f])

    def add(self, f, shard, step):
        rows = self.land_rows(f, shard)
        value = self.total[self.rows(f, self.core, shard)] + self.core_land[rows].astype(jnp.float32)
        if step is not None:
            value = value + self.lands[f][step].astype(jnp.float32)
        self.core_land[rows] = value.astype(jnp.bfloat16)

    def exchange(self, step):
        for f in range(len(self.flows)):
            shard = self.shard(f, -step)
            self.stage[self.land_rows(f, shard)] = self.total[self.rows(f, 1 - self.core, shard)].astype(jnp.bfloat16)
            self.core_copy(f, shard).start()

    def of(self, lane):
        return [f for f in range(len(self.flows)) if lane is None or self.flows[f][1] == lane]

    def towards(self, step, lane=None, first=False):
        for f in self.of(lane):
            shard = self.shard(f, step)
            self.core_copy(f, shard).wait_recv()
            if first:
                self.add(f, shard, None)
            else:
                self.ring_copy(f, step - 1, shard).wait_recv()
                self.add(f, shard, step - 1)
            self.ring_copy(f, step, shard).start()

    def back(self, step, lane=None):
        for f in self.of(lane):
            shard = self.shard(f, self.nodes - 1 + step)
            self.back_copy(f, step - 1, shard).wait_recv()
            self.back_copy(f, step, shard).start()
            self.over_copy(f, shard).start()

    def own(self, lane=None):
        for f in self.of(lane):
            shard = self.shard(f, self.nodes - 1)
            self.core_copy(f, shard).wait_recv()
            self.ring_copy(f, self.nodes - 2, shard).wait_recv()
            self.add(f, shard, self.nodes - 2)
            self.back_copy(f, None, shard).start()
            self.over_copy(f, shard, True).start()
            self.keep_copy(f, shard).start()

    def arrive(self, lane=None):
        for f in self.of(lane):
            shard = self.shard(f, 2 * self.nodes - 2)
            self.back_copy(f, self.nodes - 2, shard).wait_recv()
            self.over_copy(f, shard).start()

    def settle(self):
        def crossed(step, carry):
            for f in range(len(self.flows)):
                self.core_copy(f, step).wait_send()
                self.over_copy(f, step).wait()
            return carry

        def rounded(step, carry):
            for f in range(len(self.flows)):
                self.ring_copy(f, step, 0).wait_send()
                self.back_copy(f, step, 0).wait_send()
            return carry

        lax.fori_loop(0, self.nodes, crossed, 0)
        lax.fori_loop(0, self.nodes - 1, rounded, 0)
        for f in range(len(self.flows)):
            self.keep_copy(f, 0).wait()


def run_rings(rings, small_sum):
    ahead, behind = rings
    nodes, lanes = ahead.nodes, ahead.lanes

    def each(method, *step):
        getattr(ahead, method)(*step, 0)
        getattr(behind, method)(*step)
        for lane in range(1, lanes):
            getattr(ahead, method)(*step, lane)

    ahead.exchange(3)
    for lane in range(lanes):
        ahead.towards(1, lane)
    small_sum.step(0)
    for step in (2, 3):
        ahead.exchange(step + 2)
        behind.exchange(2 * step - 2)
        behind.exchange(2 * step - 1)
        ahead.towards(step, 0)
        behind.towards(2 * step - 4, first=step == 2)
        for lane in range(1, lanes):
            ahead.towards(step, lane)
        behind.towards(2 * step - 3)

    def towards(step, carry):
        ahead.exchange(step + 2)
        behind.exchange(step + 2)
        each("towards", step)
        return carry

    lax.fori_loop(4, nodes - 2, towards, 0)
    each("towards", nodes - 2)
    each("own")
    small_sum.step(1)
    at = 1
    for k in range(2, small_sum.steps):
        if at < nodes - 1:
            each("back", at)
            at += 1
        small_sum.step(k)

    def back(step, carry):
        each("back", step)
        return carry

    lax.fori_loop(at, nodes - 1, back, 0)
    each("arrive")
    ahead.settle()
    behind.settle()
    small_sum.settle()


class SmallSum:
    def __init__(self, ring, small, land, out, send_sem, recv_sem, other_section):
        self.peers, self.small, self.land, self.out = ring.peers + [other_section], small, land, out
        self.sems = (send_sem, recv_sem)
        self.remote = ring.remote
        self.steps = len(self.peers) + 1

    def held(self, k):
        return self.small if k == 0 else self.land.at[2 * k - 1]

    def copy(self, k):
        count = self.small.shape[0]
        target = self.out.at[pl.ds(count, count)] if k == len(self.peers) - 1 else self.land.at[2 * k]
        return self.remote(self.held(k), target, self.sems, k, self.peers[k])

    def step(self, k):
        last = len(self.peers) - 1
        if 0 < k:
            self.copy(k - 1).wait_recv()
        if 0 < k <= last:
            self.land[2 * k - 1] = self.held(k - 1)[...] + self.land[2 * k - 2]
        if k <= last:
            self.copy(k).start()
        if k == last:
            self.out[pl.ds(0, self.small.shape[0])] = self.held(k)[...]

    def settle(self):
        for k in range(len(self.peers)):
            self.copy(k).wait_send()


def finish_kernel(
    base, given, big, small, result, grad_in, grad_conv, grad_out, first_gain, first_shift, in_bias, second_gain,
    second_shift, conv_bias, third_gain, third_shift, out_bias, scores, counts,
    passed, held, wide, pass_sem, load_sem, store_sem,
):
    hidden = held.shape[2]
    blocks = held.shape[0]
    ends = grad_in.shape[1] // hidden
    first = pltpu.make_async_copy(given, passed, pass_sem.at[0])
    second = pltpu.make_async_copy(passed, result, pass_sem.at[1])

    def load(b):
        start = b * hidden if b < blocks - ends else base + (b - blocks + ends) * hidden
        return pltpu.make_async_copy(big.at[pl.ds(start, hidden)], held.at[b], load_sem.at[b])

    def store(b):
        if b < KERNEL:
            target = grad_conv.at[0, b]
        elif b < blocks - ends:
            target = grad_out.at[0, :, pl.ds((b - KERNEL) * hidden, hidden)]
        else:
            target = grad_in.at[0, pl.ds((b - blocks + ends) * hidden, hidden)]
        return pltpu.make_async_copy(wide.at[b], target, store_sem.at[b])

    for b in range(LOADS_AHEAD):
        load(b).start()
    first.start()
    first_gain[...] = small[0:1]
    first_shift[...] = small[1:2]
    out_bias[...] = small[2:3]
    for i, ref in enumerate((in_bias, second_gain, second_shift, conv_bias, third_gain, third_shift)):
        ref[...] = small[3 + i // 2 : 4 + i // 2, (i % 2) * hidden : (i % 2 + 1) * hidden]
    hits = small[6:7, 0:VOCAB] + small[14:15, 0:VOCAB]
    tally = small[7:8, 0:VOCAB] + small[15:16, 0:VOCAB]
    scores[...] = hits / jnp.maximum(tally, 1.0)
    counts[...] = tally.astype(jnp.int32)
    for b in range(blocks):
        load(b).wait()
        if b + LOADS_AHEAD < blocks:
            load(b + LOADS_AHEAD).start()
        wide[b] = held[b].astype(jnp.float32)
        store(b).start()
        if b == 1:
            first.wait()
            second.start()
    for b in range(blocks):
        store(b).wait()
    second.wait()


def finish(given, big, small, width, base):
    hidden = big.shape[1]
    blocks = 2 * width // hidden + KERNEL
    full = jnp.float32
    shapes = [(1, width, hidden), (1, KERNEL, hidden, hidden), (1, hidden, width), (1, width), (1, width)]
    shapes += [(1, hidden)] * 6 + [(1, width), (1, VOCAB)]
    out = [jax.ShapeDtypeStruct(given.shape, given.dtype)]
    out += [jax.ShapeDtypeStruct(shape, full) for shape in shapes] + [jax.ShapeDtypeStruct((1, VOCAB), jnp.int32)]
    return pl.pallas_call(
        functools.partial(finish_kernel, base),
        out_shape=out,
        in_specs=[pl.BlockSpec(memory_space=pltpu.HBM)] * 2 + [pl.BlockSpec(memory_space=pltpu.VMEM)],
        out_specs=[pl.BlockSpec(memory_space=pltpu.HBM)] * 4 + [pl.BlockSpec(memory_space=pltpu.VMEM)] * (len(out) - 4),
        scratch_shapes=[
            pltpu.VMEM(given.shape, given.dtype),
            pltpu.VMEM((blocks, hidden, hidden), big.dtype),
            pltpu.VMEM((blocks, hidden, hidden), full),
            pltpu.SemaphoreType.DMA((2,)),
            pltpu.SemaphoreType.DMA((blocks,)),
            pltpu.SemaphoreType.DMA((blocks,)),
        ],
        compiler_params=pltpu.CompilerParams(vmem_limit_bytes=VMEM_BYTES),
    )(given, big, small)


def shards(
    boundary, lengths, masked, residues, readout,
    first_gain, first_shift, in_weight, in_bias, second_gain, second_shift, conv_weight, conv_bias,
    third_gain, third_shift, out_weight, out_bias,
):
    ny, nz = lax.axis_size("seq") // 2, lax.axis_size("dp")
    width, hidden = in_weight.shape[1], in_weight.shape[2]
    given, big, small = run_blocks(
        (
            boundary, lengths, masked, residues, readout.T,
            first_gain, first_shift, in_weight, in_bias, second_gain, second_shift, conv_weight, conv_bias,
            third_gain, third_shift, out_weight, out_bias,
        ),
        ny,
        nz,
    )
    (
        boundary_out, grad_in_weight, grad_conv_weight, grad_out_weight, grad_first_gain, grad_first_shift, grad_in_bias,
        grad_second_gain, grad_second_shift, grad_conv_bias, grad_third_gain, grad_third_shift, grad_out_bias,
        scores, counts,
    ) = finish(given, big, small, width, ring_plan(width, hidden, ny * nz)[0][1][1])
    return (
        boundary_out,
        grad_first_gain,
        grad_first_shift,
        grad_in_weight,
        grad_in_bias,
        grad_second_gain,
        grad_second_shift,
        grad_conv_weight,
        grad_conv_bias,
        grad_third_gain,
        grad_third_shift,
        grad_out_weight,
        grad_out_bias,
        scores[0],
        counts[0],
    )


def solution(mesh):
    in_specs = (
        P("section", "dp", "seq", None),
        P("dp", None),
        P("dp", "seq"),
        P("dp", "seq"),
        P(),
        P("section", None),
        P("section", None),
        P("section", None, None),
        P("section", None),
        P("section", None),
        P("section", None),
        P("section", None, None, None),
        P("section", None),
        P("section", None),
        P("section", None),
        P("section", None, None),
        P("section", None),
    )
    out_specs = (
        P("section", "dp", "seq", None),
        P("section", None),
        P("section", None),
        P("section", None, None),
        P("section", None),
        P("section", None),
        P("section", None),
        P("section", None, None, None),
        P("section", None),
        P("section", None),
        P("section", None),
        P("section", None, None),
        P("section", None),
        P(),
        P(),
    )
    return jax.shard_map(shards, mesh=mesh, in_specs=in_specs, out_specs=out_specs, check_vma=False)
```

```python
import functools

import jax
import jax.numpy as jnp
from jax import lax
from jax.experimental import pallas as pl
from jax.experimental.pallas import tpu as pltpu
from jax.sharding import PartitionSpec as P

KERNEL = 5
VOCAB = 30
DILATION_STEP = 128
ITEMS = 4
EPSILON = 1e-05
ROOT_HALF = 0.7071067811865476
HALF_LOG = -0.7213475204444817
ROOT_TAU = 0.3989422804014327

MESH = pl.DeviceIdType.MESH
LANES = 2
LOADS_AHEAD = 4
VMEM_BYTES = 64 << 20


def far_rows(left, own, right, offset):
    edge, positions = left.shape[0], own.shape[0]
    first, last = offset + edge, offset + edge + positions
    pieces, at = [], 0
    for block in (left, own, right):
        lo, hi = max(first, at), min(last, at + block.shape[0])
        if lo < hi:
            pieces.append(block[lo - at : hi - at])
        at += block.shape[0]
    return pieces[0] if len(pieces) == 1 else jnp.concatenate(pieces, axis=0)


def act_forward(values, gain, shift, real):
    scale = 1.0 / values.shape[1]
    centred = values - jnp.sum(values, axis=1, keepdims=True) * scale
    spread = jnp.sum(centred * centred, axis=1, keepdims=True) * scale
    inverse = lax.rsqrt(spread + EPSILON)
    hat = centred * inverse
    moved = hat * gain + shift
    below = (0.5 + 0.5 * lax.erf(moved * ROOT_HALF)) * real
    density = jnp.exp2(moved * moved * HALF_LOG) * (ROOT_TAU * real)
    return moved * below, hat, below + moved * density, inverse


def fold(values):
    rows, columns = values.shape
    return jnp.sum(values.reshape(rows // 8, 8, columns), axis=0)


def act_backward(grad, hat, slope, inverse, gain, gain_sum, shift_sum):
    scale = 1.0 / grad.shape[1]
    hat = hat.astype(jnp.float32)
    moved = grad * slope.astype(jnp.float32)
    turned = moved * hat
    shift_sum[...] += fold(moved)
    gain_sum[...] += fold(turned)
    mean = jnp.sum(moved * gain, axis=1, keepdims=True) * scale
    tilt = jnp.sum(turned * gain, axis=1, keepdims=True) * scale
    return inverse * (moved * gain - mean - hat * tilt)


def dot_nn(a, b):
    return jnp.dot(a, b, preferred_element_type=jnp.float32)


def dot_nt(a, b):
    return lax.dot_general(a, b, (((1,), (1,)), ((), ())), preferred_element_type=jnp.float32)


def dot_tn(a, b):
    return lax.dot_general(a, b, (((0,), (0,)), ((), ())), preferred_element_type=jnp.float32)


def blocks_kernel(
    edge, plan,
    boundary, lengths, masked, residues, readout,
    first_gain, first_shift, in_weight, in_bias, second_gain, second_shift, conv_weight, conv_bias,
    third_gain, third_shift, out_weight, out_bias,
    result, big, small_out,
    buf, w_in, w_conv, w_out, total, hat1, slope1, act1, taps, back_taps,
    hat2, slope2, hat3, slope3, act3, rim_left, rim_right, near, masks,
    sums_wide, sums, hits, tally, core_land, small, small_land,
    load_sem, weight_sem, result_sem, hand_send, hand_recv, rim_send, rim_recv, small_send, small_recv, *ring_refs,
):
    grad1, grad2 = hat2, hat3
    section = lax.axis_index("section")
    seq = lax.axis_index("seq")
    dp = lax.axis_index("dp")
    n_seq = lax.axis_size("seq")
    rows, positions = buf.shape[0] // 2, buf.shape[1]
    hidden = w_in.shape[1]
    leading = section == 0
    trailing = section == 1
    row_len = n_seq * positions
    first_position = seq * positions
    reach = edge // positions
    dilation = jnp.where(leading, 1, DILATION_STEP)

    def load(m):
        return pltpu.make_async_copy(boundary.at[0, m], buf.at[section * rows + m], load_sem.at[m])

    weight_loads = [
        pltpu.make_async_copy(source.at[0], target, weight_sem.at[i])
        for i, (source, target) in enumerate(((in_weight, w_in), (conv_weight, w_conv), (out_weight, w_out)))
    ]
    load(0).start()
    weight_loads[0].start()

    def partner():
        return (1 - section, seq, dp)

    rings, at = [], 0
    for sizes, base, land in plan:
        ring = Ring(sizes, base, land, section, seq, dp, n_seq // 2, lax.axis_size("dp"))
        ring.bind(total, taps, core_land, big, ring_refs[at : at + ring.refs])
        at += ring.refs
        rings.append(ring)
    barrier = pltpu.get_barrier_semaphore()
    greet = [partner()] + rings[0].neighbours()
    for peer in greet:
        pl.semaphore_signal(barrier, inc=1, device_id=peer, device_id_type=MESH)
    greeted = len(greet)
    for j in range(1, reach + 1):
        for side in (-j, j):
            on = (seq + side >= 0) & (seq + side < n_seq)
            greeted = greeted + on.astype(jnp.int32)

            @pl.when(on)
            def _():
                pl.semaphore_signal(barrier, inc=1, device_id=(section, seq + side, dp), device_id_type=MESH)

    @pl.when(seq < reach)
    def _():
        rim_left[...] = jnp.zeros_like(rim_left)

    @pl.when(seq >= n_seq - reach)
    def _():
        rim_right[...] = jnp.zeros_like(rim_right)

    last = rows - 1
    half, quarter = positions // 2, positions // 4
    parts = ((0, half), (half, half))
    thirds = ((quarter, half), (0, quarter), (half + quarter, quarter))
    whole = ((0, positions),)

    def make_mask(m):
        lane = lax.broadcasted_iota(jnp.int32, (positions, 128), 1)
        place = lax.broadcasted_iota(jnp.int32, (positions, 128), 0) + first_position
        other = place + (lane - KERNEL // 2) * dilation
        end = 0
        here = jnp.zeros((positions, 128), jnp.int32)
        there = jnp.zeros((positions, 128), jnp.int32)
        for j in range(ITEMS):
            end = end + lengths[m, j]
            here = here + (place >= end).astype(jnp.int32)
            there = there + (other >= end).astype(jnp.int32)
        counts = (here == there) & (here < ITEMS) & (other >= 0) & (other < row_len)
        masks[m] = counts.astype(jnp.float32)

    def hand(source, m, part):
        first, count = (thirds if source is buf else parts)[part]
        block = pl.ds(first, count)
        target = buf.at[m, block] if source is buf else buf.at[rows + m, block]
        return pltpu.make_async_remote_copy(
            src_ref=source.at[m, block], dst_ref=target,
            send_sem=hand_send.at[m, part], recv_sem=hand_recv.at[m, part],
            device_id=partner(), device_id_type=MESH)

    def tap_rows(m, k, first=0, count=None):
        start = (m * KERNEL + k) * positions + first
        return pl.ds(pl.multiple_of(start, 16), positions if count is None else count)

    def near_copies(backward, m):
        slot = 2 * backward + m % 2
        turn = backward * rows + m

        def edge_rows(first):
            return grad2.at[m, pl.ds(first, 16)] if backward else taps.at[tap_rows(m, KERNEL // 2, first, 16)]

        def copy(source, target, index, to):
            return pltpu.make_async_remote_copy(
                src_ref=source, dst_ref=target, send_sem=rim_send.at[turn, index], recv_sem=rim_recv.at[turn, index],
                device_id=(section, to, dp), device_id_type=MESH)

        return [
            (seq + 1 < n_seq, seq >= 1,
             copy(edge_rows(positions - 16), rim_left.at[slot, pl.ds(edge - 16, 16)], 0, seq + 1)),
            (seq >= 1, seq + 1 < n_seq,
             copy(edge_rows(0), rim_right.at[slot, pl.ds(0, 16)], 1, seq - 1)),
        ]

    def far_copies(backward, m, part, pieces):
        first, count = pieces[part]
        slot = 2 * backward + m % 2
        turn = backward * rows + m
        own = grad2.at[m, pl.ds(first, count)] if backward else taps.at[tap_rows(m, KERNEL // 2, first, count)]

        def copy(target, index, to):
            return pltpu.make_async_remote_copy(
                src_ref=own, dst_ref=target,
                send_sem=rim_send.at[turn, 3 * index + part], recv_sem=rim_recv.at[turn, 3 * index + part],
                device_id=(section, to, dp), device_id_type=MESH)

        copies = []
        for j in range(1, reach + 1):
            copies.append((
                seq + j < n_seq, seq >= j,
                copy(rim_left.at[slot, pl.ds(edge - j * positions + first, count)], 2 * j - 2, seq + j)))
            copies.append((
                seq >= j, seq + j < n_seq,
                copy(rim_right.at[slot, pl.ds((j - 1) * positions + first, count)], 2 * j - 1, seq - j)))
        return copies

    def begin(copies):
        for sends, _, copy in copies:
            pl.when(sends)(copy.start)

    def end(copies):
        for sends, receives, copy in copies:
            pl.when(receives)(copy.wait_recv)
            pl.when(sends)(copy.wait_send)

    def gather_near(backward, m, own, store, rims):
        slot = 2 * backward + m % 2
        if not rims:
            near[16 : 16 + positions] = own.astype(jnp.float32)
            pieces = thirds[:1]
        else:
            near[0:16] = rim_left[slot, edge - 16 : edge].astype(jnp.float32)
            near[16 + positions : 32 + positions] = rim_right[slot, 0:16].astype(jnp.float32)
            pieces = thirds[1:]
        for first, count in pieces:
            mask = masks[m, first : first + count]
            for k in range(KERNEL):
                if k != KERNEL // 2:
                    at = 16 + first + k - KERNEL // 2
                    store(k, first, jnp.where(mask[:, k : k + 1] > 0, near[at : at + count], 0.0))

    def gather_far(backward, m, own, store):
        slot = 2 * backward + m % 2
        mask = masks[m]
        for k in range(KERNEL):
            if k != KERNEL // 2:
                piece = far_rows(rim_left[slot], own, rim_right[slot], (k - KERNEL // 2) * DILATION_STEP)
                store(k, 0, jnp.where(mask[:, k : k + 1] > 0, piece.astype(jnp.float32), 0.0))

    def store_tap(m):
        def store(k, first, value):
            taps[tap_rows(m, k, first, value.shape[0])] = value.astype(jnp.bfloat16)

        return store

    def store_back(k, first, value):
        back_taps[k - (k > KERNEL // 2), first : first + value.shape[0]] = value.astype(jnp.bfloat16)

    def front(m, piece):
        block = slice(piece[0], piece[0] + piece[1])
        real = masks[m, block, KERNEL // 2 : KERNEL // 2 + 1]
        act, hat, slope, inverse = act_forward(
            buf[m, block].astype(jnp.float32), first_gain[...], first_shift[...], real)
        act1[m, block] = act.astype(jnp.bfloat16)
        hat1[m, block] = hat.astype(jnp.bfloat16)
        slope1[m, block] = slope.astype(jnp.bfloat16)
        masks[m, block, 8:9] = inverse
        pre = dot_nn(act1[m, block], w_in[...]) + in_bias[...]
        act, hat, slope, inverse = act_forward(pre, second_gain[...], second_shift[...], real)
        taps[tap_rows(m, KERNEL // 2, *piece)] = act.astype(jnp.bfloat16)
        hat2[m, block] = hat.astype(jnp.bfloat16)
        slope2[m, block] = slope.astype(jnp.bfloat16)
        masks[m, block, 9:10] = inverse

    def middle_tap(m, piece):
        return conv_bias[...] + dot_nn(taps[tap_rows(m, KERNEL // 2, *piece)], w_conv[KERNEL // 2])

    def rear(m, piece, pre):
        block = slice(piece[0], piece[0] + piece[1])
        for k in range(KERNEL):
            if k != KERNEL // 2:
                pre = pre + dot_nn(taps[tap_rows(m, k, *piece)], w_conv[k])
        real = masks[m, block, KERNEL // 2 : KERNEL // 2 + 1]
        act, hat, slope, inverse = act_forward(pre, third_gain[...], third_shift[...], real)
        act3[m, block] = act.astype(jnp.bfloat16)
        hat3[m, block] = hat.astype(jnp.bfloat16)
        slope3[m, block] = slope.astype(jnp.bfloat16)
        masks[m, block, 10:11] = inverse
        out = buf[m, block].astype(jnp.float32) + (dot_nn(act3[m, block], w_out[...]) + out_bias[...])
        buf[m, block] = out.astype(jnp.bfloat16)

    def count_types(m):
        logits = dot_nt(readout[...], buf[m])
        kind = lax.broadcasted_iota(jnp.int32, logits.shape, 0)
        odds = jnp.exp(logits - jnp.max(logits, axis=0, keepdims=True))
        odds = odds / jnp.sum(odds, axis=0, keepdims=True)
        stop = lengths[m, 0]
        for j in range(1, ITEMS):
            stop = stop + lengths[m, j]
        spot = lax.broadcasted_iota(jnp.int32, (1, positions), 1) + first_position
        chosen = jnp.where(spot < stop, masked[pl.ds(m, 1)].astype(jnp.float32), 0.0)
        chosen = jnp.where(kind == residues[pl.ds(m, 1)], chosen, 0.0)
        hits[...] += chosen * odds
        tally[...] += chosen

    def back_front(m, piece):
        block = slice(piece[0], piece[0] + piece[1])
        sums_wide[2] += fold(buf[rows + m, block].astype(jnp.float32))
        grad = dot_nt(buf[rows + m, block], w_out[...])
        low = act_backward(
            grad, hat3[m, block], slope3[m, block], masks[m, block, 10:11], third_gain[...], sums.at[4], sums.at[5]
        ).astype(jnp.bfloat16)
        grad2[m, block] = low
        sums[3] += fold(low.astype(jnp.float32))

    def back_middle_tap(m):
        return dot_nt(grad2[m], w_conv[KERNEL // 2])

    def back_rear(m, grad, between=None):
        for k in range(KERNEL):
            if k != KERNEL // 2:
                grad = grad + dot_nt(back_taps[k - (k > KERNEL // 2)], w_conv[KERNEL - 1 - k])
        if between is not None:
            between()
        low = act_backward(
            grad, hat2[m], slope2[m], masks[m, :, 9:10], second_gain[...], sums.at[1], sums.at[2]
        ).astype(jnp.bfloat16)
        grad1[m] = low
        sums[0] += fold(low.astype(jnp.float32))

    def back_last(m, piece):
        block = slice(piece[0], piece[0] + piece[1])
        grad = dot_nt(grad1[m, block], w_in[...])
        grad = act_backward(
            grad, hat1[m, block], slope1[m, block], masks[m, block, 8:9], first_gain[...],
            sums_wide.at[0], sums_wide.at[1])
        hat1[m, block] = (buf[rows + m, block].astype(jnp.float32) + grad).astype(jnp.bfloat16)

    def give(source, m):
        return pltpu.make_async_copy(source.at[m], result.at[0, m], result_sem.at[m])

    wide = buf.shape[2] // hidden

    def add_block(start, value):
        total[pl.ds(start, hidden)] += value

    def weights_out(m):
        for j in range(wide):
            add_block((KERNEL + j) * hidden, dot_tn(act3[m], buf[rows + m, :, j * hidden : (j + 1) * hidden]))

    def weights_conv(m):
        for k in range(KERNEL):
            add_block(k * hidden, dot_tn(taps[tap_rows(m, k)], grad2[m]))

    def weights_in(m):
        for j in range(wide):
            add_block(rings[1].base + j * hidden, dot_tn(act1[m, :, j * hidden : (j + 1) * hidden], grad1[m]))

    def first_lane():
        rings[0].exchange(2)
        rings[0].towards(0, 0, True)

    def step(i, carry):
        fronts = i < rows
        m_start = jnp.where(leading, i - rows, i)
        m_end = m_start - 1
        m_sum = i - rows
        final = i == 2 * rows

        def on(m):
            return (m >= 0) & (m < rows)

        @pl.when(fronts)
        def _():
            make_mask(i)

        @pl.when(i == 0)
        def _():
            weight_loads[0].wait()
            for copy in weight_loads[1:]:
                copy.start()

        @pl.when(leading & fronts)
        def _():
            load(i).wait()

        @pl.when(i == 0)
        def _():
            for m in range(1, rows):
                load(m).start()

        @pl.when(trailing & (i < last))
        def _():
            for part in range(3):
                hand(buf, i, part).wait_recv()

        @pl.when(fronts & (leading | (i < last)))
        def _():
            front(i, whole[0])

        @pl.when(i == 0)
        def _():
            pl.semaphore_wait(barrier, greeted)

        @pl.when(leading & fronts)
        def _():
            begin(near_copies(0, i))

        @pl.when(trailing & (i < last))
        def _():
            begin(far_copies(0, i, 0, whole))

        @pl.when(trailing & (i == last))
        def _():
            for part in range(3):
                hand(buf, last, part).wait_recv()
                front(last, thirds[part])
                begin(far_copies(0, last, part, thirds))

        @pl.when(i == 0)
        def _():
            weight_loads[1].wait()
            weight_loads[2].wait()

        @pl.when(on(m_end))
        def _():
            grad = back_middle_tap(m_end)

            @pl.when(leading)
            def _():
                gather_near(1, m_end, grad2[m_end], store_back, False)
                end(near_copies(1, m_end))
                gather_near(1, m_end, grad2[m_end], store_back, True)

            @pl.when(trailing)
            def _():
                for part in range(2):
                    end(far_copies(1, m_end, part, parts))
                gather_far(1, m_end, grad2[m_end], store_back)

            back_rear(m_end, grad, lambda: pl.when(final)(first_lane))
            for part in range(2):
                back_last(m_end, parts[part])
                pl.when(trailing)(hand(hat1, m_end, part).start)
            pl.when(leading)(give(hat1, m_end).start)

        @pl.when(trailing & final)
        def _():
            first_lane()

        @pl.when(on(m_sum - 1))
        def _():
            weights_in(m_sum - 1)

        @pl.when(final)
        def _():
            for lane in range(1, rings[0].lanes):
                rings[0].towards(0, lane, True)
            rings[1].exchange(0)
            rings[1].exchange(1)

        @pl.when(leading & fronts)
        def _():
            gather_near(0, i, taps[tap_rows(i, KERNEL // 2)], store_tap(i), False)
            rear(i, thirds[0], middle_tap(i, thirds[0]))
            hand(buf, i, 0).start()
            end(near_copies(0, i))
            gather_near(0, i, taps[tap_rows(i, KERNEL // 2)], store_tap(i), True)
            for part in (1, 2):
                rear(i, thirds[part], middle_tap(i, thirds[part]))
                hand(buf, i, part).start()

        @pl.when((leading & (i == 2)) | (trailing & (i == 0)))
        def _():
            total[...] = jnp.zeros_like(total)
            sums_wide[...] = jnp.zeros_like(sums_wide)
            sums[...] = jnp.zeros_like(sums)
            hits[...] = jnp.zeros_like(hits)
            tally[...] = jnp.zeros_like(tally)

        @pl.when(trailing & fronts)
        def _():
            pre = middle_tap(i, whole[0])

            @pl.when(i < last)
            def _():
                end(far_copies(0, i, 0, whole))

            @pl.when(i == last)
            def _():
                for part in range(3):
                    end(far_copies(0, last, part, thirds))

            gather_far(0, i, taps[tap_rows(i, KERNEL // 2)], store_tap(i))
            rear(i, whole[0], pre)
            give(buf, i).start()

        @pl.when(on(m_start))
        def _():
            pl.when(trailing)(load(m_start).wait)
            for part in range(2):
                pl.when(leading)(hand(hat1, m_start, part).wait_recv)
                back_front(m_start, parts[part])

                @pl.when(trailing)
                def _():
                    begin(far_copies(1, m_start, part, parts))

            @pl.when(leading)
            def _():
                begin(near_copies(1, m_start))

        @pl.when(trailing & fronts)
        def _():
            count_types(i)

        @pl.when(on(m_sum))
        def _():
            weights_out(m_sum)
            weights_conv(m_sum)

        @pl.when(i == 2 * rows - 1)
        def _():
            rings[0].exchange(0)
            rings[0].exchange(1)

        return carry

    lax.fori_loop(0, 2 * rows + 1, step, 0)

    for i in range(3):
        small[i : i + 1, :] = jnp.sum(sums_wide[i], axis=0, keepdims=True)
    for i in range(6):
        small[3 + i // 2 : 4 + i // 2, (i % 2) * hidden : (i % 2 + 1) * hidden] = jnp.sum(sums[i], axis=0, keepdims=True)
    small[6:8, :] = jnp.zeros((2, small.shape[1]), jnp.float32)
    ones = jnp.ones((8, positions), jnp.float32)
    for i, counted in ((6, hits), (7, tally)):
        row = lax.dot_general(
            ones, counted[...], (((1,), (1,)), ((), ())), precision=lax.Precision.HIGHEST,
            preferred_element_type=jnp.float32)
        small[i : i + 1, 0 : counted.shape[0]] = row[0:1]
    run_rings(rings, SmallSum(rings[0], small, small_land, small_out, small_send, small_recv, partner()))
    for m in range(rows):
        @pl.when(leading)
        def _():
            for part in range(3):
                hand(buf, m, part).wait_send()
            give(hat1, m).wait()

        @pl.when(trailing)
        def _():
            for part in range(2):
                hand(hat1, m, part).wait_send()
            give(buf, m).wait()


def ring_plan(width, hidden, nodes):
    plan, base, land = [], 0, 0
    for rows, subs in (((KERNEL + width // hidden) * hidden, LANES), (width, 1)):
        sizes = ring_sizes(rows // 2, nodes, subs)
        plan.append((sizes, base, land))
        land += nodes * sum(map(sum, sizes))
        base = 2 * land
    return plan, land


def run_blocks(args, ny, nz, cid=0):
    nodes = ny * nz
    doublings = 1 + (ny - 1).bit_length() + (nz - 1).bit_length()
    boundary, in_weight, conv_weight = args[0], args[7], args[11]
    _, rows, positions, width = boundary.shape
    hidden = in_weight.shape[2]
    edge = KERNEL // 2 * DILATION_STEP
    assert edge % positions == 0 and positions % 32 == 0 and width % hidden == 0
    reach = edge // positions
    low, full = jnp.bfloat16, jnp.float32
    wide_rows = pltpu.VMEM((rows, positions, width), low)
    thin_rows = pltpu.VMEM((rows, positions, hidden), low)
    plan, half = ring_plan(width, hidden, nodes)
    where = [pltpu.HBM, pltpu.SMEM] + [pltpu.VMEM] * 15
    for i in (7, 11, 15):
        where[i] = pltpu.HBM
    return pl.pallas_call(
        functools.partial(blocks_kernel, edge, plan),
        out_shape=(
            jax.ShapeDtypeStruct(boundary.shape, low),
            jax.ShapeDtypeStruct((2 * half, hidden), low),
            jax.ShapeDtypeStruct((16, width), full),
        ),
        in_specs=[pl.BlockSpec(memory_space=space) for space in where],
        out_specs=[pl.BlockSpec(memory_space=space) for space in (pltpu.HBM, pltpu.HBM, pltpu.VMEM)],
        scratch_shapes=[
            pltpu.VMEM((2 * rows, positions, width), low),
            pltpu.VMEM((width, hidden), low),
            pltpu.VMEM((KERNEL, hidden, hidden), low),
            pltpu.VMEM((hidden, width), low),
            pltpu.VMEM((2 * half, hidden), full),
            wide_rows, wide_rows, wide_rows,
            pltpu.VMEM((max(rows * KERNEL * positions, half), hidden), low),
            pltpu.VMEM((KERNEL - 1, positions, hidden), low),
            thin_rows, thin_rows, thin_rows, thin_rows, thin_rows,
            pltpu.VMEM((4, edge, hidden), low),
            pltpu.VMEM((4, edge, hidden), low),
            pltpu.VMEM((positions + 32, hidden), full),
            pltpu.VMEM((rows, positions, 128), full),
            pltpu.VMEM((3, 8, width), full),
            pltpu.VMEM((6, 8, hidden), full),
            pltpu.VMEM((VOCAB, positions), full),
            pltpu.VMEM((VOCAB, positions), full),
            pltpu.VMEM((half, hidden), low),
            pltpu.VMEM((8, width), full),
            pltpu.VMEM((2 * doublings, 8, width), full),
            pltpu.SemaphoreType.DMA((rows,)),
            pltpu.SemaphoreType.DMA((3,)),
            pltpu.SemaphoreType.DMA((rows,)),
            pltpu.SemaphoreType.DMA((rows, 3)),
            pltpu.SemaphoreType.DMA((rows, 3)),
            pltpu.SemaphoreType.DMA((2 * rows, 6 * reach)),
            pltpu.SemaphoreType.DMA((2 * rows, 6 * reach)),
            pltpu.SemaphoreType.DMA((doublings + 1,)),
            pltpu.SemaphoreType.DMA((doublings + 1,)),
        ]
        + [scratch for sizes, _, _ in plan for scratch in ring_scratch(sizes, nodes, hidden)],
        compiler_params=pltpu.CompilerParams(
            collective_id=cid, has_side_effects=True, vmem_limit_bytes=VMEM_BYTES),
    )(*args)


def ring_sizes(rows, nodes, subs):
    units = -(-rows // (nodes * 16))
    long = -(-units // 2)
    return [[16 * ((way + i) // subs) for i in range(subs)] for way in (long, units - long)]


def ring_flows(sizes):
    return [(way, i) for i in range(len(sizes[0])) for way in range(2) if sizes[way][i]]


def ring_scratch(sizes, nodes, columns):
    flows = ring_flows(sizes)
    n = len(flows)
    counts = [(n, nodes)] * 2 + [(n, 2 * nodes - 2)] * 2 + [(n, nodes)] * 2 + [(n,)]
    return [pltpu.SemaphoreType.DMA(count) for count in counts] + [
        pltpu.VMEM((nodes - 1, sizes[way][i], columns), jnp.bfloat16) for way, i in flows]


class Ring:
    def __init__(self, sizes, base, land, section, seq, dp, ny, nz):
        self.sizes, self.base, self.land, self.nodes = sizes, base, land, ny * nz
        self.flows = ring_flows(sizes)
        self.refs = 7 + len(self.flows)
        self.lanes = len(sizes[0])
        self.section, self.nz = section, nz
        self.core, ypos = seq % 2, seq // 2
        self.spot = ypos * nz + dp + (ypos % 2) * (nz - 1 - 2 * dp)
        self.other_core = (section, seq + 1 - 2 * self.core, dp)
        self.turn = [1 - 2 * self.core, 2 * self.core - 1]
        self.next = [self.at_spot(self.wrap(self.spot + self.nodes + turn)) for turn in self.turn]
        self.half = sum(map(sum, sizes)) * self.nodes
        self.first, at = {}, 0
        for way, i in self.flows:
            self.first[way, i] = at
            at += sizes[way][i] * self.nodes
        self.peers = [self.other_core]
        reach = 1
        while reach < ny:
            self.peers.append((section, seq + 2 * reach - 4 * reach * ((ypos // reach) % 2), dp))
            reach *= 2
        reach = 1
        while reach < nz:
            self.peers.append((section, seq, dp + reach - 2 * reach * ((dp // reach) % 2)))
            reach *= 2

    def wrap(self, place):
        if self.nodes & (self.nodes - 1) == 0:
            return place & (self.nodes - 1)
        return lax.rem(place, self.nodes)

    def at_spot(self, place):
        y = place // self.nz
        z = place % self.nz
        return (self.section, y * 2 + self.core, z + (y % 2) * (self.nz - 1 - 2 * z))

    def neighbours(self):
        around = self.next
        return self.peers + around

    def bind(self, total, stage, core_land, big, refs):
        self.total, self.stage, self.core_land, self.big = total, stage, core_land, big
        self.core_sems, self.ring_sems, self.over_sems = refs[0:2], refs[2:4], refs[4:6]
        self.keep_sem, self.lands = refs[6], refs[7:]

    def count(self, f):
        way, i = self.flows[f]
        return self.sizes[way][i]

    def rows(self, f, side, shard):
        start = self.base + side * self.half + self.first[self.flows[f]] + shard * self.count(f)
        return pl.ds(pl.multiple_of(start, 16), self.count(f))

    def land_rows(self, f, shard):
        start = self.land + self.first[self.flows[f]] + shard * self.count(f)
        return pl.ds(pl.multiple_of(start, 16), self.count(f))

    def shard(self, f, step):
        return self.wrap(self.spot + 2 * self.nodes - self.turn[self.flows[f][0]] * step)

    def ahead(self, f):
        return self.next[self.flows[f][0]]

    def remote(self, source, target, sems, index, peer):
        return pltpu.make_async_remote_copy(
            src_ref=source, dst_ref=target, send_sem=sems[0].at[index], recv_sem=sems[1].at[index],
            device_id=peer, device_id_type=MESH)

    def core_copy(self, f, shard):
        rows = self.land_rows(f, shard)
        return self.remote(self.stage.at[rows], self.core_land.at[rows], self.core_sems, (f, shard), self.other_core)

    def ring_copy(self, f, step, shard):
        return self.remote(
            self.core_land.at[self.land_rows(f, shard)], self.lands[f].at[step], self.ring_sems, (f, step), self.ahead(f))

    def back_copy(self, f, step, shard):
        block = self.big.at[self.rows(f, self.core, shard)]
        return self.remote(
            self.core_land.at[self.land_rows(f, shard)] if step is None else block, block,
            self.ring_sems, (f, self.nodes - 1 + (0 if step is None else step)), self.ahead(f))

    def over_copy(self, f, shard, own=False):
        block = self.big.at[self.rows(f, self.core, shard)]
        return self.remote(
            self.core_land.at[self.land_rows(f, shard)] if own else block, block,
            self.over_sems, (f, shard), self.other_core)

    def keep_copy(self, f, shard):
        return pltpu.make_async_copy(
            self.core_land.at[self.land_rows(f, shard)], self.big.at[self.rows(f, self.core, shard)], self.keep_sem.at[f])

    def add(self, f, shard, step):
        rows = self.land_rows(f, shard)
        value = self.total[self.rows(f, self.core, shard)] + self.core_land[rows].astype(jnp.float32)
        if step is not None:
            value = value + self.lands[f][step].astype(jnp.float32)
        self.core_land[rows] = value.astype(jnp.bfloat16)

    def exchange(self, step):
        for f in range(len(self.flows)):
            shard = self.shard(f, -step)
            self.stage[self.land_rows(f, shard)] = self.total[self.rows(f, 1 - self.core, shard)].astype(jnp.bfloat16)
            self.core_copy(f, shard).start()

    def of(self, lane):
        return [f for f in range(len(self.flows)) if lane is None or self.flows[f][1] == lane]

    def towards(self, step, lane=None, first=False):
        for f in self.of(lane):
            shard = self.shard(f, step)
            self.core_copy(f, shard).wait_recv()
            if first:
                self.add(f, shard, None)
            else:
                self.ring_copy(f, step - 1, shard).wait_recv()
                self.add(f, shard, step - 1)
            self.ring_copy(f, step, shard).start()

    def back(self, step, lane=None):
        for f in self.of(lane):
            shard = self.shard(f, self.nodes - 1 + step)
            self.back_copy(f, step - 1, shard).wait_recv()
            self.back_copy(f, step, shard).start()
            self.over_copy(f, shard).start()

    def own(self, lane=None):
        for f in self.of(lane):
            shard = self.shard(f, self.nodes - 1)
            self.core_copy(f, shard).wait_recv()
            self.ring_copy(f, self.nodes - 2, shard).wait_recv()
            self.add(f, shard, self.nodes - 2)
            self.back_copy(f, None, shard).start()
            self.over_copy(f, shard, True).start()
            self.keep_copy(f, shard).start()

    def arrive(self, lane=None):
        for f in self.of(lane):
            shard = self.shard(f, 2 * self.nodes - 2)
            self.back_copy(f, self.nodes - 2, shard).wait_recv()
            self.over_copy(f, shard).start()

    def settle(self):
        def crossed(step, carry):
            for f in range(len(self.flows)):
                self.core_copy(f, step).wait_send()
                self.over_copy(f, step).wait()
            return carry

        def rounded(step, carry):
            for f in range(len(self.flows)):
                self.ring_copy(f, step, 0).wait_send()
                self.back_copy(f, step, 0).wait_send()
            return carry

        lax.fori_loop(0, self.nodes, crossed, 0)
        lax.fori_loop(0, self.nodes - 1, rounded, 0)
        for f in range(len(self.flows)):
            self.keep_copy(f, 0).wait()


def run_rings(rings, small_sum):
    ahead, behind = rings
    nodes, lanes = ahead.nodes, ahead.lanes

    def each(method, *step):
        getattr(ahead, method)(*step, 0)
        getattr(behind, method)(*step)
        for lane in range(1, lanes):
            getattr(ahead, method)(*step, lane)

    ahead.exchange(3)
    for lane in range(lanes):
        ahead.towards(1, lane)
    small_sum.step(0)
    for step in (2, 3):
        ahead.exchange(step + 2)
        behind.exchange(2 * step - 2)
        behind.exchange(2 * step - 1)
        ahead.towards(step, 0)
        behind.towards(2 * step - 4, first=step == 2)
        for lane in range(1, lanes):
            ahead.towards(step, lane)
        behind.towards(2 * step - 3)

    def towards(step, carry):
        ahead.exchange(step + 2)
        behind.exchange(step + 2)
        each("towards", step)
        return carry

    lax.fori_loop(4, nodes - 2, towards, 0)
    each("towards", nodes - 2)
    each("own")
    small_sum.step(1)
    at = 1
    for k in range(2, small_sum.steps):
        if at < nodes - 1:
            each("back", at)
            at += 1
        small_sum.step(k)

    def back(step, carry):
        each("back", step)
        return carry

    lax.fori_loop(at, nodes - 1, back, 0)
    each("arrive")
    ahead.settle()
    behind.settle()
    small_sum.settle()


class SmallSum:
    def __init__(self, ring, small, land, out, send_sem, recv_sem, other_section):
        self.peers, self.small, self.land, self.out = ring.peers + [other_section], small, land, out
        self.sems = (send_sem, recv_sem)
        self.remote = ring.remote
        self.steps = len(self.peers) + 1

    def held(self, k):
        return self.small if k == 0 else self.land.at[2 * k - 1]

    def copy(self, k):
        count = self.small.shape[0]
        target = self.out.at[pl.ds(count, count)] if k == len(self.peers) - 1 else self.land.at[2 * k]
        return self.remote(self.held(k), target, self.sems, k, self.peers[k])

    def step(self, k):
        last = len(self.peers) - 1
        if 0 < k:
            self.copy(k - 1).wait_recv()
        if 0 < k <= last:
            self.land[2 * k - 1] = self.held(k - 1)[...] + self.land[2 * k - 2]
        if k <= last:
            self.copy(k).start()
        if k == last:
            self.out[pl.ds(0, self.small.shape[0])] = self.held(k)[...]

    def settle(self):
        for k in range(len(self.peers)):
            self.copy(k).wait_send()


def finish_kernel(
    base, given, big, small, result, grad_in, grad_conv, grad_out, first_gain, first_shift, in_bias, second_gain,
    second_shift, conv_bias, third_gain, third_shift, out_bias, scores, counts,
    passed, held, wide, pass_sem, load_sem, store_sem,
):
    hidden = held.shape[2]
    blocks = held.shape[0]
    ends = grad_in.shape[1] // hidden
    first = pltpu.make_async_copy(given, passed, pass_sem.at[0])
    second = pltpu.make_async_copy(passed, result, pass_sem.at[1])

    def load(b):
        start = b * hidden if b < blocks - ends else base + (b - blocks + ends) * hidden
        return pltpu.make_async_copy(big.at[pl.ds(start, hidden)], held.at[b], load_sem.at[b])

    def store(b):
        if b < KERNEL:
            target = grad_conv.at[0, b]
        elif b < blocks - ends:
            target = grad_out.at[0, :, pl.ds((b - KERNEL) * hidden, hidden)]
        else:
            target = grad_in.at[0, pl.ds((b - blocks + ends) * hidden, hidden)]
        return pltpu.make_async_copy(wide.at[b], target, store_sem.at[b])

    for b in range(LOADS_AHEAD):
        load(b).start()
    first.start()
    first_gain[...] = small[0:1]
    first_shift[...] = small[1:2]
    out_bias[...] = small[2:3]
    for i, ref in enumerate((in_bias, second_gain, second_shift, conv_bias, third_gain, third_shift)):
        ref[...] = small[3 + i // 2 : 4 + i // 2, (i % 2) * hidden : (i % 2 + 1) * hidden]
    hits = small[6:7, 0:VOCAB] + small[14:15, 0:VOCAB]
    tally = small[7:8, 0:VOCAB] + small[15:16, 0:VOCAB]
    scores[...] = hits / jnp.maximum(tally, 1.0)
    counts[...] = tally.astype(jnp.int32)
    for b in range(blocks):
        load(b).wait()
        if b + LOADS_AHEAD < blocks:
            load(b + LOADS_AHEAD).start()
        wide[b] = held[b].astype(jnp.float32)
        store(b).start()
        if b == 1:
            first.wait()
            second.start()
    for b in range(blocks):
        store(b).wait()
    second.wait()


def finish(given, big, small, width, base):
    hidden = big.shape[1]
    blocks = 2 * width // hidden + KERNEL
    full = jnp.float32
    shapes = [(1, width, hidden), (1, KERNEL, hidden, hidden), (1, hidden, width), (1, width), (1, width)]
    shapes += [(1, hidden)] * 6 + [(1, width), (1, VOCAB)]
    out = [jax.ShapeDtypeStruct(given.shape, given.dtype)]
    out += [jax.ShapeDtypeStruct(shape, full) for shape in shapes] + [jax.ShapeDtypeStruct((1, VOCAB), jnp.int32)]
    return pl.pallas_call(
        functools.partial(finish_kernel, base),
        out_shape=out,
        in_specs=[pl.BlockSpec(memory_space=pltpu.HBM)] * 2 + [pl.BlockSpec(memory_space=pltpu.VMEM)],
        out_specs=[pl.BlockSpec(memory_space=pltpu.HBM)] * 4 + [pl.BlockSpec(memory_space=pltpu.VMEM)] * (len(out) - 4),
        scratch_shapes=[
            pltpu.VMEM(given.shape, given.dtype),
            pltpu.VMEM((blocks, hidden, hidden), big.dtype),
            pltpu.VMEM((blocks, hidden, hidden), full),
            pltpu.SemaphoreType.DMA((2,)),
            pltpu.SemaphoreType.DMA((blocks,)),
            pltpu.SemaphoreType.DMA((blocks,)),
        ],
        compiler_params=pltpu.CompilerParams(vmem_limit_bytes=VMEM_BYTES),
    )(given, big, small)


def shards(
    boundary, lengths, masked, residues, readout,
    first_gain, first_shift, in_weight, in_bias, second_gain, second_shift, conv_weight, conv_bias,
    third_gain, third_shift, out_weight, out_bias,
):
    ny, nz = lax.axis_size("seq") // 2, lax.axis_size("dp")
    width, hidden = in_weight.shape[1], in_weight.shape[2]
    given, big, small = run_blocks(
        (
            boundary, lengths, masked, residues, readout.T,
            first_gain, first_shift, in_weight, in_bias, second_gain, second_shift, conv_weight, conv_bias,
            third_gain, third_shift, out_weight, out_bias,
        ),
        ny,
        nz,
    )
    (
        boundary_out, grad_in_weight, grad_conv_weight, grad_out_weight, grad_first_gain, grad_first_shift, grad_in_bias,
        grad_second_gain, grad_second_shift, grad_conv_bias, grad_third_gain, grad_third_shift, grad_out_bias,
        scores, counts,
    ) = finish(given, big, small, width, ring_plan(width, hidden, ny * nz)[0][1][1])
    return (
        boundary_out,
        grad_first_gain,
        grad_first_shift,
        grad_in_weight,
        grad_in_bias,
        grad_second_gain,
        grad_second_shift,
        grad_conv_weight,
        grad_conv_bias,
        grad_third_gain,
        grad_third_shift,
        grad_out_weight,
        grad_out_bias,
        scores[0],
        counts[0],
    )


def solution(mesh):
    in_specs = (
        P("section", "dp", "seq", None),
        P("dp", None),
        P("dp", "seq"),
        P("dp", "seq"),
        P(),
        P("section", None),
        P("section", None),
        P("section", None, None),
        P("section", None),
        P("section", None),
        P("section", None),
        P("section", None, None, None),
        P("section", None),
        P("section", None),
        P("section", None),
        P("section", None, None),
        P("section", None),
    )
    out_specs = (
        P("section", "dp", "seq", None),
        P("section", None),
        P("section", None),
        P("section", None, None),
        P("section", None),
        P("section", None),
        P("section", None),
        P("section", None, None, None),
        P("section", None),
        P("section", None),
        P("section", None),
        P("section", None, None),
        P("section", None),
        P(),
        P(),
    )
    return jax.shard_map(shards, mesh=mesh, in_specs=in_specs, out_specs=out_specs, check_vma=False)
```

```python
import functools

import jax
import jax.numpy as jnp
from jax import lax
from jax.experimental import pallas as pl
from jax.experimental.pallas import tpu as pltpu
from jax.sharding import PartitionSpec as P

KERNEL = 5
VOCAB = 30
DILATION_STEP = 128
ITEMS = 4
EPSILON = 1e-05
ROOT_HALF = 0.7071067811865476
HALF_LOG = -0.7213475204444817
ROOT_TAU = 0.3989422804014327

MESH = pl.DeviceIdType.MESH
LANES = 2
VMEM_BYTES = 64 << 20


def far_rows(left, own, right, offset):
    edge, positions = left.shape[0], own.shape[0]
    first, last = offset + edge, offset + edge + positions
    pieces, at = [], 0
    for block in (left, own, right):
        lo, hi = max(first, at), min(last, at + block.shape[0])
        if lo < hi:
            pieces.append(block[lo - at : hi - at])
        at += block.shape[0]
    return pieces[0] if len(pieces) == 1 else jnp.concatenate(pieces, axis=0)


def act_forward(values, gain, shift, real):
    scale = 1.0 / values.shape[1]
    centred = values - jnp.sum(values, axis=1, keepdims=True) * scale
    spread = jnp.sum(centred * centred, axis=1, keepdims=True) * scale
    inverse = lax.rsqrt(spread + EPSILON)
    hat = centred * inverse
    moved = hat * gain + shift
    below = (0.5 + 0.5 * lax.erf(moved * ROOT_HALF)) * real
    density = jnp.exp2(moved * moved * HALF_LOG) * (ROOT_TAU * real)
    return moved * below, hat, below + moved * density, inverse


def fold(values):
    rows, columns = values.shape
    return jnp.sum(values.reshape(rows // 8, 8, columns), axis=0)


def act_backward(grad, hat, slope, inverse, gain, gain_sum, shift_sum):
    scale = 1.0 / grad.shape[1]
    hat = hat.astype(jnp.float32)
    moved = grad * slope.astype(jnp.float32)
    turned = moved * hat
    shift_sum[...] += fold(moved)
    gain_sum[...] += fold(turned)
    mean = jnp.sum(moved * gain, axis=1, keepdims=True) * scale
    tilt = jnp.sum(turned * gain, axis=1, keepdims=True) * scale
    return inverse * (moved * gain - mean - hat * tilt)


def dot_nn(a, b):
    return jnp.dot(a, b, preferred_element_type=jnp.float32)


def dot_nt(a, b):
    return lax.dot_general(a, b, (((1,), (1,)), ((), ())), preferred_element_type=jnp.float32)


def dot_tn(a, b):
    return lax.dot_general(a, b, (((0,), (0,)), ((), ())), preferred_element_type=jnp.float32)


def blocks_kernel(
    edge, plan,
    boundary, lengths, masked_in, residues_in, readout_in,
    first_gain_in, first_shift_in, in_weight, in_bias_in, second_gain_in, second_shift_in, conv_weight, conv_bias_in,
    third_gain_in, third_shift_in, out_weight, out_bias_in,
    result, big, small_out,
    masked, residues, readout, first_gain, first_shift, in_bias, second_gain, second_shift, conv_bias,
    third_gain, third_shift, out_bias,
    buf, w_in, w_conv, w_out, total, hat1, slope1, act1, taps, back_taps,
    hat2, slope2, hat3, slope3, act3, rim_left, rim_right, near, masks,
    sums_wide, sums, hits, tally, core_land, small, small_land,
    load_sem, weight_sem, result_sem, hand_send, hand_recv, rim_send, rim_recv, small_send, small_recv, input_sem, *ring_refs,
):
    grad1, grad2 = hat2, hat3
    section = lax.axis_index("section")
    seq = lax.axis_index("seq")
    dp = lax.axis_index("dp")
    n_seq = lax.axis_size("seq")
    rows, positions = buf.shape[0] // 2, buf.shape[1]
    hidden = w_in.shape[1]
    leading = section == 0
    trailing = section == 1
    row_len = n_seq * positions
    first_position = seq * positions
    reach = edge // positions
    dilation = jnp.where(leading, 1, DILATION_STEP)

    def load(m):
        return pltpu.make_async_copy(boundary.at[0, m], buf.at[section * rows + m], load_sem.at[m])

    weight_loads = [
        pltpu.make_async_copy(source.at[0], target, weight_sem.at[i])
        for i, (source, target) in enumerate(((in_weight, w_in), (conv_weight, w_conv), (out_weight, w_out)))
    ]
    input_loads = [
        pltpu.make_async_copy(source, target, input_sem.at[i])
        for i, (source, target) in enumerate((
            (first_gain_in, first_gain), (first_shift_in, first_shift), (in_bias_in, in_bias),
            (second_gain_in, second_gain), (second_shift_in, second_shift), (conv_bias_in, conv_bias),
            (third_gain_in, third_gain), (third_shift_in, third_shift), (out_bias_in, out_bias),
            (masked_in, masked), (residues_in, residues), (readout_in, readout),
        ))
    ]
    load(0).start()
    weight_loads[0].start()
    for copy in input_loads:
        copy.start()

    def partner():
        return (1 - section, seq, dp)

    rings, at = [], 0
    for sizes, base, land in plan:
        ring = Ring(sizes, base, land, section, seq, dp, n_seq // 2, lax.axis_size("dp"))
        ring.bind(total, taps, core_land, big, ring_refs[at : at + ring.refs])
        at += ring.refs
        rings.append(ring)
    barrier = pltpu.get_barrier_semaphore()
    greet = [partner()] + rings[0].neighbours()
    for peer in greet:
        pl.semaphore_signal(barrier, inc=1, device_id=peer, device_id_type=MESH)
    greeted = len(greet)
    for j in range(1, reach + 1):
        for side in (-j, j):
            on = (seq + side >= 0) & (seq + side < n_seq)
            greeted = greeted + on.astype(jnp.int32)

            @pl.when(on)
            def _():
                pl.semaphore_signal(barrier, inc=1, device_id=(section, seq + side, dp), device_id_type=MESH)

    @pl.when(seq < reach)
    def _():
        rim_left[...] = jnp.zeros_like(rim_left)

    @pl.when(seq >= n_seq - reach)
    def _():
        rim_right[...] = jnp.zeros_like(rim_right)

    last = rows - 1
    half, quarter = positions // 2, positions // 4
    parts = ((0, half), (half, half))
    thirds = ((quarter, half), (0, quarter), (half + quarter, quarter))
    whole = ((0, positions),)

    def make_mask(m):
        lane = lax.broadcasted_iota(jnp.int32, (positions, 128), 1)
        place = lax.broadcasted_iota(jnp.int32, (positions, 128), 0) + first_position
        other = place + (lane - KERNEL // 2) * dilation
        end = 0
        here = jnp.zeros((positions, 128), jnp.int32)
        there = jnp.zeros((positions, 128), jnp.int32)
        for j in range(ITEMS):
            end = end + lengths[m, j]
            here = here + (place >= end).astype(jnp.int32)
            there = there + (other >= end).astype(jnp.int32)
        counts = (here == there) & (here < ITEMS) & (other >= 0) & (other < row_len)
        masks[m] = counts.astype(jnp.float32)

    def hand(source, m, part):
        first, count = (thirds if source is buf else parts)[part]
        block = pl.ds(first, count)
        target = buf.at[m, block] if source is buf else buf.at[rows + m, block]
        return pltpu.make_async_remote_copy(
            src_ref=source.at[m, block], dst_ref=target,
            send_sem=hand_send.at[m, part], recv_sem=hand_recv.at[m, part],
            device_id=partner(), device_id_type=MESH)

    def tap_rows(m, k, first=0, count=None):
        start = (m * KERNEL + k) * positions + first
        return pl.ds(pl.multiple_of(start, 16), positions if count is None else count)

    def near_copies(backward, m):
        slot = 2 * backward + m % 2
        turn = backward * rows + m

        def edge_rows(first):
            return grad2.at[m, pl.ds(first, 16)] if backward else taps.at[tap_rows(m, KERNEL // 2, first, 16)]

        def copy(source, target, index, to):
            return pltpu.make_async_remote_copy(
                src_ref=source, dst_ref=target, send_sem=rim_send.at[turn, index], recv_sem=rim_recv.at[turn, index],
                device_id=(section, to, dp), device_id_type=MESH)

        return [
            (seq + 1 < n_seq, seq >= 1,
             copy(edge_rows(positions - 16), rim_left.at[slot, pl.ds(edge - 16, 16)], 0, seq + 1)),
            (seq >= 1, seq + 1 < n_seq,
             copy(edge_rows(0), rim_right.at[slot, pl.ds(0, 16)], 1, seq - 1)),
        ]

    def far_copies(backward, m, part, pieces):
        first, count = pieces[part]
        slot = 2 * backward + m % 2
        turn = backward * rows + m
        own = grad2.at[m, pl.ds(first, count)] if backward else taps.at[tap_rows(m, KERNEL // 2, first, count)]

        def copy(target, index, to):
            return pltpu.make_async_remote_copy(
                src_ref=own, dst_ref=target,
                send_sem=rim_send.at[turn, 3 * index + part], recv_sem=rim_recv.at[turn, 3 * index + part],
                device_id=(section, to, dp), device_id_type=MESH)

        copies = []
        for j in range(1, reach + 1):
            copies.append((
                seq + j < n_seq, seq >= j,
                copy(rim_left.at[slot, pl.ds(edge - j * positions + first, count)], 2 * j - 2, seq + j)))
            copies.append((
                seq >= j, seq + j < n_seq,
                copy(rim_right.at[slot, pl.ds((j - 1) * positions + first, count)], 2 * j - 1, seq - j)))
        return copies

    def begin(copies):
        for sends, _, copy in copies:
            pl.when(sends)(copy.start)

    def end(copies):
        for sends, receives, copy in copies:
            pl.when(receives)(copy.wait_recv)
            pl.when(sends)(copy.wait_send)

    def gather_near(backward, m, own, store, rims):
        slot = 2 * backward + m % 2
        if not rims:
            near[16 : 16 + positions] = own.astype(jnp.float32)
            pieces = thirds[:1]
        else:
            near[0:16] = rim_left[slot, edge - 16 : edge].astype(jnp.float32)
            near[16 + positions : 32 + positions] = rim_right[slot, 0:16].astype(jnp.float32)
            pieces = thirds[1:]
        for first, count in pieces:
            mask = masks[m, first : first + count]
            for k in range(KERNEL):
                if k != KERNEL // 2:
                    at = 16 + first + k - KERNEL // 2
                    store(k, first, jnp.where(mask[:, k : k + 1] > 0, near[at : at + count], 0.0))

    def gather_far(backward, m, own, store):
        slot = 2 * backward + m % 2
        mask = masks[m]
        for k in range(KERNEL):
            if k != KERNEL // 2:
                piece = far_rows(rim_left[slot], own, rim_right[slot], (k - KERNEL // 2) * DILATION_STEP)
                store(k, 0, jnp.where(mask[:, k : k + 1] > 0, piece.astype(jnp.float32), 0.0))

    def store_tap(m):
        def store(k, first, value):
            taps[tap_rows(m, k, first, value.shape[0])] = value.astype(jnp.bfloat16)

        return store

    def store_back(k, first, value):
        back_taps[k - (k > KERNEL // 2), first : first + value.shape[0]] = value.astype(jnp.bfloat16)

    def front(m, piece):
        block = slice(piece[0], piece[0] + piece[1])
        real = masks[m, block, KERNEL // 2 : KERNEL // 2 + 1]
        act, hat, slope, inverse = act_forward(
            buf[m, block].astype(jnp.float32), first_gain[...], first_shift[...], real)
        act1[m, block] = act.astype(jnp.bfloat16)
        hat1[m, block] = hat.astype(jnp.bfloat16)
        slope1[m, block] = slope.astype(jnp.bfloat16)
        masks[m, block, 8:9] = inverse
        pre = dot_nn(act1[m, block], w_in[...]) + in_bias[...]
        act, hat, slope, inverse = act_forward(pre, second_gain[...], second_shift[...], real)
        taps[tap_rows(m, KERNEL // 2, *piece)] = act.astype(jnp.bfloat16)
        hat2[m, block] = hat.astype(jnp.bfloat16)
        slope2[m, block] = slope.astype(jnp.bfloat16)
        masks[m, block, 9:10] = inverse

    def middle_tap(m, piece):
        return conv_bias[...] + dot_nn(taps[tap_rows(m, KERNEL // 2, *piece)], w_conv[KERNEL // 2])

    def rear(m, piece, pre):
        block = slice(piece[0], piece[0] + piece[1])
        for k in range(KERNEL):
            if k != KERNEL // 2:
                pre = pre + dot_nn(taps[tap_rows(m, k, *piece)], w_conv[k])
        real = masks[m, block, KERNEL // 2 : KERNEL // 2 + 1]
        act, hat, slope, inverse = act_forward(pre, third_gain[...], third_shift[...], real)
        act3[m, block] = act.astype(jnp.bfloat16)
        hat3[m, block] = hat.astype(jnp.bfloat16)
        slope3[m, block] = slope.astype(jnp.bfloat16)
        masks[m, block, 10:11] = inverse
        out = buf[m, block].astype(jnp.float32) + (dot_nn(act3[m, block], w_out[...]) + out_bias[...])
        buf[m, block] = out.astype(jnp.bfloat16)

    def count_types(m):
        logits = dot_nt(readout[...], buf[m])
        kind = lax.broadcasted_iota(jnp.int32, logits.shape, 0)
        odds = jnp.exp(logits - jnp.max(logits, axis=0, keepdims=True))
        odds = odds / jnp.sum(odds, axis=0, keepdims=True)
        stop = lengths[m, 0]
        for j in range(1, ITEMS):
            stop = stop + lengths[m, j]
        spot = lax.broadcasted_iota(jnp.int32, (1, positions), 1) + first_position
        chosen = jnp.where(spot < stop, masked[pl.ds(m, 1)].astype(jnp.float32), 0.0)
        chosen = jnp.where(kind == residues[pl.ds(m, 1)], chosen, 0.0)
        hits[...] += chosen * odds
        tally[...] += chosen

    def back_front(m, piece):
        block = slice(piece[0], piece[0] + piece[1])
        sums_wide[2] += fold(buf[rows + m, block].astype(jnp.float32))
        grad = dot_nt(buf[rows + m, block], w_out[...])
        low = act_backward(
            grad, hat3[m, block], slope3[m, block], masks[m, block, 10:11], third_gain[...], sums.at[4], sums.at[5]
        ).astype(jnp.bfloat16)
        grad2[m, block] = low
        sums[3] += fold(low.astype(jnp.float32))

    def back_middle_tap(m, piece=None):
        block = slice(0, positions) if piece is None else slice(piece[0], piece[0] + piece[1])
        return dot_nt(grad2[m, block], w_conv[KERNEL // 2])

    def back_rear(m, piece, grad, between=None):
        block = slice(piece[0], piece[0] + piece[1])
        for k in range(KERNEL):
            if k != KERNEL // 2:
                grad = grad + dot_nt(back_taps[k - (k > KERNEL // 2), block], w_conv[KERNEL - 1 - k])
        if between is not None:
            between()
        low = act_backward(
            grad, hat2[m, block], slope2[m, block], masks[m, block, 9:10], second_gain[...], sums.at[1], sums.at[2]
        ).astype(jnp.bfloat16)
        grad1[m, block] = low
        sums[0] += fold(low.astype(jnp.float32))

    def back_last(m, piece):
        block = slice(piece[0], piece[0] + piece[1])
        grad = dot_nt(grad1[m, block], w_in[...])
        grad = act_backward(
            grad, hat1[m, block], slope1[m, block], masks[m, block, 8:9], first_gain[...],
            sums_wide.at[0], sums_wide.at[1])
        hat1[m, block] = (buf[rows + m, block].astype(jnp.float32) + grad).astype(jnp.bfloat16)

    def give(source, m):
        return pltpu.make_async_copy(source.at[m], result.at[0, m], result_sem.at[m])

    wide = buf.shape[2] // hidden

    def add_block(start, value):
        total[pl.ds(start, hidden)] += value

    def weights_out(m):
        for j in range(wide):
            add_block((KERNEL + j) * hidden, dot_tn(act3[m], buf[rows + m, :, j * hidden : (j + 1) * hidden]))

    def weights_conv(m):
        for k in range(KERNEL):
            add_block(k * hidden, dot_tn(taps[tap_rows(m, k)], grad2[m]))

    def weights_in(m):
        for j in range(wide):
            add_block(rings[1].base + j * hidden, dot_tn(act1[m, :, j * hidden : (j + 1) * hidden], grad1[m]))

    def first_lane():
        rings[0].exchange(2)
        rings[0].towards(0, 0, True)

    def other_lanes():
        for lane in range(1, rings[0].lanes):
            rings[0].towards(0, lane, True)

    def step(i, carry):
        fronts = i < rows
        m_start = jnp.where(leading, i - rows, i)
        m_end = m_start - 1
        m_sum = jnp.where(leading, i - rows, i - rows + 1)
        final = m_sum == rows

        def on(m):
            return (m >= 0) & (m < rows)

        @pl.when(fronts)
        def _():
            make_mask(i)

        @pl.when(i == 0)
        def _():
            weight_loads[0].wait()
            for copy in weight_loads[1:]:
                copy.start()
            for copy in input_loads:
                copy.wait()

        @pl.when(leading & fronts)
        def _():
            load(i).wait()

        @pl.when(leading & fronts)
        def _():
            front(i, whole[0])

        @pl.when(i == 0)
        def _():
            weight_loads[1].wait()
            weight_loads[2].wait()
            for m in range(1, rows):
                load(m).start()

        @pl.when(leading & fronts)
        def _():
            gather_near(0, i, taps[tap_rows(i, KERNEL // 2)], store_tap(i), False)
            rear(i, thirds[0], middle_tap(i, thirds[0]))

        @pl.when(i == 0)
        def _():
            pl.semaphore_wait(barrier, greeted)

        @pl.when(leading & fronts)
        def _():
            begin(near_copies(0, i))
            hand(buf, i, 0).start()
            end(near_copies(0, i))
            gather_near(0, i, taps[tap_rows(i, KERNEL // 2)], store_tap(i), True)
            for part in (1, 2):
                rear(i, thirds[part], middle_tap(i, thirds[part]))
                hand(buf, i, part).start()

        @pl.when(trailing & fronts)
        def _():
            for part in range(3):
                hand(buf, i, part).wait_recv()
                front(i, thirds[part])
                begin(far_copies(0, i, part, thirds))

        @pl.when(leading & on(m_end))
        def _():
            grad = back_middle_tap(m_end)
            gather_near(1, m_end, grad2[m_end], store_back, False)
            end(near_copies(1, m_end))
            gather_near(1, m_end, grad2[m_end], store_back, True)
            back_rear(m_end, whole[0], grad, lambda: pl.when(final)(first_lane))
            back_last(m_end, whole[0])
            give(hat1, m_end).start()
            pl.when(final)(other_lanes)

        @pl.when(trailing & on(m_end))
        def _():
            grads = [back_middle_tap(m_end, piece) for piece in parts]
            for part in range(2):
                end(far_copies(1, m_end, part, parts))
            gather_far(1, m_end, grad2[m_end], store_back)
            for part in range(2):
                back_rear(m_end, parts[part], grads[part])
                back_last(m_end, parts[part])
                hand(hat1, m_end, part).start()

        @pl.when(trailing & final)
        def _():
            first_lane()
            other_lanes()

        @pl.when(on(m_sum - 1))
        def _():
            weights_in(m_sum - 1)

        @pl.when(final)
        def _():
            rings[0].towards(1, 0)
            rings[0].exchange(3)
            rings[1].exchange(0)
            rings[1].exchange(1)

        @pl.when((leading & (i == 2)) | (trailing & (i == 0)))
        def _():
            total[...] = jnp.zeros_like(total)
            sums_wide[...] = jnp.zeros_like(sums_wide)
            sums[...] = jnp.zeros_like(sums)
            hits[...] = jnp.zeros_like(hits)
            tally[...] = jnp.zeros_like(tally)

        @pl.when(trailing & fronts)
        def _():
            pre = middle_tap(i, whole[0])

            for part in range(3):
                end(far_copies(0, i, part, thirds))
            gather_far(0, i, taps[tap_rows(i, KERNEL // 2)], store_tap(i))
            rear(i, whole[0], pre)
            give(buf, i).start()

        @pl.when(on(m_start))
        def _():
            pl.when(trailing)(load(m_start).wait)
            for part in range(2):
                pl.when(leading)(hand(hat1, m_start, part).wait_recv)
                back_front(m_start, parts[part])

                @pl.when(trailing)
                def _():
                    begin(far_copies(1, m_start, part, parts))

            @pl.when(leading)
            def _():
                begin(near_copies(1, m_start))

        @pl.when(trailing & fronts)
        def _():
            count_types(i)

        @pl.when(on(m_sum))
        def _():
            weights_out(m_sum)
            weights_conv(m_sum)

        @pl.when(m_sum == last)
        def _():
            rings[0].exchange(0)
            rings[0].exchange(1)

        return carry

    lax.fori_loop(0, 2 * rows + 1, step, 0)

    def fill_small():
        for i in range(3):
            small[i : i + 1, :] = jnp.sum(sums_wide[i], axis=0, keepdims=True)
        for i in range(6):
            small[3 + i // 2 : 4 + i // 2, (i % 2) * hidden : (i % 2 + 1) * hidden] = jnp.sum(sums[i], axis=0, keepdims=True)
        small[6:8, :] = jnp.zeros((2, small.shape[1]), jnp.float32)
        ones = jnp.ones((8, positions), jnp.float32)
        for i, counted in ((6, hits), (7, tally)):
            row = lax.dot_general(
                ones, counted[...], (((1,), (1,)), ((), ())), precision=lax.Precision.HIGHEST,
                preferred_element_type=jnp.float32)
            small[i : i + 1, 0 : counted.shape[0]] = row[0:1]

    run_rings(rings, fill_small, SmallSum(rings[0], small, small_land, small_out, small_send, small_recv, partner()))
    for m in range(rows):
        @pl.when(leading)
        def _():
            for part in range(3):
                hand(buf, m, part).wait_send()
            give(hat1, m).wait()

        @pl.when(trailing)
        def _():
            for part in range(2):
                hand(hat1, m, part).wait_send()
            give(buf, m).wait()


def ring_plan(width, hidden, nodes):
    plan, base, land = [], 0, 0
    for rows, subs in (((KERNEL + width // hidden) * hidden, LANES), (width, 1)):
        sizes = ring_sizes(rows // 2, nodes, subs)
        plan.append((sizes, base, land))
        land += nodes * sum(map(sum, sizes))
        base = 2 * land
    return plan, land


def run_blocks(args, ny, nz, cid=0):
    nodes = ny * nz
    doublings = 1 + (ny - 1).bit_length() + (nz - 1).bit_length()
    boundary, in_weight, conv_weight = args[0], args[7], args[11]
    _, rows, positions, width = boundary.shape
    hidden = in_weight.shape[2]
    edge = KERNEL // 2 * DILATION_STEP
    assert edge % positions == 0 and positions % 32 == 0 and width % hidden == 0
    reach = edge // positions
    low, full = jnp.bfloat16, jnp.float32
    wide_rows = pltpu.VMEM((rows, positions, width), low)
    thin_rows = pltpu.VMEM((rows, positions, hidden), low)
    plan, half = ring_plan(width, hidden, nodes)
    where = [pltpu.HBM, pltpu.SMEM] + [pltpu.HBM] * 15
    smalls = [pltpu.VMEM(args[i].shape, args[i].dtype) for i in (2, 3, 4, 5, 6, 8, 9, 10, 12, 13, 14, 16)]
    return pl.pallas_call(
        functools.partial(blocks_kernel, edge, plan),
        out_shape=(
            jax.ShapeDtypeStruct(boundary.shape, low),
            jax.ShapeDtypeStruct((2 * half, hidden), low),
            jax.ShapeDtypeStruct((16, width), full),
        ),
        in_specs=[pl.BlockSpec(memory_space=space) for space in where],
        out_specs=[pl.BlockSpec(memory_space=space) for space in (pltpu.HBM, pltpu.HBM, pltpu.VMEM)],
        scratch_shapes=smalls + [
            pltpu.VMEM((2 * rows, positions, width), low),
            pltpu.VMEM((width, hidden), low),
            pltpu.VMEM((KERNEL, hidden, hidden), low),
            pltpu.VMEM((hidden, width), low),
            pltpu.VMEM((2 * half, hidden), full),
            wide_rows, wide_rows, wide_rows,
            pltpu.VMEM((max(rows * KERNEL * positions, half), hidden), low),
            pltpu.VMEM((KERNEL - 1, positions, hidden), low),
            thin_rows, thin_rows, thin_rows, thin_rows, thin_rows,
            pltpu.VMEM((4, edge, hidden), low),
            pltpu.VMEM((4, edge, hidden), low),
            pltpu.VMEM((positions + 32, hidden), full),
            pltpu.VMEM((rows, positions, 128), full),
            pltpu.VMEM((3, 8, width), full),
            pltpu.VMEM((6, 8, hidden), full),
            pltpu.VMEM((VOCAB, positions), full),
            pltpu.VMEM((VOCAB, positions), full),
            pltpu.VMEM((half, hidden), low),
            pltpu.VMEM((8, width), full),
            pltpu.VMEM((2 * doublings, 8, width), full),
            pltpu.SemaphoreType.DMA((rows,)),
            pltpu.SemaphoreType.DMA((3,)),
            pltpu.SemaphoreType.DMA((rows,)),
            pltpu.SemaphoreType.DMA((rows, 3)),
            pltpu.SemaphoreType.DMA((rows, 3)),
            pltpu.SemaphoreType.DMA((2 * rows, 6 * reach)),
            pltpu.SemaphoreType.DMA((2 * rows, 6 * reach)),
            pltpu.SemaphoreType.DMA((doublings + 1,)),
            pltpu.SemaphoreType.DMA((doublings + 1,)),
            pltpu.SemaphoreType.DMA((len(smalls),)),
        ]
        + [scratch for sizes, _, _ in plan for scratch in ring_scratch(sizes, nodes, hidden)],
        compiler_params=pltpu.CompilerParams(
            collective_id=cid, has_side_effects=True, vmem_limit_bytes=VMEM_BYTES),
    )(*args)


def ring_sizes(rows, nodes, subs):
    units = -(-rows // (nodes * 16))
    long = -(-units // 2)
    return [[16 * ((way + i) // subs) for i in range(subs)] for way in (long, units - long)]


def ring_flows(sizes):
    return [(way, i) for i in range(len(sizes[0])) for way in range(2) if sizes[way][i]]


def ring_scratch(sizes, nodes, columns):
    flows = ring_flows(sizes)
    n = len(flows)
    counts = [(n, nodes)] * 2 + [(n, 2 * nodes - 2)] * 2 + [(n, nodes)] * 2 + [(n,)]
    return [pltpu.SemaphoreType.DMA(count) for count in counts] + [
        pltpu.VMEM((nodes - 1, sizes[way][i], columns), jnp.bfloat16) for way, i in flows]


class Ring:
    def __init__(self, sizes, base, land, section, seq, dp, ny, nz):
        self.sizes, self.base, self.land, self.nodes = sizes, base, land, ny * nz
        self.flows = ring_flows(sizes)
        self.refs = 7 + len(self.flows)
        self.lanes = len(sizes[0])
        self.section, self.nz = section, nz
        self.core, ypos = seq % 2, seq // 2
        self.spot = ypos * nz + dp + (ypos % 2) * (nz - 1 - 2 * dp)
        self.other_core = (section, seq + 1 - 2 * self.core, dp)
        self.turn = [1 - 2 * self.core, 2 * self.core - 1]
        self.next = [self.at_spot(self.wrap(self.spot + self.nodes + turn)) for turn in self.turn]
        self.half = sum(map(sum, sizes)) * self.nodes
        self.first, at = {}, 0
        for way, i in self.flows:
            self.first[way, i] = at
            at += sizes[way][i] * self.nodes
        self.peers = [self.other_core]
        reach = 1
        while reach < ny:
            self.peers.append((section, seq + 2 * reach - 4 * reach * ((ypos // reach) % 2), dp))
            reach *= 2
        reach = 1
        while reach < nz:
            self.peers.append((section, seq, dp + reach - 2 * reach * ((dp // reach) % 2)))
            reach *= 2

    def wrap(self, place):
        if self.nodes & (self.nodes - 1) == 0:
            return place & (self.nodes - 1)
        return lax.rem(place, self.nodes)

    def at_spot(self, place):
        y = place // self.nz
        z = place % self.nz
        return (self.section, y * 2 + self.core, z + (y % 2) * (self.nz - 1 - 2 * z))

    def neighbours(self):
        around = self.next
        return self.peers + around

    def bind(self, total, stage, core_land, big, refs):
        self.total, self.stage, self.core_land, self.big = total, stage, core_land, big
        self.core_sems, self.ring_sems, self.over_sems = refs[0:2], refs[2:4], refs[4:6]
        self.keep_sem, self.lands = refs[6], refs[7:]

    def count(self, f):
        way, i = self.flows[f]
        return self.sizes[way][i]

    def rows(self, f, side, shard):
        start = self.base + side * self.half + self.first[self.flows[f]] + shard * self.count(f)
        return pl.ds(pl.multiple_of(start, 16), self.count(f))

    def land_rows(self, f, shard):
        start = self.land + self.first[self.flows[f]] + shard * self.count(f)
        return pl.ds(pl.multiple_of(start, 16), self.count(f))

    def shard(self, f, step):
        return self.wrap(self.spot + 2 * self.nodes - self.turn[self.flows[f][0]] * step)

    def ahead(self, f):
        return self.next[self.flows[f][0]]

    def remote(self, source, target, sems, index, peer):
        return pltpu.make_async_remote_copy(
            src_ref=source, dst_ref=target, send_sem=sems[0].at[index], recv_sem=sems[1].at[index],
            device_id=peer, device_id_type=MESH)

    def core_copy(self, f, shard):
        rows = self.land_rows(f, shard)
        return self.remote(self.stage.at[rows], self.core_land.at[rows], self.core_sems, (f, shard), self.other_core)

    def ring_copy(self, f, step, shard):
        return self.remote(
            self.core_land.at[self.land_rows(f, shard)], self.lands[f].at[step], self.ring_sems, (f, step), self.ahead(f))

    def back_copy(self, f, step, shard):
        block = self.big.at[self.rows(f, self.core, shard)]
        return self.remote(
            self.core_land.at[self.land_rows(f, shard)] if step is None else block, block,
            self.ring_sems, (f, self.nodes - 1 + (0 if step is None else step)), self.ahead(f))

    def over_copy(self, f, shard, own=False):
        block = self.big.at[self.rows(f, self.core, shard)]
        return self.remote(
            self.core_land.at[self.land_rows(f, shard)] if own else block, block,
            self.over_sems, (f, shard), self.other_core)

    def keep_copy(self, f, shard):
        return pltpu.make_async_copy(
            self.core_land.at[self.land_rows(f, shard)], self.big.at[self.rows(f, self.core, shard)], self.keep_sem.at[f])

    def add(self, f, shard, step):
        rows = self.land_rows(f, shard)
        value = self.total[self.rows(f, self.core, shard)] + self.core_land[rows].astype(jnp.float32)
        if step is not None:
            value = value + self.lands[f][step].astype(jnp.float32)
        self.core_land[rows] = value.astype(jnp.bfloat16)

    def exchange(self, step):
        for f in range(len(self.flows)):
            shard = self.shard(f, -step)
            self.stage[self.land_rows(f, shard)] = self.total[self.rows(f, 1 - self.core, shard)].astype(jnp.bfloat16)
            self.core_copy(f, shard).start()

    def of(self, lane):
        return [f for f in range(len(self.flows)) if lane is None or self.flows[f][1] == lane]

    def towards(self, step, lane=None, first=False):
        for f in self.of(lane):
            shard = self.shard(f, step)
            self.core_copy(f, shard).wait_recv()
            if first:
                self.add(f, shard, None)
            else:
                self.ring_copy(f, step - 1, shard).wait_recv()
                self.add(f, shard, step - 1)
            self.ring_copy(f, step, shard).start()

    def back(self, step, lane=None):
        for f in self.of(lane):
            shard = self.shard(f, self.nodes - 1 + step)
            self.back_copy(f, step - 1, shard).wait_recv()
            self.back_copy(f, step, shard).start()
            self.over_copy(f, shard).start()

    def own(self, lane=None):
        for f in self.of(lane):
            shard = self.shard(f, self.nodes - 1)
            self.core_copy(f, shard).wait_recv()
            self.ring_copy(f, self.nodes - 2, shard).wait_recv()
            self.add(f, shard, self.nodes - 2)
            self.back_copy(f, None, shard).start()
            self.over_copy(f, shard, True).start()
            self.keep_copy(f, shard).start()

    def arrive(self, lane=None):
        for f in self.of(lane):
            shard = self.shard(f, 2 * self.nodes - 2)
            self.back_copy(f, self.nodes - 2, shard).wait_recv()
            self.over_copy(f, shard).start()

    def settle(self):
        def crossed(step, carry):
            for f in range(len(self.flows)):
                self.core_copy(f, step).wait_send()
                self.over_copy(f, step).wait()
            return carry

        def rounded(step, carry):
            for f in range(len(self.flows)):
                self.ring_copy(f, step, 0).wait_send()
                self.back_copy(f, step, 0).wait_send()
            return carry

        lax.fori_loop(0, self.nodes, crossed, 0)
        lax.fori_loop(0, self.nodes - 1, rounded, 0)
        for f in range(len(self.flows)):
            self.keep_copy(f, 0).wait()


def run_rings(rings, fill_small, small_sum):
    ahead, behind = rings
    nodes, lanes = ahead.nodes, ahead.lanes

    def each(method, *step):
        getattr(ahead, method)(*step, 0)
        getattr(behind, method)(*step)
        for lane in range(1, lanes):
            getattr(ahead, method)(*step, lane)

    for lane in range(1, lanes):
        ahead.towards(1, lane)
    for step in (2, 3):
        ahead.exchange(step + 2)
        behind.exchange(2 * step - 2)
        behind.exchange(2 * step - 1)
        ahead.towards(step, 0)
        behind.towards(2 * step - 4, first=step == 2)
        for lane in range(1, lanes):
            ahead.towards(step, lane)
        behind.towards(2 * step - 3)

    fill_small()
    small_sum.step(0)

    def towards(step, carry):
        ahead.exchange(step + 2)
        behind.exchange(step + 2)
        each("towards", step)
        return carry

    lax.fori_loop(4, nodes - 2, towards, 0)
    each("towards", nodes - 2)
    each("own")
    small_sum.step(1)
    at = 1
    for k in range(2, small_sum.steps):
        if at < nodes - 1:
            each("back", at)
            at += 1
        small_sum.step(k)

    def back(step, carry):
        each("back", step)
        return carry

    lax.fori_loop(at, nodes - 1, back, 0)
    each("arrive")
    ahead.settle()
    behind.settle()
    small_sum.settle()


class SmallSum:
    def __init__(self, ring, small, land, out, send_sem, recv_sem, other_section):
        self.peers, self.small, self.land, self.out = ring.peers + [other_section], small, land, out
        self.sems = (send_sem, recv_sem)
        self.remote = ring.remote
        self.steps = len(self.peers) + 1

    def held(self, k):
        return self.small if k == 0 else self.land.at[2 * k - 1]

    def copy(self, k):
        count = self.small.shape[0]
        target = self.out.at[pl.ds(count, count)] if k == len(self.peers) - 1 else self.land.at[2 * k]
        return self.remote(self.held(k), target, self.sems, k, self.peers[k])

    def step(self, k):
        last = len(self.peers) - 1
        if 0 < k:
            self.copy(k - 1).wait_recv()
        if 0 < k <= last:
            self.land[2 * k - 1] = self.held(k - 1)[...] + self.land[2 * k - 2]
        if k <= last:
            self.copy(k).start()
        if k == last:
            self.out[pl.ds(0, self.small.shape[0])] = self.held(k)[...]

    def settle(self):
        for k in range(len(self.peers)):
            self.copy(k).wait_send()


def finish_kernel(
    base, given, big, small_in, result, grad_in, grad_conv, grad_out, first_gain, first_shift, in_bias, second_gain,
    second_shift, conv_bias, third_gain, third_shift, out_bias, scores, counts,
    small, passed, held, wide, rate, count, pass_sem, load_sem, store_sem, small_sem,
):
    hidden = held.shape[2]
    blocks = held.shape[0]
    ends = grad_in.shape[1] // hidden
    small_load = pltpu.make_async_copy(small_in, small, pass_sem.at[0])
    first = pltpu.make_async_copy(given, passed, pass_sem.at[1])
    second = pltpu.make_async_copy(passed, result, pass_sem.at[2])

    def load(b):
        start = b * hidden if b < blocks - ends else base + (b - blocks + ends) * hidden
        return pltpu.make_async_copy(big.at[pl.ds(start, hidden)], held.at[b], load_sem.at[b])

    def store(b):
        if b < KERNEL:
            target = grad_conv.at[0, b]
        elif b < blocks - ends:
            target = grad_out.at[0, :, pl.ds((b - KERNEL) * hidden, hidden)]
        else:
            target = grad_in.at[0, pl.ds((b - blocks + ends) * hidden, hidden)]
        return pltpu.make_async_copy(wide.at[b], target, store_sem.at[b])

    load(0).start()
    small_load.start()
    for b in range(1, blocks):
        load(b).start()
    first.start()
    for b in range(blocks):
        load(b).wait()
        wide[b] = held[b].astype(jnp.float32)
        store(b).start()
        if b == 0:
            small_load.wait()
            hits = small[6:7, 0:VOCAB] + small[14:15, 0:VOCAB]
            tally = small[7:8, 0:VOCAB] + small[15:16, 0:VOCAB]
            rate[...] = hits / jnp.maximum(tally, 1.0)
            count[...] = tally.astype(jnp.int32)
            pieces = [(small.at[pl.ds(i, 1)], ref) for i, ref in enumerate((first_gain, first_shift, out_bias))]
            thin = (in_bias, second_gain, second_shift, conv_bias, third_gain, third_shift)
            for i, ref in enumerate(thin):
                pieces.append((small.at[pl.ds(3 + i // 2, 1), pl.ds(i % 2 * hidden, hidden)], ref))
            pieces += [(rate, scores), (count, counts)]
            small_stores = [
                pltpu.make_async_copy(source, target, small_sem.at[i]) for i, (source, target) in enumerate(pieces)
            ]
            for copy in small_stores:
                copy.start()
    first.wait()
    second.start()
    for b in range(blocks):
        store(b).wait()
    for copy in small_stores:
        copy.wait()
    second.wait()


def finish(given, big, small, width, base):
    hidden = big.shape[1]
    blocks = 2 * width // hidden + KERNEL
    full = jnp.float32
    shapes = [(1, width, hidden), (1, KERNEL, hidden, hidden), (1, hidden, width), (1, width), (1, width)]
    shapes += [(1, hidden)] * 6 + [(1, width), (1, VOCAB)]
    out = [jax.ShapeDtypeStruct(given.shape, given.dtype)]
    out += [jax.ShapeDtypeStruct(shape, full) for shape in shapes] + [jax.ShapeDtypeStruct((1, VOCAB), jnp.int32)]
    return pl.pallas_call(
        functools.partial(finish_kernel, base),
        out_shape=out,
        in_specs=[pl.BlockSpec(memory_space=pltpu.HBM)] * 3,
        out_specs=[pl.BlockSpec(memory_space=pltpu.HBM)] * len(out),
        scratch_shapes=[
            pltpu.VMEM(small.shape, full),
            pltpu.VMEM(given.shape, given.dtype),
            pltpu.VMEM((blocks, hidden, hidden), big.dtype),
            pltpu.VMEM((blocks, hidden, hidden), full),
            pltpu.VMEM((1, VOCAB), full),
            pltpu.VMEM((1, VOCAB), jnp.int32),
            pltpu.SemaphoreType.DMA((3,)),
            pltpu.SemaphoreType.DMA((blocks,)),
            pltpu.SemaphoreType.DMA((blocks,)),
            pltpu.SemaphoreType.DMA((11,)),
        ],
        compiler_params=pltpu.CompilerParams(vmem_limit_bytes=VMEM_BYTES),
    )(given, big, small)


def shards(
    boundary, lengths, masked, residues, readout,
    first_gain, first_shift, in_weight, in_bias, second_gain, second_shift, conv_weight, conv_bias,
    third_gain, third_shift, out_weight, out_bias,
):
    ny, nz = lax.axis_size("seq") // 2, lax.axis_size("dp")
    width, hidden = in_weight.shape[1], in_weight.shape[2]
    given, big, small = run_blocks(
        (
            boundary, lengths, masked, residues, readout.T,
            first_gain, first_shift, in_weight, in_bias, second_gain, second_shift, conv_weight, conv_bias,
            third_gain, third_shift, out_weight, out_bias,
        ),
        ny,
        nz,
    )
    (
        boundary_out, grad_in_weight, grad_conv_weight, grad_out_weight, grad_first_gain, grad_first_shift, grad_in_bias,
        grad_second_gain, grad_second_shift, grad_conv_bias, grad_third_gain, grad_third_shift, grad_out_bias,
        scores, counts,
    ) = finish(given, big, small, width, ring_plan(width, hidden, ny * nz)[0][1][1])
    return (
        boundary_out,
        grad_first_gain,
        grad_first_shift,
        grad_in_weight,
        grad_in_bias,
        grad_second_gain,
        grad_second_shift,
        grad_conv_weight,
        grad_conv_bias,
        grad_third_gain,
        grad_third_shift,
        grad_out_weight,
        grad_out_bias,
        scores[0],
        counts[0],
    )


def solution(mesh):
    in_specs = (
        P("section", "dp", "seq", None),
        P("dp", None),
        P("dp", "seq"),
        P("dp", "seq"),
        P(),
        P("section", None),
        P("section", None),
        P("section", None, None),
        P("section", None),
        P("section", None),
        P("section", None),
        P("section", None, None, None),
        P("section", None),
        P("section", None),
        P("section", None),
        P("section", None, None),
        P("section", None),
    )
    out_specs = (
        P("section", "dp", "seq", None),
        P("section", None),
        P("section", None),
        P("section", None, None),
        P("section", None),
        P("section", None),
        P("section", None),
        P("section", None, None, None),
        P("section", None),
        P("section", None),
        P("section", None),
        P("section", None, None),
        P("section", None),
        P(),
        P(),
    )
    return jax.shard_map(shards, mesh=mesh, in_specs=in_specs, out_specs=out_specs, check_vma=False)
```

```python
import functools

import jax
import jax.numpy as jnp
from jax import lax
from jax.experimental import pallas as pl
from jax.experimental.pallas import tpu as pltpu
from jax.sharding import PartitionSpec as P

KERNEL = 5
VOCAB = 30
DILATION_STEP = 128
ITEMS = 4
EPSILON = 1e-05
ROOT_HALF = 0.7071067811865476
HALF_LOG = -0.7213475204444817
ROOT_TAU = 0.3989422804014327

MESH = pl.DeviceIdType.MESH
LANES = 2
VMEM_BYTES = 64 << 20


def far_rows(left, own, right, offset):
    edge, positions = left.shape[0], own.shape[0]
    first, last = offset + edge, offset + edge + positions
    pieces, at = [], 0
    for block in (left, own, right):
        lo, hi = max(first, at), min(last, at + block.shape[0])
        if lo < hi:
            pieces.append(block[lo - at : hi - at])
        at += block.shape[0]
    return pieces[0] if len(pieces) == 1 else jnp.concatenate(pieces, axis=0)


def act_forward(values, gain, shift, real):
    scale = 1.0 / values.shape[1]
    centred = values - jnp.sum(values, axis=1, keepdims=True) * scale
    spread = jnp.sum(centred * centred, axis=1, keepdims=True) * scale
    inverse = lax.rsqrt(spread + EPSILON)
    hat = centred * inverse
    moved = hat * gain + shift
    below = (0.5 + 0.5 * lax.erf(moved * ROOT_HALF)) * real
    density = jnp.exp2(moved * moved * HALF_LOG) * (ROOT_TAU * real)
    return moved * below, hat, below + moved * density, inverse


def fold(values):
    rows, columns = values.shape
    return jnp.sum(values.reshape(rows // 8, 8, columns), axis=0)


def act_backward(grad, hat, slope, inverse, gain, gain_sum, shift_sum):
    scale = 1.0 / grad.shape[1]
    hat = hat.astype(jnp.float32)
    moved = grad * slope.astype(jnp.float32)
    turned = moved * hat
    shift_sum[...] += fold(moved)
    gain_sum[...] += fold(turned)
    mean = jnp.sum(moved * gain, axis=1, keepdims=True) * scale
    tilt = jnp.sum(turned * gain, axis=1, keepdims=True) * scale
    return inverse * (moved * gain - mean - hat * tilt)


def dot_nn(a, b):
    return jnp.dot(a, b, preferred_element_type=jnp.float32)


def dot_nt(a, b):
    return lax.dot_general(a, b, (((1,), (1,)), ((), ())), preferred_element_type=jnp.float32)


def dot_tn(a, b):
    return lax.dot_general(a, b, (((0,), (0,)), ((), ())), preferred_element_type=jnp.float32)


def blocks_kernel(
    edge, plan,
    boundary, lengths, masked_in, residues_in, readout_in,
    first_gain_in, first_shift_in, in_weight, in_bias_in, second_gain_in, second_shift_in, conv_weight, conv_bias_in,
    third_gain_in, third_shift_in, out_weight, out_bias_in,
    result, big, small_out,
    masked, residues, readout, first_gain, first_shift, in_bias, second_gain, second_shift, conv_bias,
    third_gain, third_shift, out_bias,
    buf, w_in, w_conv, w_out, total, hat1, slope1, act1, taps, back_taps,
    hat2, slope2, hat3, slope3, act3, rim_left, rim_right, near, masks,
    sums_wide, sums, hits, tally, core_land, small, small_land,
    load_sem, weight_sem, result_sem, hand_send, hand_recv, rim_send, rim_recv, small_send, small_recv, input_sem,
    low_land, far_gain, far_shift, gift_send, gift_recv, *ring_refs,
):
    grad1, grad2 = hat2, hat3
    section = lax.axis_index("section")
    seq = lax.axis_index("seq")
    dp = lax.axis_index("dp")
    n_seq = lax.axis_size("seq")
    rows, positions = buf.shape[0] // 2, buf.shape[1]
    hidden = w_in.shape[1]
    leading = section == 0
    trailing = section == 1
    row_len = n_seq * positions
    first_position = seq * positions
    reach = edge // positions
    dilation = jnp.where(leading, 1, DILATION_STEP)

    def load(m):
        return pltpu.make_async_copy(boundary.at[0, m], buf.at[section * rows + m], load_sem.at[m])

    weight_loads = [
        pltpu.make_async_copy(source.at[0], target, weight_sem.at[i])
        for i, (source, target) in enumerate(((in_weight, w_in), (conv_weight, w_conv), (out_weight, w_out)))
    ]
    input_loads = [
        pltpu.make_async_copy(source, target, input_sem.at[i])
        for i, (source, target) in enumerate((
            (first_gain_in, first_gain), (first_shift_in, first_shift), (in_bias_in, in_bias),
            (second_gain_in, second_gain), (second_shift_in, second_shift), (conv_bias_in, conv_bias),
            (third_gain_in, third_gain), (third_shift_in, third_shift), (out_bias_in, out_bias),
            (masked_in, masked), (residues_in, residues), (readout_in, readout),
        ))
    ]
    load(0).start()
    weight_loads[0].start()
    for copy in input_loads:
        copy.start()

    def partner():
        return (1 - section, seq, dp)

    rings, at = [], 0
    for sizes, base, land in plan:
        ring = Ring(sizes, base, land, section, seq, dp, n_seq // 2, lax.axis_size("dp"))
        ring.bind(total, taps, core_land, big, ring_refs[at : at + ring.refs])
        at += ring.refs
        rings.append(ring)
    barrier = pltpu.get_barrier_semaphore()
    greet = [partner()] + rings[0].neighbours()
    for peer in greet:
        pl.semaphore_signal(barrier, inc=1, device_id=peer, device_id_type=MESH)
    greeted = len(greet)
    for j in range(1, reach + 1):
        for side in (-j, j):
            on = (seq + side >= 0) & (seq + side < n_seq)
            greeted = greeted + on.astype(jnp.int32)

            @pl.when(on)
            def _():
                pl.semaphore_signal(barrier, inc=1, device_id=(section, seq + side, dp), device_id_type=MESH)

    @pl.when(seq < reach)
    def _():
        rim_left[...] = jnp.zeros_like(rim_left)

    @pl.when(seq >= n_seq - reach)
    def _():
        rim_right[...] = jnp.zeros_like(rim_right)

    last = rows - 1
    half, quarter = positions // 2, positions // 4
    parts = ((0, half), (half, half))
    thirds = ((quarter, half), (0, quarter), (half + quarter, quarter))
    whole = ((0, positions),)

    def make_mask(m):
        lane = lax.broadcasted_iota(jnp.int32, (positions, 128), 1)
        place = lax.broadcasted_iota(jnp.int32, (positions, 128), 0) + first_position
        other = place + (lane - KERNEL // 2) * dilation
        end = 0
        here = jnp.zeros((positions, 128), jnp.int32)
        there = jnp.zeros((positions, 128), jnp.int32)
        for j in range(ITEMS):
            end = end + lengths[m, j]
            here = here + (place >= end).astype(jnp.int32)
            there = there + (other >= end).astype(jnp.int32)
        counts = (here == there) & (here < ITEMS) & (other >= 0) & (other < row_len)
        masks[m] = counts.astype(jnp.float32)

    def hand(source, m, part):
        first, count = (thirds if source is buf else parts)[part]
        block = pl.ds(first, count)
        target = buf.at[m, block] if source is buf else buf.at[rows + m, block]
        return pltpu.make_async_remote_copy(
            src_ref=source.at[m, block], dst_ref=target,
            send_sem=hand_send.at[m, part], recv_sem=hand_recv.at[m, part],
            device_id=partner(), device_id_type=MESH)

    def low_hand(part):
        block = pl.ds(*parts[part])
        return pltpu.make_async_remote_copy(
            src_ref=grad1.at[last, block], dst_ref=low_land.at[block],
            send_sem=hand_send.at[last, part], recv_sem=hand_recv.at[last, part],
            device_id=partner(), device_id_type=MESH)

    core = seq % 2
    wide_half = buf.shape[2] // 2
    own_half = pl.ds(pl.multiple_of(core * wide_half, 16), wide_half)
    other_half = pl.ds(pl.multiple_of((1 - core) * wide_half, 16), wide_half)

    def gift(i):
        source, target = (
            (w_in.at[own_half], core_land.at[own_half]),
            (buf.at[rows + last], buf.at[rows + last]),
            (first_gain, far_gain),
            (first_shift, far_shift),
        )[i]
        return pltpu.make_async_remote_copy(
            src_ref=source, dst_ref=target, send_sem=gift_send.at[i], recv_sem=gift_recv.at[i],
            device_id=partner(), device_id_type=MESH)

    def pass_on(half):
        return pltpu.make_async_remote_copy(
            src_ref=core_land.at[half], dst_ref=core_land.at[half],
            send_sem=gift_send.at[4], recv_sem=gift_recv.at[4],
            device_id=(section, seq + 1 - 2 * core, dp), device_id_type=MESH)

    def far_norm():
        for m in (1, 2):
            for part in range(3):
                hand(buf, m, part).wait_send()
        for first, count in parts:
            block = slice(first, first + count)
            real = masks[last, block, KERNEL // 2 : KERNEL // 2 + 1]
            _, hat, slope, inverse = act_forward(
                buf[last, block].astype(jnp.float32), far_gain[...], far_shift[...], real)
            buf[1, block] = hat.astype(jnp.bfloat16)
            buf[2, block] = slope.astype(jnp.bfloat16)
            masks[last, block, 11:12] = inverse

    def far_last(piece):
        block = slice(piece[0], piece[0] + piece[1])
        scale = 1.0 / buf.shape[2]
        hat = buf[1, block].astype(jnp.float32)
        grad = dot_nt(low_land[block], core_land[0 : 2 * wide_half]) * buf[2, block].astype(jnp.float32) * far_gain[...]
        mean = jnp.sum(grad, axis=1, keepdims=True) * scale
        tilt = jnp.sum(grad * hat, axis=1, keepdims=True) * scale
        grad = masks[last, block, 11:12] * (grad - mean - hat * tilt)
        buf[rows + last, block] = (buf[rows + last, block].astype(jnp.float32) + grad).astype(jnp.bfloat16)

    def tap_rows(m, k, first=0, count=None):
        start = (m * KERNEL + k) * positions + first
        return pl.ds(pl.multiple_of(start, 16), positions if count is None else count)

    def near_copies(backward, m):
        slot = 2 * backward + m % 2
        turn = backward * rows + m

        def edge_rows(first):
            return grad2.at[m, pl.ds(first, 16)] if backward else taps.at[tap_rows(m, KERNEL // 2, first, 16)]

        def copy(source, target, index, to):
            return pltpu.make_async_remote_copy(
                src_ref=source, dst_ref=target, send_sem=rim_send.at[turn, index], recv_sem=rim_recv.at[turn, index],
                device_id=(section, to, dp), device_id_type=MESH)

        return [
            (seq + 1 < n_seq, seq >= 1,
             copy(edge_rows(positions - 16), rim_left.at[slot, pl.ds(edge - 16, 16)], 0, seq + 1)),
            (seq >= 1, seq + 1 < n_seq,
             copy(edge_rows(0), rim_right.at[slot, pl.ds(0, 16)], 1, seq - 1)),
        ]

    def far_copies(backward, m, part, pieces):
        first, count = pieces[part]
        slot = 2 * backward + m % 2
        turn = backward * rows + m
        own = grad2.at[m, pl.ds(first, count)] if backward else taps.at[tap_rows(m, KERNEL // 2, first, count)]

        def copy(target, index, to):
            return pltpu.make_async_remote_copy(
                src_ref=own, dst_ref=target,
                send_sem=rim_send.at[turn, 3 * index + part], recv_sem=rim_recv.at[turn, 3 * index + part],
                device_id=(section, to, dp), device_id_type=MESH)

        copies = []
        for j in range(1, reach + 1):
            copies.append((
                seq + j < n_seq, seq >= j,
                copy(rim_left.at[slot, pl.ds(edge - j * positions + first, count)], 2 * j - 2, seq + j)))
            copies.append((
                seq >= j, seq + j < n_seq,
                copy(rim_right.at[slot, pl.ds((j - 1) * positions + first, count)], 2 * j - 1, seq - j)))
        return copies

    def begin(copies):
        for sends, _, copy in copies:
            pl.when(sends)(copy.start)

    def end(copies):
        for sends, receives, copy in copies:
            pl.when(receives)(copy.wait_recv)
            pl.when(sends)(copy.wait_send)

    def gather_near(backward, m, own, store, rims):
        slot = 2 * backward + m % 2
        if not rims:
            near[16 : 16 + positions] = own.astype(jnp.float32)
            pieces = thirds[:1]
        else:
            near[0:16] = rim_left[slot, edge - 16 : edge].astype(jnp.float32)
            near[16 + positions : 32 + positions] = rim_right[slot, 0:16].astype(jnp.float32)
            pieces = thirds[1:]
        for first, count in pieces:
            mask = masks[m, first : first + count]
            for k in range(KERNEL):
                if k != KERNEL // 2:
                    at = 16 + first + k - KERNEL // 2
                    store(k, first, jnp.where(mask[:, k : k + 1] > 0, near[at : at + count], 0.0))

    def gather_far(backward, m, own, store):
        slot = 2 * backward + m % 2
        mask = masks[m]
        for k in range(KERNEL):
            if k != KERNEL // 2:
                piece = far_rows(rim_left[slot], own, rim_right[slot], (k - KERNEL // 2) * DILATION_STEP)
                store(k, 0, jnp.where(mask[:, k : k + 1] > 0, piece.astype(jnp.float32), 0.0))

    def store_tap(m):
        def store(k, first, value):
            taps[tap_rows(m, k, first, value.shape[0])] = value.astype(jnp.bfloat16)

        return store

    def store_back(k, first, value):
        back_taps[k - (k > KERNEL // 2), first : first + value.shape[0]] = value.astype(jnp.bfloat16)

    def front(m, piece):
        block = slice(piece[0], piece[0] + piece[1])
        real = masks[m, block, KERNEL // 2 : KERNEL // 2 + 1]
        act, hat, slope, inverse = act_forward(
            buf[m, block].astype(jnp.float32), first_gain[...], first_shift[...], real)
        act1[m, block] = act.astype(jnp.bfloat16)
        hat1[m, block] = hat.astype(jnp.bfloat16)
        slope1[m, block] = slope.astype(jnp.bfloat16)
        masks[m, block, 8:9] = inverse
        pre = dot_nn(act1[m, block], w_in[...]) + in_bias[...]
        act, hat, slope, inverse = act_forward(pre, second_gain[...], second_shift[...], real)
        taps[tap_rows(m, KERNEL // 2, *piece)] = act.astype(jnp.bfloat16)
        hat2[m, block] = hat.astype(jnp.bfloat16)
        slope2[m, block] = slope.astype(jnp.bfloat16)
        masks[m, block, 9:10] = inverse

    def middle_tap(m, piece):
        return conv_bias[...] + dot_nn(taps[tap_rows(m, KERNEL // 2, *piece)], w_conv[KERNEL // 2])

    def rear(m, piece, pre):
        block = slice(piece[0], piece[0] + piece[1])
        for k in range(KERNEL):
            if k != KERNEL // 2:
                pre = pre + dot_nn(taps[tap_rows(m, k, *piece)], w_conv[k])
        real = masks[m, block, KERNEL // 2 : KERNEL // 2 + 1]
        act, hat, slope, inverse = act_forward(pre, third_gain[...], third_shift[...], real)
        act3[m, block] = act.astype(jnp.bfloat16)
        hat3[m, block] = hat.astype(jnp.bfloat16)
        slope3[m, block] = slope.astype(jnp.bfloat16)
        masks[m, block, 10:11] = inverse
        out = buf[m, block].astype(jnp.float32) + (dot_nn(act3[m, block], w_out[...]) + out_bias[...])
        buf[m, block] = out.astype(jnp.bfloat16)

    def count_types(m):
        logits = dot_nt(readout[...], buf[m])
        kind = lax.broadcasted_iota(jnp.int32, logits.shape, 0)
        odds = jnp.exp(logits - jnp.max(logits, axis=0, keepdims=True))
        odds = odds / jnp.sum(odds, axis=0, keepdims=True)
        stop = lengths[m, 0]
        for j in range(1, ITEMS):
            stop = stop + lengths[m, j]
        spot = lax.broadcasted_iota(jnp.int32, (1, positions), 1) + first_position
        chosen = jnp.where(spot < stop, masked[pl.ds(m, 1)].astype(jnp.float32), 0.0)
        chosen = jnp.where(kind == residues[pl.ds(m, 1)], chosen, 0.0)
        hits[...] += chosen * odds
        tally[...] += chosen

    def back_front(m, piece):
        block = slice(piece[0], piece[0] + piece[1])
        sums_wide[2] += fold(buf[rows + m, block].astype(jnp.float32))
        grad = dot_nt(buf[rows + m, block], w_out[...])
        low = act_backward(
            grad, hat3[m, block], slope3[m, block], masks[m, block, 10:11], third_gain[...], sums.at[4], sums.at[5]
        ).astype(jnp.bfloat16)
        grad2[m, block] = low
        sums[3] += fold(low.astype(jnp.float32))

    def back_middle_tap(m, piece=None):
        block = slice(0, positions) if piece is None else slice(piece[0], piece[0] + piece[1])
        return dot_nt(grad2[m, block], w_conv[KERNEL // 2])

    def back_rear(m, piece, grad, between=None):
        block = slice(piece[0], piece[0] + piece[1])
        for k in range(KERNEL):
            if k != KERNEL // 2:
                grad = grad + dot_nt(back_taps[k - (k > KERNEL // 2), block], w_conv[KERNEL - 1 - k])
        if between is not None:
            between()
        low = act_backward(
            grad, hat2[m, block], slope2[m, block], masks[m, block, 9:10], second_gain[...], sums.at[1], sums.at[2]
        ).astype(jnp.bfloat16)
        grad1[m, block] = low
        sums[0] += fold(low.astype(jnp.float32))

    def back_last(m, piece):
        block = slice(piece[0], piece[0] + piece[1])
        grad = dot_nt(grad1[m, block], w_in[...])
        grad = act_backward(
            grad, hat1[m, block], slope1[m, block], masks[m, block, 8:9], first_gain[...],
            sums_wide.at[0], sums_wide.at[1])
        hat1[m, block] = (buf[rows + m, block].astype(jnp.float32) + grad).astype(jnp.bfloat16)

    def give(source, m):
        return pltpu.make_async_copy(source.at[m], result.at[0, m], result_sem.at[m])

    wide = buf.shape[2] // hidden

    def add_block(start, value):
        total[pl.ds(start, hidden)] += value

    def weights_out(m):
        for j in range(wide):
            add_block((KERNEL + j) * hidden, dot_tn(act3[m], buf[rows + m, :, j * hidden : (j + 1) * hidden]))

    def weights_conv(m):
        for k in range(KERNEL):
            add_block(k * hidden, dot_tn(taps[tap_rows(m, k)], grad2[m]))

    def weights_in(m):
        for j in range(wide):
            add_block(rings[1].base + j * hidden, dot_tn(act1[m, :, j * hidden : (j + 1) * hidden], grad1[m]))

    def first_lane():
        rings[0].exchange(2)
        rings[0].towards(0, 0, True)

    def other_lanes():
        for lane in range(1, rings[0].lanes):
            rings[0].towards(0, lane, True)

    def step(i, carry):
        fronts = i < rows
        m_start = jnp.where(leading, i - rows, i)
        m_sum = jnp.where(leading, i - rows, i - rows + 1)
        put_off = i >= 2 * rows - 1
        m_end = jnp.where(leading, jnp.where(put_off, i - rows - 2, i - rows - 1), i - 1)
        ends = trailing | (i != 2 * rows - 1)
        m_in = jnp.where(leading, m_end, i - rows)
        final = trailing & (i == 2 * rows - 1)

        def on(m):
            return (m >= 0) & (m < rows)

        @pl.when(fronts)
        def _():
            make_mask(i)

        @pl.when(i == 0)
        def _():
            weight_loads[0].wait()
            for copy in weight_loads[1:]:
                copy.start()
            for m in range(1, rows):
                load(m).start()
            for copy in input_loads:
                copy.wait()

        @pl.when(leading & fronts)
        def _():
            load(i).wait()

        @pl.when(trailing & (i == 0))
        def _():
            pl.semaphore_wait(barrier, greeted)
            gift(0).start()
            for k in (2, 3):
                gift(k).start()
            load(last).wait()
            gift(1).start()

        @pl.when(leading & fronts)
        def _():
            front(i, whole[0])

        @pl.when(i == 0)
        def _():
            weight_loads[1].wait()
            weight_loads[2].wait()

        @pl.when(leading & fronts)
        def _():
            gather_near(0, i, taps[tap_rows(i, KERNEL // 2)], store_tap(i), False)
            rear(i, thirds[0], middle_tap(i, thirds[0]))

        @pl.when(leading & (i == 0))
        def _():
            pl.semaphore_wait(barrier, greeted)

        @pl.when(leading & fronts)
        def _():
            begin(near_copies(0, i))
            hand(buf, i, 0).start()
            end(near_copies(0, i))
            gather_near(0, i, taps[tap_rows(i, KERNEL // 2)], store_tap(i), True)
            for part in (1, 2):
                rear(i, thirds[part], middle_tap(i, thirds[part]))
                hand(buf, i, part).start()

        @pl.when(trailing & fronts)
        def _():
            for part in range(3):
                hand(buf, i, part).wait_recv()
                front(i, thirds[part])
                begin(far_copies(0, i, part, thirds))

        @pl.when(leading & (i == last))
        def _():
            gift(0).wait_recv()
            pass_on(own_half).start()

        @pl.when(leading & (i == rows + 1))
        def _():
            for k in range(1, 4):
                gift(k).wait_recv()
            far_norm()
            pass_on(own_half).wait_send()
            pass_on(other_half).wait_recv()

        @pl.when(leading & on(m_end) & ends)
        def _():
            grad = back_middle_tap(m_end)
            gather_near(1, m_end, grad2[m_end], store_back, False)

            @pl.when(m_end < last - 1)
            def _():
                end(near_copies(1, m_end))

            gather_near(1, m_end, grad2[m_end], store_back, True)

            def lanes_between():
                pl.when(i == 2 * rows)(first_lane)

                @pl.when(i == 2 * rows + 1)
                def _():
                    rings[0].towards(1, 0)
                    rings[0].exchange(3)

            back_rear(m_end, whole[0], grad, lanes_between)
            back_last(m_end, whole[0])
            give(hat1, m_end).start()
            pl.when(i == 2 * rows)(other_lanes)

        @pl.when(trailing & on(m_end))
        def _():
            grads = [back_middle_tap(m_end, piece) for piece in parts]
            for part in range(2):
                end(far_copies(1, m_end, part, parts))
            gather_far(1, m_end, grad2[m_end], store_back)
            for part in range(2):
                back_rear(m_end, parts[part], grads[part])
                pl.when(m_end == last)(low_hand(part).start)
                back_last(m_end, parts[part])
                pl.when(m_end < last)(hand(hat1, m_end, part).start)

        @pl.when(final)
        def _():
            first_lane()
            other_lanes()

        @pl.when(on(m_in) & ends)
        def _():
            weights_in(m_in)

        @pl.when(final)
        def _():
            rings[0].towards(1, 0)
            rings[0].exchange(3)

        @pl.when(final | (leading & (i == 2 * rows + 1)))
        def _():
            rings[1].exchange(0)
            rings[1].exchange(1)

        @pl.when((leading & (i == 2)) | (trailing & (i == 0)))
        def _():
            total[...] = jnp.zeros_like(total)
            sums_wide[...] = jnp.zeros_like(sums_wide)
            sums[...] = jnp.zeros_like(sums)
            hits[...] = jnp.zeros_like(hits)
            tally[...] = jnp.zeros_like(tally)

        @pl.when(trailing & fronts)
        def _():
            pre = middle_tap(i, whole[0])

            for part in range(3):
                end(far_copies(0, i, part, thirds))
            gather_far(0, i, taps[tap_rows(i, KERNEL // 2)], store_tap(i))
            rear(i, whole[0], pre)
            give(buf, i).start()

        @pl.when(on(m_start))
        def _():
            pl.when(trailing & (m_start < last))(load(m_start).wait)
            for part in range(2):
                pl.when(leading & (m_start < last))(hand(hat1, m_start, part).wait_recv)

                @pl.when(leading & (m_start == last))
                def _():
                    low_hand(part).wait_recv()
                    far_last(parts[part])

                back_front(m_start, parts[part])

                @pl.when(trailing)
                def _():
                    begin(far_copies(1, m_start, part, parts))

            @pl.when(leading & (m_start == last))
            def _():
                end(near_copies(1, last - 1))

            @pl.when(leading)
            def _():
                begin(near_copies(1, m_start))

        @pl.when(trailing & fronts)
        def _():
            count_types(i)

        @pl.when(on(m_sum))
        def _():
            weights_out(m_sum)
            weights_conv(m_sum)

        @pl.when(leading & (m_sum == last))
        def _():
            end(near_copies(1, last))

        @pl.when(m_sum == last)
        def _():
            rings[0].exchange(0)
            rings[0].exchange(1)

        return carry

    lax.fori_loop(0, 2 * rows + 2, step, 0)

    def fill_small():
        for i in range(3):
            small[i : i + 1, :] = jnp.sum(sums_wide[i], axis=0, keepdims=True)
        for i in range(6):
            small[3 + i // 2 : 4 + i // 2, (i % 2) * hidden : (i % 2 + 1) * hidden] = jnp.sum(sums[i], axis=0, keepdims=True)
        small[6:8, :] = jnp.zeros((2, small.shape[1]), jnp.float32)
        ones = jnp.ones((8, positions), jnp.float32)
        for i, counted in ((6, hits), (7, tally)):
            row = lax.dot_general(
                ones, counted[...], (((1,), (1,)), ((), ())), precision=lax.Precision.HIGHEST,
                preferred_element_type=jnp.float32)
            small[i : i + 1, 0 : counted.shape[0]] = row[0:1]

    run_rings(rings, fill_small, SmallSum(rings[0], small, small_land, small_out, small_send, small_recv, partner()))
    for m in range(rows):
        @pl.when(leading)
        def _():
            if m not in (1, 2):
                for part in range(3):
                    hand(buf, m, part).wait_send()
            give(hat1, m).wait()

        @pl.when(trailing)
        def _():
            for part in range(2):
                (hand(hat1, m, part) if m < last else low_hand(part)).wait_send()
            give(buf, m).wait()

    @pl.when(trailing)
    def _():
        for k in range(4):
            gift(k).wait_send()


def ring_plan(width, hidden, nodes):
    plan, base, land = [], 0, 0
    for rows, subs in (((KERNEL + width // hidden) * hidden, LANES), (width, 1)):
        sizes = ring_sizes(rows // 2, nodes, subs)
        plan.append((sizes, base, land))
        land += nodes * sum(map(sum, sizes))
        base = 2 * land
    return plan, land


def run_blocks(args, ny, nz, cid=0):
    nodes = ny * nz
    doublings = 1 + (ny - 1).bit_length() + (nz - 1).bit_length()
    boundary, in_weight, conv_weight = args[0], args[7], args[11]
    _, rows, positions, width = boundary.shape
    hidden = in_weight.shape[2]
    edge = KERNEL // 2 * DILATION_STEP
    assert edge % positions == 0 and positions % 32 == 0 and width % hidden == 0
    reach = edge // positions
    low, full = jnp.bfloat16, jnp.float32
    wide_rows = pltpu.VMEM((rows, positions, width), low)
    thin_rows = pltpu.VMEM((rows, positions, hidden), low)
    plan, half = ring_plan(width, hidden, nodes)
    where = [pltpu.HBM, pltpu.SMEM] + [pltpu.HBM] * 15
    smalls = [pltpu.VMEM(args[i].shape, args[i].dtype) for i in (2, 3, 4, 5, 6, 8, 9, 10, 12, 13, 14, 16)]
    return pl.pallas_call(
        functools.partial(blocks_kernel, edge, plan),
        out_shape=(
            jax.ShapeDtypeStruct(boundary.shape, low),
            jax.ShapeDtypeStruct((2 * half, hidden), low),
            jax.ShapeDtypeStruct((16, width), full),
        ),
        in_specs=[pl.BlockSpec(memory_space=space) for space in where],
        out_specs=[pl.BlockSpec(memory_space=space) for space in (pltpu.HBM, pltpu.HBM, pltpu.VMEM)],
        scratch_shapes=smalls + [
            pltpu.VMEM((2 * rows, positions, width), low),
            pltpu.VMEM((width, hidden), low),
            pltpu.VMEM((KERNEL, hidden, hidden), low),
            pltpu.VMEM((hidden, width), low),
            pltpu.VMEM((2 * half, hidden), full),
            wide_rows, wide_rows, wide_rows,
            pltpu.VMEM((max(rows * KERNEL * positions, half), hidden), low),
            pltpu.VMEM((KERNEL - 1, positions, hidden), low),
            thin_rows, thin_rows, thin_rows, thin_rows, thin_rows,
            pltpu.VMEM((4, edge, hidden), low),
            pltpu.VMEM((4, edge, hidden), low),
            pltpu.VMEM((positions + 32, hidden), full),
            pltpu.VMEM((rows, positions, 128), full),
            pltpu.VMEM((3, 8, width), full),
            pltpu.VMEM((6, 8, hidden), full),
            pltpu.VMEM((VOCAB, positions), full),
            pltpu.VMEM((VOCAB, positions), full),
            pltpu.VMEM((half, hidden), low),
            pltpu.VMEM((8, width), full),
            pltpu.VMEM((2 * doublings, 8, width), full),
            pltpu.SemaphoreType.DMA((rows,)),
            pltpu.SemaphoreType.DMA((3,)),
            pltpu.SemaphoreType.DMA((rows,)),
            pltpu.SemaphoreType.DMA((rows, 3)),
            pltpu.SemaphoreType.DMA((rows, 3)),
            pltpu.SemaphoreType.DMA((2 * rows, 6 * reach)),
            pltpu.SemaphoreType.DMA((2 * rows, 6 * reach)),
            pltpu.SemaphoreType.DMA((doublings + 1,)),
            pltpu.SemaphoreType.DMA((doublings + 1,)),
            pltpu.SemaphoreType.DMA((len(smalls),)),
            pltpu.VMEM((positions, hidden), low),
            pltpu.VMEM((1, width), full),
            pltpu.VMEM((1, width), full),
            pltpu.SemaphoreType.DMA((5,)),
            pltpu.SemaphoreType.DMA((5,)),
        ]
        + [scratch for sizes, _, _ in plan for scratch in ring_scratch(sizes, nodes, hidden)],
        compiler_params=pltpu.CompilerParams(
            collective_id=cid, has_side_effects=True, vmem_limit_bytes=VMEM_BYTES),
    )(*args)


def ring_sizes(rows, nodes, subs):
    units = -(-rows // (nodes * 16))
    long = -(-units // 2)
    return [[16 * ((way + i) // subs) for i in range(subs)] for way in (long, units - long)]


def ring_flows(sizes):
    return [(way, i) for i in range(len(sizes[0])) for way in range(2) if sizes[way][i]]


def ring_scratch(sizes, nodes, columns):
    flows = ring_flows(sizes)
    n = len(flows)
    counts = [(n, nodes)] * 2 + [(n, 2 * nodes - 2)] * 2 + [(n, nodes)] * 2 + [(n,)]
    return [pltpu.SemaphoreType.DMA(count) for count in counts] + [
        pltpu.VMEM((nodes - 1, sizes[way][i], columns), jnp.bfloat16) for way, i in flows]


class Ring:
    def __init__(self, sizes, base, land, section, seq, dp, ny, nz):
        self.sizes, self.base, self.land, self.nodes = sizes, base, land, ny * nz
        self.flows = ring_flows(sizes)
        self.refs = 7 + len(self.flows)
        self.lanes = len(sizes[0])
        self.section, self.nz = section, nz
        self.core, ypos = seq % 2, seq // 2
        self.spot = ypos * nz + dp + (ypos % 2) * (nz - 1 - 2 * dp)
        self.other_core = (section, seq + 1 - 2 * self.core, dp)
        self.turn = [1 - 2 * self.core, 2 * self.core - 1]
        self.next = [self.at_spot(self.wrap(self.spot + self.nodes + turn)) for turn in self.turn]
        self.half = sum(map(sum, sizes)) * self.nodes
        self.first, at = {}, 0
        for way, i in self.flows:
            self.first[way, i] = at
            at += sizes[way][i] * self.nodes
        self.peers = [self.other_core]
        reach = 1
        while reach < ny:
            self.peers.append((section, seq + 2 * reach - 4 * reach * ((ypos // reach) % 2), dp))
            reach *= 2
        reach = 1
        while reach < nz:
            self.peers.append((section, seq, dp + reach - 2 * reach * ((dp // reach) % 2)))
            reach *= 2

    def wrap(self, place):
        if self.nodes & (self.nodes - 1) == 0:
            return place & (self.nodes - 1)
        return lax.rem(place, self.nodes)

    def at_spot(self, place):
        y = place // self.nz
        z = place % self.nz
        return (self.section, y * 2 + self.core, z + (y % 2) * (self.nz - 1 - 2 * z))

    def neighbours(self):
        around = self.next
        return self.peers + around

    def bind(self, total, stage, core_land, big, refs):
        self.total, self.stage, self.core_land, self.big = total, stage, core_land, big
        self.core_sems, self.ring_sems, self.over_sems = refs[0:2], refs[2:4], refs[4:6]
        self.keep_sem, self.lands = refs[6], refs[7:]

    def count(self, f):
        way, i = self.flows[f]
        return self.sizes[way][i]

    def rows(self, f, side, shard):
        start = self.base + side * self.half + self.first[self.flows[f]] + shard * self.count(f)
        return pl.ds(pl.multiple_of(start, 16), self.count(f))

    def land_rows(self, f, shard):
        start = self.land + self.first[self.flows[f]] + shard * self.count(f)
        return pl.ds(pl.multiple_of(start, 16), self.count(f))

    def shard(self, f, step):
        return self.wrap(self.spot + 2 * self.nodes - self.turn[self.flows[f][0]] * step)

    def ahead(self, f):
        return self.next[self.flows[f][0]]

    def remote(self, source, target, sems, index, peer):
        return pltpu.make_async_remote_copy(
            src_ref=source, dst_ref=target, send_sem=sems[0].at[index], recv_sem=sems[1].at[index],
            device_id=peer, device_id_type=MESH)

    def core_copy(self, f, shard):
        rows = self.land_rows(f, shard)
        return self.remote(self.stage.at[rows], self.core_land.at[rows], self.core_sems, (f, shard), self.other_core)

    def ring_copy(self, f, step, shard):
        return self.remote(
            self.core_land.at[self.land_rows(f, shard)], self.lands[f].at[step], self.ring_sems, (f, step), self.ahead(f))

    def back_copy(self, f, step, shard):
        block = self.big.at[self.rows(f, self.core, shard)]
        return self.remote(
            self.core_land.at[self.land_rows(f, shard)] if step is None else block, block,
            self.ring_sems, (f, self.nodes - 1 + (0 if step is None else step)), self.ahead(f))

    def over_copy(self, f, shard, own=False):
        block = self.big.at[self.rows(f, self.core, shard)]
        return self.remote(
            self.core_land.at[self.land_rows(f, shard)] if own else block, block,
            self.over_sems, (f, shard), self.other_core)

    def keep_copy(self, f, shard):
        return pltpu.make_async_copy(
            self.core_land.at[self.land_rows(f, shard)], self.big.at[self.rows(f, self.core, shard)], self.keep_sem.at[f])

    def add(self, f, shard, step):
        rows = self.land_rows(f, shard)
        value = self.total[self.rows(f, self.core, shard)] + self.core_land[rows].astype(jnp.float32)
        if step is not None:
            value = value + self.lands[f][step].astype(jnp.float32)
        self.core_land[rows] = value.astype(jnp.bfloat16)

    def exchange(self, step):
        for f in range(len(self.flows)):
            shard = self.shard(f, -step)
            self.stage[self.land_rows(f, shard)] = self.total[self.rows(f, 1 - self.core, shard)].astype(jnp.bfloat16)
            self.core_copy(f, shard).start()

    def of(self, lane):
        return [f for f in range(len(self.flows)) if lane is None or self.flows[f][1] == lane]

    def towards(self, step, lane=None, first=False):
        for f in self.of(lane):
            shard = self.shard(f, step)
            self.core_copy(f, shard).wait_recv()
            if first:
                self.add(f, shard, None)
            else:
                self.ring_copy(f, step - 1, shard).wait_recv()
                self.add(f, shard, step - 1)
            self.ring_copy(f, step, shard).start()

    def back(self, step, lane=None):
        for f in self.of(lane):
            shard = self.shard(f, self.nodes - 1 + step)
            self.back_copy(f, step - 1, shard).wait_recv()
            self.back_copy(f, step, shard).start()
            self.over_copy(f, shard).start()

    def own(self, lane=None):
        for f in self.of(lane):
            shard = self.shard(f, self.nodes - 1)
            self.core_copy(f, shard).wait_recv()
            self.ring_copy(f, self.nodes - 2, shard).wait_recv()
            self.add(f, shard, self.nodes - 2)
            self.back_copy(f, None, shard).start()
            self.over_copy(f, shard, True).start()
            self.keep_copy(f, shard).start()

    def arrive(self, lane=None):
        for f in self.of(lane):
            shard = self.shard(f, 2 * self.nodes - 2)
            self.back_copy(f, self.nodes - 2, shard).wait_recv()
            self.over_copy(f, shard).start()

    def settle(self):
        def crossed(step, carry):
            for f in range(len(self.flows)):
                self.core_copy(f, step).wait_send()
                self.over_copy(f, step).wait()
            return carry

        def rounded(step, carry):
            for f in range(len(self.flows)):
                self.ring_copy(f, step, 0).wait_send()
                self.back_copy(f, step, 0).wait_send()
            return carry

        lax.fori_loop(0, self.nodes, crossed, 0)
        lax.fori_loop(0, self.nodes - 1, rounded, 0)
        for f in range(len(self.flows)):
            self.keep_copy(f, 0).wait()


def run_rings(rings, fill_small, small_sum):
    ahead, behind = rings
    nodes, lanes = ahead.nodes, ahead.lanes

    def each(method, *step):
        for lane in range(lanes):
            getattr(ahead, method)(*step, lane)
        getattr(behind, method)(*step)

    for lane in range(1, lanes):
        ahead.towards(1, lane)
    for step in (2, 3):
        ahead.exchange(step + 2)
        behind.exchange(2 * step - 2)
        behind.exchange(2 * step - 1)
        ahead.towards(step, 0)
        behind.towards(2 * step - 4, first=step == 2)
        for lane in range(1, lanes):
            ahead.towards(step, lane)
        behind.towards(2 * step - 3)

    fill_small()
    small_sum.step(0)

    def towards(step, carry):
        ahead.exchange(step + 2)
        behind.exchange(step + 2)
        each("towards", step)
        return carry

    lax.fori_loop(4, nodes - 2, towards, 0)
    each("towards", nodes - 2)
    each("own")
    small_sum.step(1)
    at = 1
    for k in range(2, small_sum.steps):
        if at < nodes - 1:
            each("back", at)
            at += 1
        small_sum.step(k)

    def back(step, carry):
        each("back", step)
        return carry

    lax.fori_loop(at, nodes - 1, back, 0)
    each("arrive")
    ahead.settle()
    behind.settle()
    small_sum.settle()


class SmallSum:
    def __init__(self, ring, small, land, out, send_sem, recv_sem, other_section):
        self.peers, self.small, self.land, self.out = ring.peers + [other_section], small, land, out
        self.sems = (send_sem, recv_sem)
        self.remote = ring.remote
        self.steps = len(self.peers) + 1

    def held(self, k):
        return self.small if k == 0 else self.land.at[2 * k - 1]

    def copy(self, k):
        count = self.small.shape[0]
        target = self.out.at[pl.ds(count, count)] if k == len(self.peers) - 1 else self.land.at[2 * k]
        return self.remote(self.held(k), target, self.sems, k, self.peers[k])

    def step(self, k):
        last = len(self.peers) - 1
        if 0 < k:
            self.copy(k - 1).wait_recv()
        if 0 < k <= last:
            self.land[2 * k - 1] = self.held(k - 1)[...] + self.land[2 * k - 2]
        if k <= last:
            self.copy(k).start()
        if k == last:
            self.out[pl.ds(0, self.small.shape[0])] = self.held(k)[...]

    def settle(self):
        for k in range(len(self.peers)):
            self.copy(k).wait_send()


def finish_kernel(
    base, given, big, small_in, result, grad_in, grad_conv, grad_out, first_gain, first_shift, in_bias, second_gain,
    second_shift, conv_bias, third_gain, third_shift, out_bias, scores, counts,
    small, passed, held, wide, rate, count, pass_sem, load_sem, store_sem, small_sem,
):
    hidden = held.shape[2]
    blocks = held.shape[0]
    ends = grad_in.shape[1] // hidden
    small_load = pltpu.make_async_copy(small_in, small, pass_sem.at[0])
    first = pltpu.make_async_copy(given, passed, pass_sem.at[1])
    second = pltpu.make_async_copy(passed, result, pass_sem.at[2])

    def load(b):
        start = b * hidden if b < blocks - ends else base + (b - blocks + ends) * hidden
        return pltpu.make_async_copy(big.at[pl.ds(start, hidden)], held.at[b], load_sem.at[b])

    def store(b):
        if b < KERNEL:
            target = grad_conv.at[0, b]
        elif b < blocks - ends:
            target = grad_out.at[0, :, pl.ds((b - KERNEL) * hidden, hidden)]
        else:
            target = grad_in.at[0, pl.ds((b - blocks + ends) * hidden, hidden)]
        return pltpu.make_async_copy(wide.at[b], target, store_sem.at[b])

    load(0).start()
    small_load.start()
    for b in range(1, blocks):
        load(b).start()
    first.start()
    for b in range(blocks):
        load(b).wait()
        wide[b] = held[b].astype(jnp.float32)
        store(b).start()
        if b == 0:
            small_load.wait()
            hits = small[6:7, 0:VOCAB] + small[14:15, 0:VOCAB]
            tally = small[7:8, 0:VOCAB] + small[15:16, 0:VOCAB]
            rate[...] = hits / jnp.maximum(tally, 1.0)
            count[...] = tally.astype(jnp.int32)
            pieces = [(small.at[pl.ds(i, 1)], ref) for i, ref in enumerate((first_gain, first_shift, out_bias))]
            thin = (in_bias, second_gain, second_shift, conv_bias, third_gain, third_shift)
            for i, ref in enumerate(thin):
                pieces.append((small.at[pl.ds(3 + i // 2, 1), pl.ds(i % 2 * hidden, hidden)], ref))
            pieces += [(rate, scores), (count, counts)]
            small_stores = [
                pltpu.make_async_copy(source, target, small_sem.at[i]) for i, (source, target) in enumerate(pieces)
            ]
            for copy in small_stores:
                copy.start()
    first.wait()
    second.start()
    for b in range(blocks):
        store(b).wait()
    for copy in small_stores:
        copy.wait()
    second.wait()


def finish(given, big, small, width, base):
    hidden = big.shape[1]
    blocks = 2 * width // hidden + KERNEL
    full = jnp.float32
    shapes = [(1, width, hidden), (1, KERNEL, hidden, hidden), (1, hidden, width), (1, width), (1, width)]
    shapes += [(1, hidden)] * 6 + [(1, width), (1, VOCAB)]
    out = [jax.ShapeDtypeStruct(given.shape, given.dtype)]
    out += [jax.ShapeDtypeStruct(shape, full) for shape in shapes] + [jax.ShapeDtypeStruct((1, VOCAB), jnp.int32)]
    return pl.pallas_call(
        functools.partial(finish_kernel, base),
        out_shape=out,
        in_specs=[pl.BlockSpec(memory_space=pltpu.HBM)] * 3,
        out_specs=[pl.BlockSpec(memory_space=pltpu.HBM)] * len(out),
        scratch_shapes=[
            pltpu.VMEM(small.shape, full),
            pltpu.VMEM(given.shape, given.dtype),
            pltpu.VMEM((blocks, hidden, hidden), big.dtype),
            pltpu.VMEM((blocks, hidden, hidden), full),
            pltpu.VMEM((1, VOCAB), full),
            pltpu.VMEM((1, VOCAB), jnp.int32),
            pltpu.SemaphoreType.DMA((3,)),
            pltpu.SemaphoreType.DMA((blocks,)),
            pltpu.SemaphoreType.DMA((blocks,)),
            pltpu.SemaphoreType.DMA((11,)),
        ],
        compiler_params=pltpu.CompilerParams(vmem_limit_bytes=VMEM_BYTES),
    )(given, big, small)


def shards(
    boundary, lengths, masked, residues, readout,
    first_gain, first_shift, in_weight, in_bias, second_gain, second_shift, conv_weight, conv_bias,
    third_gain, third_shift, out_weight, out_bias,
):
    ny, nz = lax.axis_size("seq") // 2, lax.axis_size("dp")
    width, hidden = in_weight.shape[1], in_weight.shape[2]
    given, big, small = run_blocks(
        (
            boundary, lengths, masked, residues, readout.T,
            first_gain, first_shift, in_weight, in_bias, second_gain, second_shift, conv_weight, conv_bias,
            third_gain, third_shift, out_weight, out_bias,
        ),
        ny,
        nz,
    )
    (
        boundary_out, grad_in_weight, grad_conv_weight, grad_out_weight, grad_first_gain, grad_first_shift, grad_in_bias,
        grad_second_gain, grad_second_shift, grad_conv_bias, grad_third_gain, grad_third_shift, grad_out_bias,
        scores, counts,
    ) = finish(given, big, small, width, ring_plan(width, hidden, ny * nz)[0][1][1])
    return (
        boundary_out,
        grad_first_gain,
        grad_first_shift,
        grad_in_weight,
        grad_in_bias,
        grad_second_gain,
        grad_second_shift,
        grad_conv_weight,
        grad_conv_bias,
        grad_third_gain,
        grad_third_shift,
        grad_out_weight,
        grad_out_bias,
        scores[0],
        counts[0],
    )


def solution(mesh):
    in_specs = (
        P("section", "dp", "seq", None),
        P("dp", None),
        P("dp", "seq"),
        P("dp", "seq"),
        P(),
        P("section", None),
        P("section", None),
        P("section", None, None),
        P("section", None),
        P("section", None),
        P("section", None),
        P("section", None, None, None),
        P("section", None),
        P("section", None),
        P("section", None),
        P("section", None, None),
        P("section", None),
    )
    out_specs = (
        P("section", "dp", "seq", None),
        P("section", None),
        P("section", None),
        P("section", None, None),
        P("section", None),
        P("section", None),
        P("section", None),
        P("section", None, None, None),
        P("section", None),
        P("section", None),
        P("section", None),
        P("section", None, None),
        P("section", None),
        P(),
        P(),
    )
    return jax.shard_map(shards, mesh=mesh, in_specs=in_specs, out_specs=out_specs, check_vma=False)
```

```python
import functools

import jax
import jax.numpy as jnp
from jax import lax
from jax.experimental import pallas as pl
from jax.experimental.pallas import tpu as pltpu
from jax.sharding import PartitionSpec as P

KERNEL = 5
VOCAB = 30
DILATION_STEP = 128
ITEMS = 4
EPSILON = 1e-05
ROOT_HALF = 0.7071067811865476
HALF_LOG = -0.7213475204444817
ROOT_TAU = 0.3989422804014327

MESH = pl.DeviceIdType.MESH
LANES = 2
VMEM_BYTES = 64 << 20


def far_rows(left, own, right, offset):
    edge, positions = left.shape[0], own.shape[0]
    first, last = offset + edge, offset + edge + positions
    pieces, at = [], 0
    for block in (left, own, right):
        lo, hi = max(first, at), min(last, at + block.shape[0])
        if lo < hi:
            pieces.append(block[lo - at : hi - at])
        at += block.shape[0]
    return pieces[0] if len(pieces) == 1 else jnp.concatenate(pieces, axis=0)


def act_forward(values, gain, shift, real):
    scale = 1.0 / values.shape[1]
    centred = values - jnp.sum(values, axis=1, keepdims=True) * scale
    spread = jnp.sum(centred * centred, axis=1, keepdims=True) * scale
    inverse = lax.rsqrt(spread + EPSILON)
    hat = centred * inverse
    moved = hat * gain + shift
    below = (0.5 + 0.5 * lax.erf(moved * ROOT_HALF)) * real
    density = jnp.exp2(moved * moved * HALF_LOG) * (ROOT_TAU * real)
    return moved * below, hat, below + moved * density, inverse


def fold(values):
    rows, columns = values.shape
    return jnp.sum(values.reshape(rows // 8, 8, columns), axis=0)


def act_backward(grad, hat, slope, inverse, gain, gain_sum, shift_sum):
    scale = 1.0 / grad.shape[1]
    hat = hat.astype(jnp.float32)
    moved = grad * slope.astype(jnp.float32)
    turned = moved * hat
    shift_sum[...] += fold(moved)
    gain_sum[...] += fold(turned)
    mean = jnp.sum(moved * gain, axis=1, keepdims=True) * scale
    tilt = jnp.sum(turned * gain, axis=1, keepdims=True) * scale
    return inverse * (moved * gain - mean - hat * tilt)


def dot_nn(a, b):
    return jnp.dot(a, b, preferred_element_type=jnp.float32)


def dot_nt(a, b):
    return lax.dot_general(a, b, (((1,), (1,)), ((), ())), preferred_element_type=jnp.float32)


def dot_tn(a, b):
    return lax.dot_general(a, b, (((0,), (0,)), ((), ())), preferred_element_type=jnp.float32)


def blocks_kernel(
    edge, plan,
    boundary, lengths, masked_in, residues_in, readout_in,
    first_gain_in, first_shift_in, in_weight, in_bias_in, second_gain_in, second_shift_in, conv_weight, conv_bias_in,
    third_gain_in, third_shift_in, out_weight, out_bias_in,
    result, big, small_out,
    masked, residues, readout, first_gain, first_shift, in_bias, second_gain, second_shift, conv_bias,
    third_gain, third_shift, out_bias,
    buf, w_in, w_conv, w_out, total, hat1, slope1, act1, taps, back_taps,
    hat2, slope2, hat3, slope3, act3, rim_left, rim_right, near, masks,
    sums_wide, sums, hits, tally, core_land, small, small_land,
    load_sem, weight_sem, result_sem, hand_send, hand_recv, rim_send, rim_recv, small_send, small_recv, input_sem,
    low_land, far_gain, far_shift, gift_send, gift_recv, *ring_refs,
):
    grad1, grad2 = hat2, hat3
    section = lax.axis_index("section")
    seq = lax.axis_index("seq")
    dp = lax.axis_index("dp")
    n_seq = lax.axis_size("seq")
    rows, positions = buf.shape[0] // 2, buf.shape[1]
    hidden = w_in.shape[1]
    leading = section == 0
    trailing = section == 1
    row_len = n_seq * positions
    first_position = seq * positions
    reach = edge // positions
    dilation = jnp.where(leading, 1, DILATION_STEP)

    def load(m):
        return pltpu.make_async_copy(boundary.at[0, m], buf.at[section * rows + m], load_sem.at[m])

    weight_loads = [
        pltpu.make_async_copy(source.at[0], target, weight_sem.at[i])
        for i, (source, target) in enumerate(((in_weight, w_in), (conv_weight, w_conv), (out_weight, w_out)))
    ]
    input_loads = [
        pltpu.make_async_copy(source, target, input_sem.at[i])
        for i, (source, target) in enumerate((
            (first_gain_in, first_gain), (first_shift_in, first_shift), (in_bias_in, in_bias),
            (second_gain_in, second_gain), (second_shift_in, second_shift), (conv_bias_in, conv_bias),
            (third_gain_in, third_gain), (third_shift_in, third_shift), (out_bias_in, out_bias),
            (masked_in, masked), (residues_in, residues), (readout_in, readout),
        ))
    ]
    load(0).start()
    weight_loads[0].start()
    for copy in input_loads:
        copy.start()

    def partner():
        return (1 - section, seq, dp)

    rings, at = [], 0
    for sizes, base, land in plan:
        ring = Ring(sizes, base, land, section, seq, dp, n_seq // 2, lax.axis_size("dp"))
        ring.bind(total, taps, core_land, big, ring_refs[at : at + ring.refs])
        at += ring.refs
        rings.append(ring)
    barrier = pltpu.get_barrier_semaphore()
    greet = [partner()] + rings[0].neighbours()
    for peer in greet:
        pl.semaphore_signal(barrier, inc=1, device_id=peer, device_id_type=MESH)
    greeted = len(greet)
    for j in range(1, reach + 1):
        for side in (-j, j):
            on = (seq + side >= 0) & (seq + side < n_seq)
            greeted = greeted + on.astype(jnp.int32)

            @pl.when(on)
            def _():
                pl.semaphore_signal(barrier, inc=1, device_id=(section, seq + side, dp), device_id_type=MESH)

    @pl.when(seq < reach)
    def _():
        rim_left[...] = jnp.zeros_like(rim_left)

    @pl.when(seq >= n_seq - reach)
    def _():
        rim_right[...] = jnp.zeros_like(rim_right)

    last = rows - 1
    half, quarter = positions // 2, positions // 4
    parts = ((0, half), (half, half))
    thirds = ((quarter, half), (0, quarter), (half + quarter, quarter))
    whole = ((0, positions),)

    def make_mask(m):
        lane = lax.broadcasted_iota(jnp.int32, (positions, 128), 1)
        place = lax.broadcasted_iota(jnp.int32, (positions, 128), 0) + first_position
        other = place + (lane - KERNEL // 2) * dilation
        end = 0
        here = jnp.zeros((positions, 128), jnp.int32)
        there = jnp.zeros((positions, 128), jnp.int32)
        for j in range(ITEMS):
            end = end + lengths[m, j]
            here = here + (place >= end).astype(jnp.int32)
            there = there + (other >= end).astype(jnp.int32)
        counts = (here == there) & (here < ITEMS) & (other >= 0) & (other < row_len)
        masks[m] = counts.astype(jnp.float32)

    def hand(source, m, part):
        first, count = (thirds if source is buf else parts)[part]
        block = pl.ds(first, count)
        target = buf.at[m, block] if source is buf else buf.at[rows + m, block]
        return pltpu.make_async_remote_copy(
            src_ref=source.at[m, block], dst_ref=target,
            send_sem=hand_send.at[m, part], recv_sem=hand_recv.at[m, part],
            device_id=partner(), device_id_type=MESH)

    def low_hand(part):
        block = pl.ds(*parts[part])
        return pltpu.make_async_remote_copy(
            src_ref=grad1.at[last, block], dst_ref=low_land.at[block],
            send_sem=hand_send.at[last, part], recv_sem=hand_recv.at[last, part],
            device_id=partner(), device_id_type=MESH)

    core = seq % 2
    wide_half = buf.shape[2] // 2
    own_half = pl.ds(pl.multiple_of(core * wide_half, 16), wide_half)
    other_half = pl.ds(pl.multiple_of((1 - core) * wide_half, 16), wide_half)

    def gift(i):
        source, target = (
            (w_in.at[own_half], core_land.at[own_half]),
            (buf.at[rows + last], buf.at[rows + last]),
            (first_gain, far_gain),
            (first_shift, far_shift),
        )[i]
        return pltpu.make_async_remote_copy(
            src_ref=source, dst_ref=target, send_sem=gift_send.at[i], recv_sem=gift_recv.at[i],
            device_id=partner(), device_id_type=MESH)

    def pass_on(half):
        return pltpu.make_async_remote_copy(
            src_ref=core_land.at[half], dst_ref=core_land.at[half],
            send_sem=gift_send.at[4], recv_sem=gift_recv.at[4],
            device_id=(section, seq + 1 - 2 * core, dp), device_id_type=MESH)

    def far_norm():
        for m in (1, 2):
            for part in range(3):
                hand(buf, m, part).wait_send()
        for first, count in parts:
            block = slice(first, first + count)
            real = masks[last, block, KERNEL // 2 : KERNEL // 2 + 1]
            _, hat, slope, inverse = act_forward(
                buf[last, block].astype(jnp.float32), far_gain[...], far_shift[...], real)
            buf[1, block] = hat.astype(jnp.bfloat16)
            buf[2, block] = slope.astype(jnp.bfloat16)
            masks[last, block, 11:12] = inverse

    def far_last(piece):
        block = slice(piece[0], piece[0] + piece[1])
        scale = 1.0 / buf.shape[2]
        hat = buf[1, block].astype(jnp.float32)
        grad = dot_nt(low_land[block], core_land[0 : 2 * wide_half]) * buf[2, block].astype(jnp.float32) * far_gain[...]
        mean = jnp.sum(grad, axis=1, keepdims=True) * scale
        tilt = jnp.sum(grad * hat, axis=1, keepdims=True) * scale
        grad = masks[last, block, 11:12] * (grad - mean - hat * tilt)
        buf[rows + last, block] = (buf[rows + last, block].astype(jnp.float32) + grad).astype(jnp.bfloat16)

    def tap_rows(m, k, first=0, count=None):
        start = (m * KERNEL + k) * positions + first
        return pl.ds(pl.multiple_of(start, 16), positions if count is None else count)

    def near_copies(backward, m):
        slot = 2 * backward + m % 2
        turn = backward * rows + m

        def edge_rows(first):
            return grad2.at[m, pl.ds(first, 16)] if backward else taps.at[tap_rows(m, KERNEL // 2, first, 16)]

        def copy(source, target, index, to):
            return pltpu.make_async_remote_copy(
                src_ref=source, dst_ref=target, send_sem=rim_send.at[turn, index], recv_sem=rim_recv.at[turn, index],
                device_id=(section, to, dp), device_id_type=MESH)

        return [
            (seq + 1 < n_seq, seq >= 1,
             copy(edge_rows(positions - 16), rim_left.at[slot, pl.ds(edge - 16, 16)], 0, seq + 1)),
            (seq >= 1, seq + 1 < n_seq,
             copy(edge_rows(0), rim_right.at[slot, pl.ds(0, 16)], 1, seq - 1)),
        ]

    def far_copies(backward, m, part, pieces):
        first, count = pieces[part]
        slot = 2 * backward + m % 2
        turn = backward * rows + m
        own = grad2.at[m, pl.ds(first, count)] if backward else taps.at[tap_rows(m, KERNEL // 2, first, count)]

        def copy(target, index, to):
            return pltpu.make_async_remote_copy(
                src_ref=own, dst_ref=target,
                send_sem=rim_send.at[turn, 3 * index + part], recv_sem=rim_recv.at[turn, 3 * index + part],
                device_id=(section, to, dp), device_id_type=MESH)

        copies = []
        for j in range(1, reach + 1):
            copies.append((
                seq + j < n_seq, seq >= j,
                copy(rim_left.at[slot, pl.ds(edge - j * positions + first, count)], 2 * j - 2, seq + j)))
            copies.append((
                seq >= j, seq + j < n_seq,
                copy(rim_right.at[slot, pl.ds((j - 1) * positions + first, count)], 2 * j - 1, seq - j)))
        return copies

    def begin(copies):
        for sends, _, copy in copies:
            pl.when(sends)(copy.start)

    def end(copies):
        for sends, receives, copy in copies:
            pl.when(receives)(copy.wait_recv)
            pl.when(sends)(copy.wait_send)

    def gather_near(backward, m, own, store, rims):
        slot = 2 * backward + m % 2
        if not rims:
            near[16 : 16 + positions] = own.astype(jnp.float32)
            pieces = thirds[:1]
        else:
            near[0:16] = rim_left[slot, edge - 16 : edge].astype(jnp.float32)
            near[16 + positions : 32 + positions] = rim_right[slot, 0:16].astype(jnp.float32)
            pieces = thirds[1:]
        for first, count in pieces:
            mask = masks[m, first : first + count]
            for k in range(KERNEL):
                if k != KERNEL // 2:
                    at = 16 + first + k - KERNEL // 2
                    store(k, first, jnp.where(mask[:, k : k + 1] > 0, near[at : at + count], 0.0))

    def gather_far(backward, m, own, store):
        slot = 2 * backward + m % 2
        mask = masks[m]
        for k in range(KERNEL):
            if k != KERNEL // 2:
                piece = far_rows(rim_left[slot], own, rim_right[slot], (k - KERNEL // 2) * DILATION_STEP)
                store(k, 0, jnp.where(mask[:, k : k + 1] > 0, piece.astype(jnp.float32), 0.0))

    def store_tap(m):
        def store(k, first, value):
            taps[tap_rows(m, k, first, value.shape[0])] = value.astype(jnp.bfloat16)

        return store

    def store_back(k, first, value):
        back_taps[k - (k > KERNEL // 2), first : first + value.shape[0]] = value.astype(jnp.bfloat16)

    def front(m, piece):
        block = slice(piece[0], piece[0] + piece[1])
        real = masks[m, block, KERNEL // 2 : KERNEL // 2 + 1]
        act, hat, slope, inverse = act_forward(
            buf[m, block].astype(jnp.float32), first_gain[...], first_shift[...], real)
        act1[m, block] = act.astype(jnp.bfloat16)
        hat1[m, block] = hat.astype(jnp.bfloat16)
        slope1[m, block] = slope.astype(jnp.bfloat16)
        masks[m, block, 8:9] = inverse
        pre = dot_nn(act1[m, block], w_in[...]) + in_bias[...]
        act, hat, slope, inverse = act_forward(pre, second_gain[...], second_shift[...], real)
        taps[tap_rows(m, KERNEL // 2, *piece)] = act.astype(jnp.bfloat16)
        hat2[m, block] = hat.astype(jnp.bfloat16)
        slope2[m, block] = slope.astype(jnp.bfloat16)
        masks[m, block, 9:10] = inverse

    def middle_tap(m, piece):
        return conv_bias[...] + dot_nn(taps[tap_rows(m, KERNEL // 2, *piece)], w_conv[KERNEL // 2])

    def rear(m, piece, pre):
        block = slice(piece[0], piece[0] + piece[1])
        for k in range(KERNEL):
            if k != KERNEL // 2:
                pre = pre + dot_nn(taps[tap_rows(m, k, *piece)], w_conv[k])
        real = masks[m, block, KERNEL // 2 : KERNEL // 2 + 1]
        act, hat, slope, inverse = act_forward(pre, third_gain[...], third_shift[...], real)
        act3[m, block] = act.astype(jnp.bfloat16)
        hat3[m, block] = hat.astype(jnp.bfloat16)
        slope3[m, block] = slope.astype(jnp.bfloat16)
        masks[m, block, 10:11] = inverse
        out = buf[m, block].astype(jnp.float32) + (dot_nn(act3[m, block], w_out[...]) + out_bias[...])
        buf[m, block] = out.astype(jnp.bfloat16)

    def count_types(m):
        logits = dot_nt(readout[...], buf[m])
        kind = lax.broadcasted_iota(jnp.int32, logits.shape, 0)
        odds = jnp.exp(logits - jnp.max(logits, axis=0, keepdims=True))
        odds = odds / jnp.sum(odds, axis=0, keepdims=True)
        stop = lengths[m, 0]
        for j in range(1, ITEMS):
            stop = stop + lengths[m, j]
        spot = lax.broadcasted_iota(jnp.int32, (1, positions), 1) + first_position
        chosen = jnp.where(spot < stop, masked[pl.ds(m, 1)].astype(jnp.float32), 0.0)
        chosen = jnp.where(kind == residues[pl.ds(m, 1)], chosen, 0.0)
        hits[...] += chosen * odds
        tally[...] += chosen

    def back_front(m, piece):
        block = slice(piece[0], piece[0] + piece[1])
        sums_wide[2] += fold(buf[rows + m, block].astype(jnp.float32))
        grad = dot_nt(buf[rows + m, block], w_out[...])
        low = act_backward(
            grad, hat3[m, block], slope3[m, block], masks[m, block, 10:11], third_gain[...], sums.at[4], sums.at[5]
        ).astype(jnp.bfloat16)
        grad2[m, block] = low
        sums[3] += fold(low.astype(jnp.float32))

    def back_middle_tap(m, piece=None):
        block = slice(0, positions) if piece is None else slice(piece[0], piece[0] + piece[1])
        return dot_nt(grad2[m, block], w_conv[KERNEL // 2])

    def back_rear(m, piece, grad, between=None):
        block = slice(piece[0], piece[0] + piece[1])
        for k in range(KERNEL):
            if k != KERNEL // 2:
                grad = grad + dot_nt(back_taps[k - (k > KERNEL // 2), block], w_conv[KERNEL - 1 - k])
        if between is not None:
            between()
        low = act_backward(
            grad, hat2[m, block], slope2[m, block], masks[m, block, 9:10], second_gain[...], sums.at[1], sums.at[2]
        ).astype(jnp.bfloat16)
        grad1[m, block] = low
        sums[0] += fold(low.astype(jnp.float32))

    def back_last(m, piece):
        block = slice(piece[0], piece[0] + piece[1])
        grad = dot_nt(grad1[m, block], w_in[...])
        grad = act_backward(
            grad, hat1[m, block], slope1[m, block], masks[m, block, 8:9], first_gain[...],
            sums_wide.at[0], sums_wide.at[1])
        hat1[m, block] = (buf[rows + m, block].astype(jnp.float32) + grad).astype(jnp.bfloat16)

    def give(source, m):
        return pltpu.make_async_copy(source.at[m], result.at[0, m], result_sem.at[m])

    wide = buf.shape[2] // hidden

    def add_block(start, value):
        total[pl.ds(start, hidden)] += value

    def weights_out(m):
        for j in range(wide):
            add_block((KERNEL + j) * hidden, dot_tn(act3[m], buf[rows + m, :, j * hidden : (j + 1) * hidden]))

    def weights_conv(m):
        for k in range(KERNEL):
            add_block(k * hidden, dot_tn(taps[tap_rows(m, k)], grad2[m]))

    def weights_in(m):
        for j in range(wide):
            add_block(rings[1].base + j * hidden, dot_tn(act1[m, :, j * hidden : (j + 1) * hidden], grad1[m]))

    def first_lane():
        rings[0].exchange(2)
        rings[0].towards(0, 0, True)

    def other_lanes():
        for lane in range(1, rings[0].lanes):
            rings[0].towards(0, lane, True)

    def later_lanes():
        for lane in range(1, rings[0].lanes):
            rings[0].towards(1, lane)

    def step(i, carry):
        fronts = i < rows
        m_start = jnp.where(leading, i - rows, i)
        m_sum = jnp.where(leading, i - rows, i - rows + 1)
        put_off = i >= 2 * rows - 1
        m_end = jnp.where(leading, jnp.where(put_off, i - rows - 2, i - rows - 1), i - 1)
        ends = trailing | (i != 2 * rows - 1)
        m_in = jnp.where(leading, m_end, i - rows)
        final = trailing & (i == 2 * rows - 1)

        def on(m):
            return (m >= 0) & (m < rows)

        @pl.when(fronts)
        def _():
            make_mask(i)

        @pl.when(i == 0)
        def _():
            weight_loads[0].wait()
            for copy in weight_loads[1:]:
                copy.start()
            for m in range(1, rows):
                load(m).start()
            for copy in input_loads:
                copy.wait()

        @pl.when(leading & fronts)
        def _():
            load(i).wait()

        @pl.when(trailing & (i == 0))
        def _():
            pl.semaphore_wait(barrier, greeted)
            gift(0).start()
            for k in (2, 3):
                gift(k).start()
            load(last).wait()
            gift(1).start()

        @pl.when(leading & fronts)
        def _():
            front(i, whole[0])

        @pl.when(i == 0)
        def _():
            weight_loads[1].wait()
            weight_loads[2].wait()

        @pl.when(leading & fronts)
        def _():
            gather_near(0, i, taps[tap_rows(i, KERNEL // 2)], store_tap(i), False)
            rear(i, thirds[0], middle_tap(i, thirds[0]))

        @pl.when(leading & (i == 0))
        def _():
            pl.semaphore_wait(barrier, greeted)

        @pl.when(leading & fronts)
        def _():
            begin(near_copies(0, i))
            hand(buf, i, 0).start()
            end(near_copies(0, i))
            gather_near(0, i, taps[tap_rows(i, KERNEL // 2)], store_tap(i), True)
            for part in (1, 2):
                rear(i, thirds[part], middle_tap(i, thirds[part]))
                hand(buf, i, part).start()

        @pl.when(trailing & fronts)
        def _():
            for part in range(3):
                hand(buf, i, part).wait_recv()
                front(i, thirds[part])
                begin(far_copies(0, i, part, thirds))

        @pl.when(leading & (i == last))
        def _():
            gift(0).wait_recv()
            pass_on(own_half).start()

        @pl.when(leading & (i == rows + 1))
        def _():
            for k in range(1, 4):
                gift(k).wait_recv()
            far_norm()
            pass_on(own_half).wait_send()
            pass_on(other_half).wait_recv()

        @pl.when(leading & on(m_end) & ends)
        def _():
            grad = back_middle_tap(m_end)
            gather_near(1, m_end, grad2[m_end], store_back, False)

            @pl.when(m_end < last - 1)
            def _():
                end(near_copies(1, m_end))

            gather_near(1, m_end, grad2[m_end], store_back, True)

            def lanes_between():
                pl.when(i == 2 * rows)(first_lane)

                @pl.when(i == 2 * rows + 1)
                def _():
                    rings[0].towards(1, 0)
                    rings[0].exchange(3)

            back_rear(m_end, whole[0], grad, lanes_between)
            back_last(m_end, whole[0])
            give(hat1, m_end).start()
            pl.when(i == 2 * rows)(other_lanes)
            pl.when(i == 2 * rows + 1)(later_lanes)

        @pl.when(trailing & on(m_end))
        def _():
            grads = [back_middle_tap(m_end, piece) for piece in parts]
            for part in range(2):
                end(far_copies(1, m_end, part, parts))
            gather_far(1, m_end, grad2[m_end], store_back)
            for part in range(2):
                back_rear(m_end, parts[part], grads[part])
                pl.when(m_end == last)(low_hand(part).start)
                back_last(m_end, parts[part])
                pl.when(m_end < last)(hand(hat1, m_end, part).start)

        @pl.when(final)
        def _():
            first_lane()
            other_lanes()

        @pl.when(on(m_in) & ends)
        def _():
            weights_in(m_in)

        @pl.when(final)
        def _():
            rings[0].towards(1, 0)
            rings[0].exchange(3)
            later_lanes()

        @pl.when(final | (leading & (i == 2 * rows + 1)))
        def _():
            rings[1].exchange(0)
            rings[1].exchange(1)

        @pl.when((leading & (i == 2)) | (trailing & (i == 0)))
        def _():
            total[...] = jnp.zeros_like(total)
            sums_wide[...] = jnp.zeros_like(sums_wide)
            sums[...] = jnp.zeros_like(sums)
            hits[...] = jnp.zeros_like(hits)
            tally[...] = jnp.zeros_like(tally)

        @pl.when(trailing & fronts)
        def _():
            pre = middle_tap(i, whole[0])

            for part in range(3):
                end(far_copies(0, i, part, thirds))
            gather_far(0, i, taps[tap_rows(i, KERNEL // 2)], store_tap(i))
            rear(i, whole[0], pre)
            give(buf, i).start()

        @pl.when(on(m_start))
        def _():
            pl.when(trailing & (m_start < last))(load(m_start).wait)
            for part in range(2):
                pl.when(leading & (m_start < last))(hand(hat1, m_start, part).wait_recv)

                @pl.when(leading & (m_start == last))
                def _():
                    low_hand(part).wait_recv()
                    far_last(parts[part])

                back_front(m_start, parts[part])

                @pl.when(trailing)
                def _():
                    begin(far_copies(1, m_start, part, parts))

            @pl.when(leading & (m_start == last))
            def _():
                end(near_copies(1, last - 1))

            @pl.when(leading)
            def _():
                begin(near_copies(1, m_start))

        @pl.when(trailing & fronts)
        def _():
            count_types(i)

        @pl.when(on(m_sum))
        def _():
            weights_out(m_sum)
            weights_conv(m_sum)

        @pl.when(leading & (m_sum == last))
        def _():
            end(near_copies(1, last))

        @pl.when(m_sum == last)
        def _():
            rings[0].exchange(0)
            rings[0].exchange(1)

        return carry

    lax.fori_loop(0, 2 * rows + 2, step, 0)

    def fill_small():
        for i in range(3):
            small[i : i + 1, :] = jnp.sum(sums_wide[i], axis=0, keepdims=True)
        for i in range(6):
            small[3 + i // 2 : 4 + i // 2, (i % 2) * hidden : (i % 2 + 1) * hidden] = jnp.sum(sums[i], axis=0, keepdims=True)
        small[6:8, :] = jnp.zeros((2, small.shape[1]), jnp.float32)
        ones = jnp.ones((8, positions), jnp.float32)
        for i, counted in ((6, hits), (7, tally)):
            row = lax.dot_general(
                ones, counted[...], (((1,), (1,)), ((), ())), precision=lax.Precision.HIGHEST,
                preferred_element_type=jnp.float32)
            small[i : i + 1, 0 : counted.shape[0]] = row[0:1]

    run_rings(rings, fill_small, SmallSum(rings[0], small, small_land, small_out, small_send, small_recv, partner()))
    for m in range(rows):
        @pl.when(leading)
        def _():
            if m not in (1, 2):
                for part in range(3):
                    hand(buf, m, part).wait_send()
            give(hat1, m).wait()

        @pl.when(trailing)
        def _():
            for part in range(2):
                (hand(hat1, m, part) if m < last else low_hand(part)).wait_send()
            give(buf, m).wait()

    @pl.when(trailing)
    def _():
        for k in range(4):
            gift(k).wait_send()


def ring_plan(width, hidden, nodes):
    plan, base, land = [], 0, 0
    for rows, subs in (((KERNEL + width // hidden) * hidden, LANES), (width, 1)):
        sizes = ring_sizes(rows // 2, nodes, subs)
        plan.append((sizes, base, land))
        land += nodes * sum(map(sum, sizes))
        base = 2 * land
    return plan, land


def run_blocks(args, ny, nz, cid=0):
    nodes = ny * nz
    doublings = 1 + (ny - 1).bit_length() + (nz - 1).bit_length()
    boundary, in_weight, conv_weight = args[0], args[7], args[11]
    _, rows, positions, width = boundary.shape
    hidden = in_weight.shape[2]
    edge = KERNEL // 2 * DILATION_STEP
    assert edge % positions == 0 and positions % 32 == 0 and width % hidden == 0
    reach = edge // positions
    low, full = jnp.bfloat16, jnp.float32
    wide_rows = pltpu.VMEM((rows, positions, width), low)
    thin_rows = pltpu.VMEM((rows, positions, hidden), low)
    plan, half = ring_plan(width, hidden, nodes)
    where = [pltpu.HBM, pltpu.SMEM] + [pltpu.HBM] * 15
    smalls = [pltpu.VMEM(args[i].shape, args[i].dtype) for i in (2, 3, 4, 5, 6, 8, 9, 10, 12, 13, 14, 16)]
    return pl.pallas_call(
        functools.partial(blocks_kernel, edge, plan),
        out_shape=(
            jax.ShapeDtypeStruct(boundary.shape, low),
            jax.ShapeDtypeStruct((2 * half, hidden), low),
            jax.ShapeDtypeStruct((16, width), full),
        ),
        in_specs=[pl.BlockSpec(memory_space=space) for space in where],
        out_specs=[pl.BlockSpec(memory_space=space) for space in (pltpu.HBM, pltpu.HBM, pltpu.VMEM)],
        scratch_shapes=smalls + [
            pltpu.VMEM((2 * rows, positions, width), low),
            pltpu.VMEM((width, hidden), low),
            pltpu.VMEM((KERNEL, hidden, hidden), low),
            pltpu.VMEM((hidden, width), low),
            pltpu.VMEM((2 * half, hidden), full),
            wide_rows, wide_rows, wide_rows,
            pltpu.VMEM((max(rows * KERNEL * positions, half), hidden), low),
            pltpu.VMEM((KERNEL - 1, positions, hidden), low),
            thin_rows, thin_rows, thin_rows, thin_rows, thin_rows,
            pltpu.VMEM((4, edge, hidden), low),
            pltpu.VMEM((4, edge, hidden), low),
            pltpu.VMEM((positions + 32, hidden), full),
            pltpu.VMEM((rows, positions, 128), full),
            pltpu.VMEM((3, 8, width), full),
            pltpu.VMEM((6, 8, hidden), full),
            pltpu.VMEM((VOCAB, positions), full),
            pltpu.VMEM((VOCAB, positions), full),
            pltpu.VMEM((half, hidden), low),
            pltpu.VMEM((8, width), full),
            pltpu.VMEM((2 * doublings, 8, width), full),
            pltpu.SemaphoreType.DMA((rows,)),
            pltpu.SemaphoreType.DMA((3,)),
            pltpu.SemaphoreType.DMA((rows,)),
            pltpu.SemaphoreType.DMA((rows, 3)),
            pltpu.SemaphoreType.DMA((rows, 3)),
            pltpu.SemaphoreType.DMA((2 * rows, 6 * reach)),
            pltpu.SemaphoreType.DMA((2 * rows, 6 * reach)),
            pltpu.SemaphoreType.DMA((doublings + 1,)),
            pltpu.SemaphoreType.DMA((doublings + 1,)),
            pltpu.SemaphoreType.DMA((len(smalls),)),
            pltpu.VMEM((positions, hidden), low),
            pltpu.VMEM((1, width), full),
            pltpu.VMEM((1, width), full),
            pltpu.SemaphoreType.DMA((5,)),
            pltpu.SemaphoreType.DMA((5,)),
        ]
        + [scratch for sizes, _, _ in plan for scratch in ring_scratch(sizes, nodes, hidden)],
        compiler_params=pltpu.CompilerParams(
            collective_id=cid, has_side_effects=True, vmem_limit_bytes=VMEM_BYTES),
    )(*args)


def ring_sizes(rows, nodes, subs):
    units = -(-rows // (nodes * 16))
    long = -(-units // 2)
    return [[16 * ((way + i) // subs) for i in range(subs)] for way in (long, units - long)]


def ring_flows(sizes):
    return [(way, i) for i in range(len(sizes[0])) for way in range(2) if sizes[way][i]]


def ring_scratch(sizes, nodes, columns):
    flows = ring_flows(sizes)
    n = len(flows)
    counts = [(n, nodes)] * 2 + [(n, 2 * nodes - 2)] * 2 + [(n, nodes)] * 2 + [(n,)]
    return [pltpu.SemaphoreType.DMA(count) for count in counts] + [
        pltpu.VMEM((nodes - 1, sizes[way][i], columns), jnp.bfloat16) for way, i in flows]


class Ring:
    def __init__(self, sizes, base, land, section, seq, dp, ny, nz):
        self.sizes, self.base, self.land, self.nodes = sizes, base, land, ny * nz
        self.flows = ring_flows(sizes)
        self.refs = 7 + len(self.flows)
        self.lanes = len(sizes[0])
        self.section, self.nz = section, nz
        self.core, ypos = seq % 2, seq // 2
        self.spot = ypos * nz + dp + (ypos % 2) * (nz - 1 - 2 * dp)
        self.other_core = (section, seq + 1 - 2 * self.core, dp)
        self.turn = [1 - 2 * self.core, 2 * self.core - 1]
        self.next = [self.at_spot(self.wrap(self.spot + self.nodes + turn)) for turn in self.turn]
        self.half = sum(map(sum, sizes)) * self.nodes
        self.first, at = {}, 0
        for way, i in self.flows:
            self.first[way, i] = at
            at += sizes[way][i] * self.nodes
        self.peers = [self.other_core]
        reach = 1
        while reach < ny:
            self.peers.append((section, seq + 2 * reach - 4 * reach * ((ypos // reach) % 2), dp))
            reach *= 2
        reach = 1
        while reach < nz:
            self.peers.append((section, seq, dp + reach - 2 * reach * ((dp // reach) % 2)))
            reach *= 2

    def wrap(self, place):
        if self.nodes & (self.nodes - 1) == 0:
            return place & (self.nodes - 1)
        return lax.rem(place, self.nodes)

    def at_spot(self, place):
        y = place // self.nz
        z = place % self.nz
        return (self.section, y * 2 + self.core, z + (y % 2) * (self.nz - 1 - 2 * z))

    def neighbours(self):
        around = self.next
        return self.peers + around

    def bind(self, total, stage, core_land, big, refs):
        self.total, self.stage, self.core_land, self.big = total, stage, core_land, big
        self.core_sems, self.ring_sems, self.over_sems = refs[0:2], refs[2:4], refs[4:6]
        self.keep_sem, self.lands = refs[6], refs[7:]

    def count(self, f):
        way, i = self.flows[f]
        return self.sizes[way][i]

    def rows(self, f, side, shard):
        start = self.base + side * self.half + self.first[self.flows[f]] + shard * self.count(f)
        return pl.ds(pl.multiple_of(start, 16), self.count(f))

    def land_rows(self, f, shard):
        start = self.land + self.first[self.flows[f]] + shard * self.count(f)
        return pl.ds(pl.multiple_of(start, 16), self.count(f))

    def shard(self, f, step):
        return self.wrap(self.spot + 2 * self.nodes - self.turn[self.flows[f][0]] * step)

    def ahead(self, f):
        return self.next[self.flows[f][0]]

    def remote(self, source, target, sems, index, peer):
        return pltpu.make_async_remote_copy(
            src_ref=source, dst_ref=target, send_sem=sems[0].at[index], recv_sem=sems[1].at[index],
            device_id=peer, device_id_type=MESH)

    def core_copy(self, f, shard):
        rows = self.land_rows(f, shard)
        return self.remote(self.stage.at[rows], self.core_land.at[rows], self.core_sems, (f, shard), self.other_core)

    def ring_copy(self, f, step, shard):
        return self.remote(
            self.core_land.at[self.land_rows(f, shard)], self.lands[f].at[step], self.ring_sems, (f, step), self.ahead(f))

    def back_copy(self, f, step, shard):
        block = self.big.at[self.rows(f, self.core, shard)]
        return self.remote(
            self.core_land.at[self.land_rows(f, shard)] if step is None else block, block,
            self.ring_sems, (f, self.nodes - 1 + (0 if step is None else step)), self.ahead(f))

    def over_copy(self, f, shard, own=False):
        block = self.big.at[self.rows(f, self.core, shard)]
        return self.remote(
            self.core_land.at[self.land_rows(f, shard)] if own else block, block,
            self.over_sems, (f, shard), self.other_core)

    def keep_copy(self, f, shard):
        return pltpu.make_async_copy(
            self.core_land.at[self.land_rows(f, shard)], self.big.at[self.rows(f, self.core, shard)], self.keep_sem.at[f])

    def add(self, f, shard, step):
        rows = self.land_rows(f, shard)
        value = self.total[self.rows(f, self.core, shard)] + self.core_land[rows].astype(jnp.float32)
        if step is not None:
            value = value + self.lands[f][step].astype(jnp.float32)
        self.core_land[rows] = value.astype(jnp.bfloat16)

    def exchange(self, step):
        for f in range(len(self.flows)):
            shard = self.shard(f, -step)
            self.stage[self.land_rows(f, shard)] = self.total[self.rows(f, 1 - self.core, shard)].astype(jnp.bfloat16)
            self.core_copy(f, shard).start()

    def of(self, lane):
        return [f for f in range(len(self.flows)) if lane is None or self.flows[f][1] == lane]

    def towards(self, step, lane=None, first=False):
        for f in self.of(lane):
            shard = self.shard(f, step)
            self.core_copy(f, shard).wait_recv()
            if first:
                self.add(f, shard, None)
            else:
                self.ring_copy(f, step - 1, shard).wait_recv()
                self.add(f, shard, step - 1)
            self.ring_copy(f, step, shard).start()

    def back(self, step, lane=None):
        for f in self.of(lane):
            shard = self.shard(f, self.nodes - 1 + step)
            self.back_copy(f, step - 1, shard).wait_recv()
            self.back_copy(f, step, shard).start()
            self.over_copy(f, shard).start()

    def own(self, lane=None):
        for f in self.of(lane):
            shard = self.shard(f, self.nodes - 1)
            self.core_copy(f, shard).wait_recv()
            self.ring_copy(f, self.nodes - 2, shard).wait_recv()
            self.add(f, shard, self.nodes - 2)
            self.back_copy(f, None, shard).start()
            self.over_copy(f, shard, True).start()
            self.keep_copy(f, shard).start()

    def arrive(self, lane=None):
        for f in self.of(lane):
            shard = self.shard(f, 2 * self.nodes - 2)
            self.back_copy(f, self.nodes - 2, shard).wait_recv()
            self.over_copy(f, shard).start()

    def settle(self):
        def crossed(step, carry):
            for f in range(len(self.flows)):
                self.core_copy(f, step).wait_send()
                self.over_copy(f, step).wait()
            return carry

        def rounded(step, carry):
            for f in range(len(self.flows)):
                self.ring_copy(f, step, 0).wait_send()
                self.back_copy(f, step, 0).wait_send()
            return carry

        lax.fori_loop(0, self.nodes, crossed, 0)
        lax.fori_loop(0, self.nodes - 1, rounded, 0)
        for f in range(len(self.flows)):
            self.keep_copy(f, 0).wait()


def run_rings(rings, fill_small, small_sum):
    ahead, behind = rings
    nodes, lanes = ahead.nodes, ahead.lanes

    def each(method, *step):
        for lane in range(lanes):
            getattr(ahead, method)(*step, lane)
        getattr(behind, method)(*step)

    for step in (2, 3):
        ahead.exchange(step + 2)
        behind.exchange(2 * step - 2)
        behind.exchange(2 * step - 1)
        ahead.towards(step, 0)
        behind.towards(2 * step - 4, first=step == 2)
        for lane in range(1, lanes):
            ahead.towards(step, lane)
        behind.towards(2 * step - 3)

    fill_small()
    small_sum.step(0)

    def towards(step, carry):
        ahead.exchange(step + 2)
        behind.exchange(step + 2)
        each("towards", step)
        return carry

    lax.fori_loop(4, nodes - 2, towards, 0)
    each("towards", nodes - 2)
    each("own")
    small_sum.step(1)
    at = 1
    for k in range(2, small_sum.steps):
        if at < nodes - 1:
            each("back", at)
            at += 1
        small_sum.step(k)

    def back(step, carry):
        each("back", step)
        return carry

    lax.fori_loop(at, nodes - 1, back, 0)
    each("arrive")
    ahead.settle()
    behind.settle()
    small_sum.settle()


class SmallSum:
    def __init__(self, ring, small, land, out, send_sem, recv_sem, other_section):
        self.peers, self.small, self.land, self.out = ring.peers + [other_section], small, land, out
        self.sems = (send_sem, recv_sem)
        self.remote = ring.remote
        self.steps = len(self.peers) + 1

    def held(self, k):
        return self.small if k == 0 else self.land.at[2 * k - 1]

    def copy(self, k):
        count = self.small.shape[0]
        target = self.out.at[pl.ds(count, count)] if k == len(self.peers) - 1 else self.land.at[2 * k]
        return self.remote(self.held(k), target, self.sems, k, self.peers[k])

    def step(self, k):
        last = len(self.peers) - 1
        if 0 < k:
            self.copy(k - 1).wait_recv()
        if 0 < k <= last:
            self.land[2 * k - 1] = self.held(k - 1)[...] + self.land[2 * k - 2]
        if k <= last:
            self.copy(k).start()
        if k == last:
            self.out[pl.ds(0, self.small.shape[0])] = self.held(k)[...]

    def settle(self):
        for k in range(len(self.peers)):
            self.copy(k).wait_send()


def finish_kernel(
    base, given, big, small_in, result, grad_in, grad_conv, grad_out, first_gain, first_shift, in_bias, second_gain,
    second_shift, conv_bias, third_gain, third_shift, out_bias, scores, counts,
    small, passed, held, wide, rate, count, pass_sem, load_sem, store_sem, small_sem,
):
    hidden = held.shape[2]
    blocks = held.shape[0]
    ends = grad_in.shape[1] // hidden
    small_load = pltpu.make_async_copy(small_in, small, pass_sem.at[0])
    first = pltpu.make_async_copy(given, passed, pass_sem.at[1])
    second = pltpu.make_async_copy(passed, result, pass_sem.at[2])

    def load(b):
        start = b * hidden if b < blocks - ends else base + (b - blocks + ends) * hidden
        return pltpu.make_async_copy(big.at[pl.ds(start, hidden)], held.at[b], load_sem.at[b])

    def store(b):
        if b < KERNEL:
            target = grad_conv.at[0, b]
        elif b < blocks - ends:
            target = grad_out.at[0, :, pl.ds((b - KERNEL) * hidden, hidden)]
        else:
            target = grad_in.at[0, pl.ds((b - blocks + ends) * hidden, hidden)]
        return pltpu.make_async_copy(wide.at[b], target, store_sem.at[b])

    load(0).start()
    small_load.start()
    for b in range(1, blocks):
        load(b).start()
    first.start()
    for b in range(blocks):
        load(b).wait()
        wide[b] = held[b].astype(jnp.float32)
        store(b).start()
        if b == 0:
            small_load.wait()
            hits = small[6:7, 0:VOCAB] + small[14:15, 0:VOCAB]
            tally = small[7:8, 0:VOCAB] + small[15:16, 0:VOCAB]
            rate[...] = hits / jnp.maximum(tally, 1.0)
            count[...] = tally.astype(jnp.int32)
            pieces = [(small.at[pl.ds(i, 1)], ref) for i, ref in enumerate((first_gain, first_shift, out_bias))]
            thin = (in_bias, second_gain, second_shift, conv_bias, third_gain, third_shift)
            for i, ref in enumerate(thin):
                pieces.append((small.at[pl.ds(3 + i // 2, 1), pl.ds(i % 2 * hidden, hidden)], ref))
            pieces += [(rate, scores), (count, counts)]
            small_stores = [
                pltpu.make_async_copy(source, target, small_sem.at[i]) for i, (source, target) in enumerate(pieces)
            ]
            for copy in small_stores:
                copy.start()
    first.wait()
    second.start()
    for b in range(blocks):
        store(b).wait()
    for copy in small_stores:
        copy.wait()
    second.wait()


def finish(given, big, small, width, base):
    hidden = big.shape[1]
    blocks = 2 * width // hidden + KERNEL
    full = jnp.float32
    shapes = [(1, width, hidden), (1, KERNEL, hidden, hidden), (1, hidden, width), (1, width), (1, width)]
    shapes += [(1, hidden)] * 6 + [(1, width), (1, VOCAB)]
    out = [jax.ShapeDtypeStruct(given.shape, given.dtype)]
    out += [jax.ShapeDtypeStruct(shape, full) for shape in shapes] + [jax.ShapeDtypeStruct((1, VOCAB), jnp.int32)]
    return pl.pallas_call(
        functools.partial(finish_kernel, base),
        out_shape=out,
        in_specs=[pl.BlockSpec(memory_space=pltpu.HBM)] * 3,
        out_specs=[pl.BlockSpec(memory_space=pltpu.HBM)] * len(out),
        scratch_shapes=[
            pltpu.VMEM(small.shape, full),
            pltpu.VMEM(given.shape, given.dtype),
            pltpu.VMEM((blocks, hidden, hidden), big.dtype),
            pltpu.VMEM((blocks, hidden, hidden), full),
            pltpu.VMEM((1, VOCAB), full),
            pltpu.VMEM((1, VOCAB), jnp.int32),
            pltpu.SemaphoreType.DMA((3,)),
            pltpu.SemaphoreType.DMA((blocks,)),
            pltpu.SemaphoreType.DMA((blocks,)),
            pltpu.SemaphoreType.DMA((11,)),
        ],
        compiler_params=pltpu.CompilerParams(vmem_limit_bytes=VMEM_BYTES),
    )(given, big, small)


def shards(
    boundary, lengths, masked, residues, readout,
    first_gain, first_shift, in_weight, in_bias, second_gain, second_shift, conv_weight, conv_bias,
    third_gain, third_shift, out_weight, out_bias,
):
    ny, nz = lax.axis_size("seq") // 2, lax.axis_size("dp")
    width, hidden = in_weight.shape[1], in_weight.shape[2]
    given, big, small = run_blocks(
        (
            boundary, lengths, masked, residues, readout.T,
            first_gain, first_shift, in_weight, in_bias, second_gain, second_shift, conv_weight, conv_bias,
            third_gain, third_shift, out_weight, out_bias,
        ),
        ny,
        nz,
    )
    (
        boundary_out, grad_in_weight, grad_conv_weight, grad_out_weight, grad_first_gain, grad_first_shift, grad_in_bias,
        grad_second_gain, grad_second_shift, grad_conv_bias, grad_third_gain, grad_third_shift, grad_out_bias,
        scores, counts,
    ) = finish(given, big, small, width, ring_plan(width, hidden, ny * nz)[0][1][1])
    return (
        boundary_out,
        grad_first_gain,
        grad_first_shift,
        grad_in_weight,
        grad_in_bias,
        grad_second_gain,
        grad_second_shift,
        grad_conv_weight,
        grad_conv_bias,
        grad_third_gain,
        grad_third_shift,
        grad_out_weight,
        grad_out_bias,
        scores[0],
        counts[0],
    )


def solution(mesh):
    in_specs = (
        P("section", "dp", "seq", None),
        P("dp", None),
        P("dp", "seq"),
        P("dp", "seq"),
        P(),
        P("section", None),
        P("section", None),
        P("section", None, None),
        P("section", None),
        P("section", None),
        P("section", None),
        P("section", None, None, None),
        P("section", None),
        P("section", None),
        P("section", None),
        P("section", None, None),
        P("section", None),
    )
    out_specs = (
        P("section", "dp", "seq", None),
        P("section", None),
        P("section", None),
        P("section", None, None),
        P("section", None),
        P("section", None),
        P("section", None),
        P("section", None, None, None),
        P("section", None),
        P("section", None),
        P("section", None),
        P("section", None, None),
        P("section", None),
        P(),
        P(),
    )
    return jax.shard_map(shards, mesh=mesh, in_specs=in_specs, out_specs=out_specs, check_vma=False)
```
